256 devices in a mesh: seq: 16 (over y, x), tp: 8 (over z), tea: 2 (over core).
Axes of the slice: x: 4, y: 4, z: 8, core: 2. Of those that a mesh axis runs over, the one named last changes fastest.
Arguments:
- hidden_states: bfloat16 [12288, 3072], P(('seq', 'tea')), may hold values from -6 to 6
- w_in: bfloat16 [3072, 2048], P(None, 'tp'), may hold values from -0.109375 to 0.109375
- w_out: bfloat16 [2048, 1408], P('tp'), may hold values from -0.125 to 0.125
- teacher: bfloat16 [6144, 1408], P(('seq', 'tea')), may hold values from -6 to 6
- patch_map: int32 [12288], P(('seq', 'tea')), may hold values from 0 to 6143, as said below
- row_pick: int32 [16, 8, 2, 16], P('seq', 'tp', 'tea'), may hold values from 0 to 2
- key_pick: int32 [16, 8, 2, 16], P(None, 'tp', 'tea'), may hold values from 0 to 2
Outputs:
- grad_hidden: float32 [12288, 3072], P(('seq', 'tea'), 'tp')
- grad_w_in: float32 [3072, 2048], P(None, 'tp')
- grad_w_out: float32 [2048, 1408], P('tp')
The draws below stay inside these ranges and needn't reach their ends.
Inputs may be any that keep to these rules, and one draw needn't show every extreme that they name: `patch_map`: the tokens of group q (rows q * 384 onward) name teacher rows q * 192 to (q + 1) * 192 - 1 only, each of them exactly 384 / 192 times.
All inputs are finite; a program needn't handle non-finite values.
Results may differ from the reference program's by a relative error of at most 0.0055.
Values may be sent and summed in bfloat16 or wider, within the bound.
No kernel may reach another device: no remote copies, remote signals or barrier semaphores. Data moves between devices by JAX's collectives and lax.ppermute only.
A program may use at most 128 MiB of HBM per device.

```python
import jax
import jax.numpy as jnp
from jax import lax

D = 3072
E = 1408
PH = 2048
BLK = 128
TOK_DEV = 384
TT_DEV = 192
RB = 3
TOKENS = 12288
TEACH = 6144
N_SEQ = 16
N_TP = 8
N_TEA = 2


def draw_patch_map(key, part):
    key = jax.random.fold_in(key, 5)
    group_count = N_SEQ * N_TEA
    group_keys = jax.random.split(key, group_count)
    shuffled = jax.vmap(lambda group_key: jax.random.permutation(group_key, TOK_DEV))(group_keys)
    local_rows = shuffled.astype(jnp.int32) % TT_DEV
    group_base = (jnp.arange(group_count, dtype=jnp.int32) * TT_DEV)[:, None]
    return (local_rows + group_base).reshape(-1).astype(jnp.int32)


def place_ends(entries, stream_key, smallest, top_value):
    longest = entries.shape.index(max(entries.shape))
    spots = []
    for shift in (0, 1):
        where = [jax.random.randint(jax.random.fold_in(stream_key, axis), (), 0, length) for axis, length in enumerate(entries.shape)]
        where[longest] = (where[longest] + shift) % entries.shape[longest]
        spots.append(tuple(where))
    return entries.at[spots[0]].set(smallest).at[spots[1]].set(top_value)


def block_levels(stream_key, dims, cuts, least, high):
    def one(dim, blocks):
        steps = jax.random.uniform(jax.random.fold_in(jax.random.fold_in(stream_key, 6), dim), (blocks,), jnp.float32, least / len(cuts), high / len(cuts))
        return jnp.repeat(jnp.exp(steps), dims[dim] // blocks).reshape((-1,) + (1,) * (len(dims) - dim - 1))

    level = one(*cuts[0])
    for cut in cuts[1:]:
        level = level * one(*cut)
    return level


def gaussian(own_key, shape, spread, reach, cuts=(), kind=jnp.bfloat16):
    drawn = jax.random.normal(own_key, shape, jnp.float32) * spread
    if len(cuts) > 0:
        drawn = block_levels(own_key, shape, cuts, -0.22, 0.18) * drawn
    return jnp.clip(drawn, min=-reach, max=reach).astype(kind)


def setup_inputs(seed: int = 0) -> dict:
    keys = jax.random.split(jax.random.key(seed), 8)
    hidden_states = gaussian(keys[0], (TOKENS, D), 1.0, 6.0, ((0, 32),))
    w_in = gaussian(keys[1], (D, PH), D ** -0.5, 0.109375, ((1, 8),))
    w_out = gaussian(keys[2], (PH, E), PH ** -0.5, 0.125, ((0, 8),))
    teacher = gaussian(keys[3], (TEACH, E), 1.0, 6.0, ((0, 32),))
    patch_map = draw_patch_map(jax.random.fold_in(keys[7], 71), 0)
    row_pick = place_ends(jax.random.randint(keys[5], (N_SEQ, N_TP, N_TEA, N_SEQ), 0, RB), jax.random.fold_in(keys[5], 1), 0, RB - 1).astype(jnp.int32)
    key_pick = place_ends(jax.random.randint(keys[6], (N_SEQ, N_TP, N_TEA, N_SEQ), 0, RB), jax.random.fold_in(keys[6], 1), 0, RB - 1).astype(jnp.int32)
    return {"hidden_states": hidden_states, "w_in": w_in, "w_out": w_out, "teacher": teacher, "patch_map": patch_map, "row_pick": row_pick, "key_pick": key_pick}


eps = 1e-06

def reference(hidden_states, w_in, w_out, teacher, patch_map, row_pick, key_pick):
    pre_act = jnp.dot(hidden_states, w_in, preferred_element_type=jnp.float32)
    activation = jax.nn.silu(pre_act).astype(jnp.bfloat16)
    projected = jnp.dot(activation, w_out, preferred_element_type=jnp.float32)
    inv_norm = lax.rsqrt(lax.optimization_barrier(jnp.sum(projected * projected, axis=-1, keepdims=True)) + eps)
    unit_student = projected * inv_norm
    student_bf = unit_student.astype(jnp.bfloat16)
    teacher_f = teacher.astype(jnp.float32)
    teacher_unit = (teacher_f * lax.rsqrt(lax.optimization_barrier(jnp.sum(teacher_f * teacher_f, axis=-1, keepdims=True)) + eps)).astype(jnp.bfloat16)
    aligned = jnp.take(teacher_unit, patch_map, axis=0)
    group_count = N_SEQ * N_TEA
    student_blocks = student_bf.reshape(group_count, RB, BLK, E)
    teacher_blocks = aligned.reshape(group_count, RB, BLK, E)
    row_table = row_pick.reshape(-1, N_SEQ)
    key_table = key_pick.reshape(-1, N_SEQ)
    source_base = jnp.arange(N_SEQ, dtype=jnp.int32) * N_TEA
    highest = lax.Precision.HIGHEST

    def one_group(grads, flat_index):
        seq_index = flat_index // (N_TP * N_TEA)
        tea_index = flat_index % N_TEA
        owner = seq_index * N_TEA + tea_index
        row_list = row_table[flat_index]
        key_list = key_table[flat_index]
        source_list = source_base + tea_index
        row_student = student_blocks[owner][row_list].astype(jnp.float32)
        row_teacher = teacher_blocks[owner][row_list].astype(jnp.float32)
        key_student = student_blocks[source_list, key_list].astype(jnp.float32)
        key_teacher = teacher_blocks[source_list, key_list].astype(jnp.float32)
        gram_diff = jnp.einsum('pbe,pce->pbc', row_student, key_student, precision=highest) - jnp.einsum('pbe,pce->pbc', row_teacher, key_teacher, precision=highest)
        gram_grad = gram_diff * (E / 8.0)
        row_terms = jnp.einsum('pbc,pce->pbe', gram_grad, key_student, precision=highest)
        key_terms = jnp.einsum('pbc,pbe->pce', gram_grad, row_student, precision=highest).astype(jnp.bfloat16)
        grads = grads.at[owner, row_list].add(row_terms)
        grads = grads.at[source_list, key_list].add(key_terms.astype(jnp.float32))
        return (grads, None)
    grads = jnp.zeros((group_count, RB, BLK, E), jnp.float32)
    grads, _ = lax.scan(one_group, grads, jnp.arange(N_SEQ * N_TP * N_TEA, dtype=jnp.int32))
    unit_grad = grads.reshape(TOKENS, E)
    inner = lax.optimization_barrier(jnp.sum(unit_student * unit_grad, axis=-1, keepdims=True))
    grad_proj = ((unit_grad - unit_student * inner) * inv_norm).astype(jnp.bfloat16)
    grad_act = jnp.dot(grad_proj, w_out.T, preferred_element_type=jnp.float32)
    sigma = jax.nn.sigmoid(pre_act)
    grad_pre = (grad_act * sigma * (1.0 + pre_act * (1.0 - sigma))).astype(jnp.bfloat16)
    grad_w_out = jnp.dot(activation.T, grad_proj, preferred_element_type=jnp.float32)
    grad_w_in = jnp.dot(hidden_states.T, grad_pre, preferred_element_type=jnp.float32)
    grad_hidden = jnp.dot(grad_pre, w_in.T, preferred_element_type=jnp.float32)
    return (grad_hidden, grad_w_in, grad_w_out)
```

```python
import jax
import jax.numpy as jnp
from jax import lax
from jax.sharding import PartitionSpec as P

E = 1408
BLK = 128
RB = 3
SIDE = 4
NT = 8
GROUPS = SIDE * SIDE
SHARD = 48
HALF = SHARD // 2
EXTRA = 8
ROWS = 384
W_ROWS = 4608

eps = 1e-06
bf16 = jnp.bfloat16
f32 = jnp.float32


def shift_tp(x, step):
    return lax.ppermute(x, "tp", [(i, (i + step) % NT) for i in range(NT)])


def shift_x(x, step):
    pairs = [(y * SIDE + i, y * SIDE + (i + step) % SIDE) for y in range(SIDE) for i in range(SIDE)]
    return lax.ppermute(x, "seq", pairs)


def shift_y(x, step):
    pairs = [(i * SIDE + c, (i + step) % SIDE * SIDE + c) for i in range(SIDE) for c in range(SIDE)]
    return lax.ppermute(x, "seq", pairs)


def swap_tea(x):
    return lax.ppermute(x, "tea", [(0, 1), (1, 0)])


def gather_around(x, shift, size):
    order = sorted(range(1, size), key=lambda d: -min(d, size - d))
    got = {0: x}
    for d in order:
        got[size - d] = shift(x, d)
    return [got[d] for d in range(size)]


def scatter_around(pieces, shift):
    size = len(pieces)
    order = sorted(range(1, size), key=lambda d: -min(d, size - d))
    got = [shift(pieces[d].astype(bf16), d) for d in order]
    total = pieces[0].astype(f32)
    for piece in got:
        total = total + piece.astype(f32)
    return total


def gather_plane(first, second):
    first = jnp.concatenate(gather_around(first, shift_x, SIDE), axis=0)
    second = jnp.concatenate(gather_around(second, shift_y, SIDE), axis=0)
    first = gather_around(first, shift_y, SIDE)
    second = gather_around(second, shift_x, SIDE)
    return first, second


def turn(x, start, size):
    return lax.dynamic_slice_in_dim(jnp.concatenate([x, x], axis=0), start, size, axis=0)


def reduce_plane(part, outer_index, inner_index, outer, inner):
    rows = part.shape[0]
    quarter, small = rows // SIDE, rows // SIDE // SIDE
    doubled = jnp.concatenate([part, part], axis=0)
    pieces = [
        lax.dynamic_slice_in_dim(doubled, outer_index * quarter + d * quarter, quarter, axis=0)
        for d in range(SIDE)
    ]
    mine = scatter_around(pieces, outer)
    doubled = jnp.concatenate([mine, mine], axis=0)
    pieces = [
        lax.dynamic_slice_in_dim(doubled, inner_index * small + d * small, small, axis=0)
        for d in range(SIDE)
    ]
    mine = scatter_around(pieces, inner).astype(bf16)
    mine = jnp.concatenate(gather_around(mine, inner, SIDE), axis=0)
    mine = turn(mine, (SIDE - inner_index) % SIDE * small, quarter)
    mine = jnp.concatenate(gather_around(mine, outer, SIDE), axis=0)
    return turn(mine, (SIDE - outer_index) % SIDE * quarter, rows)


def pair_weights(row_pick, key_pick, seq_index):
    rows = row_pick.reshape(1, GROUPS)
    keys = key_pick.reshape(GROUPS, GROUPS)
    both = jnp.concatenate([rows, keys], axis=0).astype(f32)[None]
    for step in (1, 2, 4):
        both = jnp.concatenate([both, shift_tp(both, -step)], axis=0)
    return both[:, 0], both[:, 1:]


def on_device(hidden_states, w_in, w_out, teacher, patch_map, row_pick, key_pick):
    seq_index = lax.axis_index("seq")
    y_index, x_index = seq_index // SIDE, seq_index % SIDE
    tp_index = lax.axis_index("tp")
    tea_index = lax.axis_index("tea")
    block_ids = jnp.arange(RB, dtype=jnp.int32)

    own_picks, key_picks = pair_weights(row_pick, key_pick, seq_index)

    teacher_rows = teacher.shape[0]
    teacher_f = teacher.astype(f32)
    teacher_unit = (
        teacher_f * lax.rsqrt(jnp.sum(teacher_f * teacher_f, axis=-1, keepdims=True) + eps)
    ).astype(bf16)
    local_patch = patch_map - lax.axis_index(("seq", "tea")) * teacher_rows
    local_patch = turn(local_patch, tp_index * SHARD, ROWS)
    patch_hot = (local_patch[:, None] == jnp.arange(teacher_rows, dtype=jnp.int32)[None, :]).astype(bf16)
    row_teacher = jnp.dot(patch_hot, teacher_unit, preferred_element_type=f32).astype(bf16)
    own_line = jnp.pad(own_picks.reshape(1, NT * GROUPS).astype(bf16), ((0, EXTRA - 1), (0, E - NT * GROUPS)))
    first, second = gather_plane(
        jnp.concatenate([row_teacher[:HALF], own_line], axis=0), row_teacher[HALF:SHARD]
    )
    first = jnp.stack([p.reshape(SIDE, HALF + EXTRA, E) for p in first])
    key_teacher = jnp.concatenate(
        [first[:, :, :HALF].reshape(GROUPS * HALF, E)] + second, axis=0
    )

    all_picks = first[:, :, HALF, : NT * GROUPS].reshape(SIDE, SIDE, NT, GROUPS).astype(f32)
    all_picks = lax.dynamic_index_in_dim(all_picks, seq_index, axis=3, keepdims=False)
    rel_y = (y_index + jnp.arange(SIDE, dtype=jnp.int32)) % SIDE
    rel_x = (x_index + jnp.arange(SIDE, dtype=jnp.int32)) % SIDE
    rel_group = (rel_y[:, None] * SIDE + rel_x[None, :]).reshape(GROUPS)
    own_keys = lax.dynamic_index_in_dim(key_picks, seq_index, axis=1, keepdims=False)
    group_hot = (rel_group[:, None] == jnp.arange(GROUPS, dtype=jnp.int32)[None, :]).astype(f32)
    to_rel = lambda v: jnp.sum(v[:, None, :] * group_hot[None], axis=-1)
    fits = lambda v: (v[..., None] == block_ids.astype(f32)).astype(f32)
    row_side = fits(to_rel(own_picks))
    key_side = fits(to_rel(own_keys))
    other_row = fits(all_picks.reshape(GROUPS, NT).T)
    other_key = fits(to_rel(lax.dynamic_index_in_dim(key_picks, seq_index, axis=2, keepdims=False)))
    weights = jnp.sum(
        row_side[:, :, :, None] * key_side[:, :, None, :] + other_key[:, :, :, None] * other_row[:, :, None, :],
        axis=0,
    )
    by_x = weights.reshape(SIDE, SIDE, RB, RB).transpose(1, 0, 2, 3).reshape(GROUPS, RB, RB)
    spot = tp_index * SHARD + jnp.arange(SHARD, dtype=jnp.int32)
    spot_hot = (spot[:, None] // BLK == block_ids[None, :]).astype(f32)
    wide = lambda w, hot: jnp.sum(w[:, :, None, :] * hot[None, None], axis=-1).transpose(1, 0, 2).reshape(RB, -1)
    wide_weights = jnp.concatenate([wide(weights, spot_hot[:HALF]), wide(by_x, spot_hot[HALF:])], axis=1)
    row_spot = (tp_index * SHARD + jnp.arange(ROWS, dtype=jnp.int32)) % ROWS // BLK
    row_hot = (row_spot[:, None] == block_ids[None, :]).astype(f32)
    tile_weights = jnp.sum(row_hot[:, :, None] * wide_weights[None], axis=1).astype(bf16)

    pre_act = jnp.dot(hidden_states, w_in, preferred_element_type=f32)
    pre_act = turn(pre_act, tp_index * SHARD, ROWS)
    activation = jax.nn.silu(pre_act).astype(bf16)
    partial_out = jnp.dot(activation, w_out, preferred_element_type=f32)
    projected = scatter_around([partial_out[d * SHARD : (d + 1) * SHARD] for d in range(NT)], shift_tp)
    inv_norm = lax.rsqrt(jnp.sum(projected * projected, axis=-1, keepdims=True) + eps)
    unit_student = projected * inv_norm
    student_bf = unit_student.astype(bf16)

    row_student = jnp.concatenate(gather_around(student_bf, shift_tp, NT), axis=0)
    first, second = gather_plane(student_bf[:HALF], student_bf[HALF:])
    key_student = jnp.concatenate(first + second, axis=0)

    contract = (((1,), (1,)), ((), ()))
    gram_teacher = lax.dot_general(row_teacher, key_teacher, contract, preferred_element_type=f32)
    gram_student = lax.dot_general(row_student, key_student, contract, preferred_element_type=f32)
    gram_grad = (gram_student - gram_teacher) * (tile_weights.astype(f32) * (E / 8.0))
    row_grad = jnp.dot(gram_grad.astype(bf16), key_student, preferred_element_type=f32)
    unit_grad = scatter_around([row_grad[d * SHARD : (d + 1) * SHARD] for d in range(NT)], shift_tp)
    inner = jnp.sum(unit_student * unit_grad, axis=-1, keepdims=True)
    grad_proj = ((unit_grad - unit_student * inner) * inv_norm).astype(bf16)
    grad_proj = jnp.concatenate(gather_around(grad_proj, shift_tp, NT), axis=0)

    grad_act = lax.dot_general(grad_proj, w_out, contract, preferred_element_type=f32)
    sigma = jax.nn.sigmoid(pre_act)
    grad_pre = (grad_act * sigma * (1.0 + pre_act * (1.0 - sigma))).astype(bf16)
    grad_pre = turn(grad_pre, (NT - tp_index) % NT * SHARD, ROWS)
    over_rows = (((0,), (0,)), ((), ()))
    local_w_out = lax.dot_general(grad_proj, activation, over_rows, preferred_element_type=f32)
    local_w_in = lax.dot_general(hidden_states, grad_pre, over_rows, preferred_element_type=f32)
    d_model, width = local_w_in.shape
    local = jnp.concatenate(
        [local_w_in, local_w_out, jnp.zeros((W_ROWS - d_model - E, width), f32)], axis=0
    )
    half = W_ROWS // 2
    keep = lax.dynamic_slice_in_dim(local, tea_index * half, half, axis=0)
    give = lax.dynamic_slice_in_dim(local, (1 - tea_index) * half, half, axis=0).astype(bf16)
    chip = keep + swap_tea(give).astype(f32)
    by_rows = reduce_plane(chip[:, : width // 2], x_index, y_index, shift_x, shift_y)
    by_cols = reduce_plane(chip[:, width // 2 :], y_index, x_index, shift_y, shift_x)
    mine = jnp.concatenate([by_rows, by_cols], axis=1)
    other = swap_tea(mine)
    low_half = jnp.where(tea_index == 0, mine, other)
    high_half = jnp.where(tea_index == 0, other, mine)
    summed = jnp.concatenate([low_half, high_half], axis=0)
    grad_w_in = summed[:d_model].astype(f32)
    grad_w_out = summed[d_model : d_model + E].T.astype(f32)

    share = d_model // NT
    w_in_rel = turn(w_in, tp_index * share, d_model)
    hidden_terms = lax.dot_general(grad_pre, w_in_rel, contract, preferred_element_type=f32)
    grad_hidden = scatter_around(
        [hidden_terms[:, d * share : (d + 1) * share] for d in range(NT)], shift_tp
    )
    return (grad_hidden, grad_w_in, grad_w_out)


def solution(mesh):
    return jax.shard_map(
        on_device,
        mesh=mesh,
        in_specs=(
            P(("seq", "tea"), None),
            P(None, "tp"),
            P("tp", None),
            P(("seq", "tea"), None),
            P(("seq", "tea")),
            P("seq", "tp", "tea", None),
            P(None, "tp", "tea", None),
        ),
        out_specs=(P(("seq", "tea"), "tp"), P(None, "tp"), P("tp", None)),
        check_vma=False,
    )
```

```python
import jax
import jax.numpy as jnp
from jax import lax
from jax.experimental import pallas as pl
from jax.experimental.pallas import tpu as pltpu
from jax.sharding import PartitionSpec as P

E = 1408
BLK = 128
RB = 3
SIDE = 4
NT = 8
GROUPS = SIDE * SIDE
SHARD = 48
ROWS = 384
E_WIDE = 1536
E_PAD = 1536

eps = 1e-06
bf16 = jnp.bfloat16
f32 = jnp.float32


def shift_tp(x, step):
    return lax.ppermute(x, "tp", [(i, (i + step) % NT) for i in range(NT)])


def swap_tea(x):
    return lax.ppermute(x, "tea", [(0, 1), (1, 0)])


def gather_around(x, shift, size):
    order = sorted(range(1, size), key=lambda d: -min(d, size - d))
    got = {0: x}
    for d in order:
        got[size - d] = shift(x, d)
    return [got[d] for d in range(size)]


def scatter_around(pieces, shift):
    size = len(pieces)
    order = sorted(range(1, size), key=lambda d: -min(d, size - d))
    got = [shift(pieces[d], d) for d in order]
    total = pieces[0]
    for piece in got:
        total = total + piece.astype(f32)
    return total


def turn(x, start, size):
    return lax.dynamic_slice_in_dim(jnp.concatenate([x, x], axis=0), start, size, axis=0)


def to_all(x):
    return lax.all_to_all(jnp.broadcast_to(x[None], (GROUPS,) + x.shape), "seq", 0, 0, tiled=True)


def gram_body(at_ref, *refs):
    pieces, refs = refs[:NT], refs[NT:]
    key_ref, key_teacher_ref, row_teacher_ref, spread_ref = refs[:4]
    own_ref, others = refs[4], refs[5 : 5 + NT - 1]
    row_ref, grad_ref, total_ref = refs[5 + NT - 1 :]
    at = at_ref[0]
    contract = (((1,), (1,)), ((), ()))
    counts = jnp.zeros((16, E_WIDE - E), f32)
    for d in range(NT):
        spot = pl.multiple_of(lax.rem(at + d, NT) * SHARD, SHARD)
        row_ref[pl.ds(spot, SHARD), :] = pieces[d][:, :E]
        counts = counts + pieces[d][:16, E:].astype(f32)
    tile = jnp.dot(counts.astype(bf16), spread_ref[...], preferred_element_type=f32) * (E / 8.0)
    step = 256
    for k in range(0, GROUPS * SHARD, step):
        span = pl.ds(k, step)
        diff = lax.dot_general(
            row_ref[...], key_ref[span, :], contract, preferred_element_type=f32
        ) - lax.dot_general(
            row_teacher_ref[...], key_teacher_ref[span, :], contract, preferred_element_type=f32
        )
        for a in range(RB):
            grad_ref[pl.ds(a * BLK, BLK), span] = (
                diff[a * BLK : (a + 1) * BLK] * tile[a : a + 1, k : k + step]
            ).astype(bf16)
    for c, wide in ((0, 768), (768, 640)):
        total_ref[:, pl.ds(c, wide)] = jnp.dot(
            grad_ref[...], key_ref[:, pl.ds(c, wide)], preferred_element_type=f32
        )
    for d in range(NT):
        spot = pl.multiple_of(lax.rem(at + d, NT) * SHARD, SHARD)
        block = total_ref[pl.ds(spot, SHARD), :]
        if d == 0:
            own_ref[...] = block
        else:
            others[d - 1][...] = block.astype(bf16)


def gram_grads(at, pieces, keys, key_teacher, row_teacher, spread):
    vmem = pl.BlockSpec(memory_space=pltpu.VMEM)
    return pl.pallas_call(
        gram_body,
        out_shape=[jax.ShapeDtypeStruct((SHARD, E), f32)]
        + [jax.ShapeDtypeStruct((SHARD, E), bf16)] * (NT - 1),
        in_specs=[pl.BlockSpec(memory_space=pltpu.SMEM)] + [vmem] * (NT + 4),
        out_specs=[vmem] * NT,
        scratch_shapes=[
            pltpu.VMEM((ROWS, E), bf16),
            pltpu.VMEM((ROWS, GROUPS * SHARD), bf16),
            pltpu.VMEM((ROWS, E), f32),
        ],
        compiler_params=pltpu.CompilerParams(vmem_limit_bytes=40 * 1024 * 1024),
        cost_estimate=pl.CostEstimate(flops=2_500_000_000, bytes_accessed=9_000_000, transcendentals=0),
        name="gram_grads",
    )(at, *pieces, keys, key_teacher, row_teacher, spread)


def on_device(hidden_states, w_in, w_out, teacher, patch_map, row_pick, key_pick):
    seq_index = lax.axis_index("seq")
    tp_index = lax.axis_index("tp")
    tea_index = lax.axis_index("tea")
    at = jnp.full((1,), tp_index, jnp.int32)
    block_ids = jnp.arange(RB, dtype=jnp.int32)
    contract = (((1,), (1,)), ((), ()))

    pre_act = jnp.dot(hidden_states, w_in, preferred_element_type=f32)
    pre_act = turn(pre_act, tp_index * SHARD, ROWS)
    activation = jax.nn.silu(pre_act).astype(bf16)
    partial_out = jnp.dot(activation, w_out, preferred_element_type=f32)
    chunks = [partial_out[:SHARD]] + [
        partial_out[d * SHARD : (d + 1) * SHARD].astype(bf16) for d in range(1, NT)
    ]
    *chunks, teacher, row_pick = lax.optimization_barrier((*chunks, teacher, row_pick))
    projected = scatter_around(chunks, shift_tp)

    teacher_rows = teacher.shape[0]
    teacher_f = teacher.astype(f32)
    teacher_unit = (
        teacher_f * lax.rsqrt(jnp.sum(teacher_f * teacher_f, axis=-1, keepdims=True) + eps)
    ).astype(bf16)
    local_patch = patch_map - lax.axis_index(("seq", "tea")) * teacher_rows
    patch_hot = (local_patch[:, None] == jnp.arange(teacher_rows, dtype=jnp.int32)[None, :]).astype(bf16)
    row_teacher = jnp.dot(patch_hot, teacher_unit, preferred_element_type=f32).astype(bf16)
    own_teacher = lax.dynamic_slice_in_dim(row_teacher, tp_index * SHARD, SHARD, axis=0)
    key_teacher = lax.all_gather(own_teacher, "seq", axis=0, tiled=True)

    picks = row_pick.reshape(GROUPS)
    sent = jnp.broadcast_to(picks.astype(f32)[:, None, None], (GROUPS, 8, 128))
    theirs = lax.all_to_all(sent, "seq", 0, 0, tiled=True)[:, 0, 0]
    table = key_pick.reshape(GROUPS, GROUPS)
    fits = lambda v: (v[:, None].astype(jnp.int32) == block_ids[None, :]).astype(f32)
    row_side = fits(picks)
    key_side = fits(lax.dynamic_index_in_dim(table, seq_index, axis=0, keepdims=False))
    other_row = fits(theirs)
    other_key = fits(lax.dynamic_index_in_dim(table, seq_index, axis=1, keepdims=False))
    counts = row_side.T[:, :, None] * key_side[None] + other_key.T[:, :, None] * other_row[None]
    counts = jnp.pad(
        counts.reshape(RB, GROUPS * RB).astype(bf16), ((0, SHARD - RB), (0, E_WIDE - E - GROUPS * RB))
    )
    key_ids = jnp.arange(GROUPS * SHARD, dtype=jnp.int32)
    key_cell = key_ids // SHARD * RB + (tp_index * SHARD + key_ids % SHARD) // BLK
    spread = (jnp.arange(E_WIDE - E, dtype=jnp.int32)[:, None] == key_cell[None, :]).astype(bf16)

    inv_norm = lax.rsqrt(jnp.sum(projected * projected, axis=-1, keepdims=True) + eps)
    unit_student = projected * inv_norm
    student_bf = unit_student.astype(bf16)
    pieces = gather_around(jnp.concatenate([student_bf, counts], axis=1), shift_tp, NT)
    keys = to_all(student_bf).reshape(GROUPS * SHARD, E)

    row_grad = gram_grads(at, pieces, keys, key_teacher, row_teacher, spread)
    unit_grad = scatter_around(row_grad, shift_tp)
    inner = jnp.sum(unit_student * unit_grad, axis=-1, keepdims=True)
    grad_proj = ((unit_grad - unit_student * inner) * inv_norm).astype(bf16)
    grad_proj = jnp.concatenate(gather_around(grad_proj, shift_tp, NT), axis=0)

    grad_act = lax.dot_general(grad_proj, w_out, contract, preferred_element_type=f32)
    sigma = jax.nn.sigmoid(pre_act)
    grad_pre = (grad_act * sigma * (1.0 + pre_act * (1.0 - sigma))).astype(bf16)
    grad_pre = turn(grad_pre, (NT - tp_index) % NT * SHARD, ROWS)
    hidden_terms = lax.dot_general(grad_pre, w_in, contract, preferred_element_type=f32).astype(bf16)
    grad_hidden = lax.psum_scatter(hidden_terms, "tp", scatter_dimension=1, tiled=True).astype(f32)

    over_rows = (((0,), (0,)), ((), ()))
    local_w_out = lax.dot_general(grad_proj, activation, over_rows, preferred_element_type=f32)
    local_w_in = lax.dot_general(hidden_states, grad_pre, over_rows, preferred_element_type=f32)
    d_model, width = local_w_in.shape
    in_rows = d_model // 2 // GROUPS
    out_rows = E_PAD // 2 // GROUPS
    local_w_out = jnp.pad(local_w_out, ((0, E_PAD - E), (0, 0)))
    local = jnp.concatenate(
        [
            local_w_in.reshape(2, GROUPS, in_rows, width),
            local_w_out.reshape(2, GROUPS, out_rows, width),
        ],
        axis=2,
    )
    keep = lax.dynamic_index_in_dim(local, tea_index, axis=0, keepdims=False)
    give = lax.dynamic_index_in_dim(local, 1 - tea_index, axis=0, keepdims=False).astype(bf16)
    chip = (keep + swap_tea(give).astype(f32)).astype(bf16)
    chip = lax.all_to_all(chip, "seq", 0, 0, tiled=True)
    mine = jnp.sum(chip.astype(f32), axis=0).astype(bf16)
    mine = to_all(mine).reshape(GROUPS, in_rows + out_rows, width)
    other = swap_tea(mine)
    first = tea_index == 0
    low_half = jnp.where(first, mine, other)
    high_half = jnp.where(first, other, mine)
    summed = jnp.stack([low_half, high_half])
    grad_w_in = summed[:, :, :in_rows].reshape(d_model, width).astype(f32)
    grad_w_out = summed[:, :, in_rows:].reshape(E_PAD, width)[:E].T.astype(f32)
    return (grad_hidden, grad_w_in, grad_w_out)


def solution(mesh):
    return jax.shard_map(
        on_device,
        mesh=mesh,
        in_specs=(
            P(("seq", "tea"), None),
            P(None, "tp"),
            P("tp", None),
            P(("seq", "tea"), None),
            P(("seq", "tea")),
            P("seq", "tp", "tea", None),
            P(None, "tp", "tea", None),
        ),
        out_specs=(P(("seq", "tea"), "tp"), P(None, "tp"), P("tp", None)),
        check_vma=False,
    )
```

```python
import jax
import jax.numpy as jnp
from jax import lax
from jax.experimental import pallas as pl
from jax.experimental.pallas import tpu as pltpu
from jax.sharding import PartitionSpec as P

E = 1408
BLK = 128
RB = 3
SIDE = 4
NT = 8
GROUPS = SIDE * SIDE
SHARD = 48
ROWS = 384
E_WIDE = 1536
E_PAD = 1536

eps = 1e-06
bf16 = jnp.bfloat16
f32 = jnp.float32


def shift_tp(x, step):
    return lax.ppermute(x, "tp", [(i, (i + step) % NT) for i in range(NT)])


def swap_tea(x):
    return lax.ppermute(x, "tea", [(0, 1), (1, 0)])


def gather_around(x, shift, size):
    order = sorted(range(1, size), key=lambda d: -min(d, size - d))
    got = {0: x}
    for d in order:
        got[size - d] = shift(x, d)
    return [got[d] for d in range(size)]


def scatter_around(pieces, shift):
    size = len(pieces)
    order = sorted(range(1, size), key=lambda d: -min(d, size - d))
    order = [1] + [d for d in order if d != 1]
    return [shift(pieces[d], d) for d in order]


def to_all(x):
    return lax.all_to_all(jnp.broadcast_to(x[None], (GROUPS,) + x.shape), "seq", 0, 0, tiled=True)


def in_vmem(count):
    return [pl.BlockSpec(memory_space=pltpu.VMEM)] * count


def in_place(count):
    return [pl.BlockSpec(memory_space=pl.ANY)] * count


IN_SMEM = pl.BlockSpec(memory_space=pltpu.SMEM)
ROOMY = pltpu.CompilerParams(vmem_limit_bytes=44 * 1024 * 1024)


def spot_of(at, d):
    return pl.multiple_of(lax.rem(at + d, NT) * SHARD, SHARD)


def chunk_out(total_ref, at, own_ref, others):
    for d in range(NT):
        block = total_ref[pl.ds(spot_of(at, d), SHARD), :]
        if d == 0:
            own_ref[...] = block
        else:
            others[d - 1][...] = block.astype(bf16)


CHUNKS = [jax.ShapeDtypeStruct((SHARD, E), f32)] + [jax.ShapeDtypeStruct((SHARD, E), bf16)] * (NT - 1)


def forward_body(at_ref, hidden_hbm, w_in_hbm, w_out_hbm, pre_ref, act_ref, *refs):
    own_ref, others = refs[0], refs[1:NT]
    hidden_ref, w_in_ref, w_out_ref, total_ref, sems = refs[NT:]
    parts = hidden_ref.shape[0]
    deep = hidden_ref.shape[2]
    copies = []
    for p in range(parts):
        span = pl.ds(p * deep, deep)
        copies.append(
            (
                pltpu.make_async_copy(hidden_hbm.at[:, span], hidden_ref.at[p], sems.at[2 * p]),
                pltpu.make_async_copy(w_in_hbm.at[span, :], w_in_ref.at[p], sems.at[2 * p + 1]),
            )
        )
    last = pltpu.make_async_copy(w_out_hbm, w_out_ref, sems.at[2 * parts])
    for pair in copies:
        pair[0].start()
        pair[1].start()
    last.start()
    pre = jnp.zeros(pre_ref.shape, f32)
    for p in range(parts):
        copies[p][0].wait()
        copies[p][1].wait()
        pre = pre + jnp.dot(hidden_ref[p], w_in_ref[p], preferred_element_type=f32)
    pre_ref[...] = pre
    act = (pre / (1.0 + jnp.exp(-pre))).astype(bf16)
    act_ref[...] = act
    last.wait()
    total_ref[...] = jnp.dot(act, w_out_ref[...], preferred_element_type=f32)
    chunk_out(total_ref, at_ref[0], own_ref, others)


def forward(at, hidden_states, w_in, w_out):
    rows, d_model = hidden_states.shape
    width = w_in.shape[1]
    parts = 4
    return pl.pallas_call(
        forward_body,
        out_shape=[jax.ShapeDtypeStruct((rows, width), f32), jax.ShapeDtypeStruct((rows, width), bf16)] + CHUNKS,
        in_specs=[IN_SMEM] + in_place(3),
        out_specs=in_vmem(2 + NT),
        scratch_shapes=[
            pltpu.VMEM((parts, rows, d_model // parts), bf16),
            pltpu.VMEM((parts, d_model // parts, width), bf16),
            pltpu.VMEM((width, E), bf16),
            pltpu.VMEM((rows, E), f32),
            pltpu.SemaphoreType.DMA((2 * parts + 1,)),
        ],
        compiler_params=ROOMY,
        cost_estimate=pl.CostEstimate(flops=900_000_000, bytes_accessed=8_000_000, transcendentals=100_000),
        name="forward",
    )(at, hidden_states, w_in, w_out)


def gram_body(at_ref, rows_hbm, keys_hbm, teacher_hbm, spread_ref, own_ref, *refs):
    others = refs[: NT - 1]
    row_ref, key_ref, teacher_ref, grad_ref, total_ref, sems = refs[NT - 1 :]
    contract = (((1,), (1,)), ((), ()))
    step = 256
    spans = [pl.ds(k, step) for k in range(0, GROUPS * SHARD, step)]
    row_copy = pltpu.make_async_copy(rows_hbm, row_ref, sems.at[0])
    row_copy.start()
    copies = []
    for i, span in enumerate(spans):
        pair = (
            pltpu.make_async_copy(keys_hbm.at[span, :], key_ref.at[span, :], sems.at[1 + 2 * i]),
            pltpu.make_async_copy(teacher_hbm.at[:, span], teacher_ref.at[:, span], sems.at[2 + 2 * i]),
        )
        pair[0].start()
        pair[1].start()
        copies.append(pair)
    row_copy.wait()
    counts = jnp.zeros((16, E_WIDE - E), f32)
    for d in range(NT):
        counts = counts + row_ref[pl.ds(d * SHARD, 16), E:].astype(f32)
    tile = jnp.dot(counts.astype(bf16), spread_ref[...], preferred_element_type=f32) * (E / 8.0)
    for i, span in enumerate(spans):
        copies[i][0].wait()
        copies[i][1].wait()
        diff = (
            lax.dot_general(row_ref[:, :E], key_ref[span, :], contract, preferred_element_type=f32)
            - teacher_ref[:, span]
        )
        for a in range(RB):
            grad_ref[pl.ds(a * BLK, BLK), span] = (
                diff[a * BLK : (a + 1) * BLK] * tile[a : a + 1, i * step : (i + 1) * step]
            ).astype(bf16)
    for c, wide in ((0, 768), (768, 640)):
        total_ref[:, pl.ds(c, wide)] = jnp.dot(
            grad_ref[...], key_ref[:, pl.ds(c, wide)], preferred_element_type=f32
        )
    chunk_out(total_ref, at_ref[0], own_ref, others)


def gram_grads(at, rows, keys, gram_teacher, spread):
    steps = GROUPS * SHARD // 256
    return pl.pallas_call(
        gram_body,
        out_shape=CHUNKS,
        in_specs=[IN_SMEM] + in_place(3) + in_vmem(1),
        out_specs=in_vmem(NT),
        scratch_shapes=[
            pltpu.VMEM((ROWS, E_WIDE), bf16),
            pltpu.VMEM((GROUPS * SHARD, E), bf16),
            pltpu.VMEM((ROWS, GROUPS * SHARD), f32),
            pltpu.VMEM((ROWS, GROUPS * SHARD), bf16),
            pltpu.VMEM((ROWS, E), f32),
            pltpu.SemaphoreType.DMA((1 + 2 * steps,)),
        ],
        compiler_params=ROOMY,
        cost_estimate=pl.CostEstimate(flops=1_700_000_000, bytes_accessed=9_000_000, transcendentals=0),
        name="gram_grads",
    )(at, rows, keys, gram_teacher, spread)


def backward_body(at_ref, *refs):
    pieces, refs = refs[:NT], refs[NT:]
    hidden_ref, w_in_ref, w_out_ref, pre_ref, act_ref = refs[:5]
    keep_ref, give_ref, terms_ref, proj_ref, sems = refs[5:]
    at, tea = at_ref[0], at_ref[1]
    contract = (((1,), (1,)), ((), ()))
    over_rows = (((0,), (0,)), ((), ()))
    copies = [
        pltpu.make_async_copy(pieces[d], proj_ref.at[pl.ds(spot_of(at, d), SHARD), pl.ds(0, E)], sems.at[d])
        for d in range(NT)
    ]
    for copy in copies:
        copy.start()
    proj_ref[:, E:] = jnp.zeros((ROWS, E_PAD - E), bf16)
    pre = pre_ref[...]
    sigma = 1.0 / (1.0 + jnp.exp(-pre))
    slope = sigma * (1.0 + pre * (1.0 - sigma))
    for copy in copies:
        copy.wait()
    grad_act = lax.dot_general(proj_ref[:, :E], w_out_ref[...], contract, preferred_element_type=f32)
    grad_pre = (grad_act * slope).astype(bf16)
    d_half, e_half = hidden_ref.shape[1] // 2, E_PAD // 2
    in_rows, out_rows = d_half // GROUPS, e_half // GROUPS
    for ref, side in ((give_ref, 1 - tea), (keep_ref, tea)):
        part = hidden_ref[:, pl.ds(pl.multiple_of(side * d_half, d_half), d_half)]
        grad = lax.dot_general(part, grad_pre, over_rows, preferred_element_type=f32)
        for c in range(GROUPS):
            ref[c, pl.ds(0, in_rows), :] = grad[c * in_rows : (c + 1) * in_rows].astype(ref.dtype)
        part = proj_ref[:, pl.ds(pl.multiple_of(side * e_half, e_half), e_half)]
        grad = lax.dot_general(part, act_ref[...], over_rows, preferred_element_type=f32)
        for c in range(GROUPS):
            ref[c, pl.ds(in_rows, out_rows), :] = grad[c * out_rows : (c + 1) * out_rows].astype(ref.dtype)
    share = w_in_ref.shape[0] // NT
    for d in range(NT):
        terms_ref[pl.ds(d * ROWS, ROWS), :] = lax.dot_general(
            grad_pre, w_in_ref[pl.ds(d * share, share), :], contract, preferred_element_type=f32
        ).astype(terms_ref.dtype)


def backward(where, pieces, hidden_states, w_in, w_out, pre_act, activation):
    d_model, width = w_in.shape
    half_rows = (d_model + E_PAD) // 2 // GROUPS
    return pl.pallas_call(
        backward_body,
        out_shape=[
            jax.ShapeDtypeStruct((GROUPS, half_rows, width), f32),
            jax.ShapeDtypeStruct((GROUPS, half_rows, width), bf16),
            jax.ShapeDtypeStruct((NT * ROWS, d_model // NT), bf16),
        ],
        in_specs=[IN_SMEM] + in_place(NT) + in_vmem(5),
        out_specs=in_vmem(3),
        scratch_shapes=[pltpu.VMEM((ROWS, E_PAD), bf16), pltpu.SemaphoreType.DMA((NT,))],
        compiler_params=ROOMY,
        cost_estimate=pl.CostEstimate(flops=1_800_000_000, bytes_accessed=12_000_000, transcendentals=100_000),
        name="backward",
    )(where, *pieces, hidden_states, w_in, w_out, pre_act, activation)


def final_body(tea_ref, mine_ref, other_ref, w_in_ref, w_out_ref, flat_ref):
    tea = tea_ref[0]
    d_half, e_half = w_in_ref.shape[0] // 2, E_PAD // 2
    in_rows, out_rows = d_half // GROUPS, e_half // GROUPS
    for ref, side in ((mine_ref, tea), (other_ref, 1 - tea)):
        d_at = pl.multiple_of(side * d_half, d_half)
        e_at = pl.multiple_of(side * e_half, e_half)
        for c in range(GROUPS):
            w_in_ref[pl.ds(d_at + c * in_rows, in_rows), :] = ref[c, pl.ds(0, in_rows), :].astype(f32)
            flat_ref[pl.ds(e_at + c * out_rows, out_rows), :] = ref[c, pl.ds(in_rows, out_rows), :].astype(f32)
    for c in range(0, E, BLK):
        w_out_ref[:, pl.ds(c, BLK)] = flat_ref[pl.ds(c, BLK), :].T


def final_layout(tea, mine, other, d_model):
    width = mine.shape[-1]
    return pl.pallas_call(
        final_body,
        out_shape=[jax.ShapeDtypeStruct((d_model, width), f32), jax.ShapeDtypeStruct((width, E), f32)],
        in_specs=[IN_SMEM] + in_vmem(2),
        out_specs=in_vmem(2),
        scratch_shapes=[pltpu.VMEM((E_PAD, width), f32)],
        compiler_params=ROOMY,
        cost_estimate=pl.CostEstimate(flops=0, bytes_accessed=7_000_000, transcendentals=0),
        name="final_layout",
    )(tea, mine, other)


def on_device(hidden_states, w_in, w_out, teacher, patch_map, row_pick, key_pick):
    seq_index = lax.axis_index("seq")
    tp_index = lax.axis_index("tp")
    tea_index = lax.axis_index("tea")
    at = jnp.full((1,), tp_index, jnp.int32)
    tea = jnp.full((1,), tea_index, jnp.int32)
    block_ids = jnp.arange(RB, dtype=jnp.int32)
    contract = (((1,), (1,)), ((), ()))

    pre_act, activation, *chunks = forward(at, hidden_states, w_in, w_out)
    received = scatter_around(chunks, shift_tp)
    nearby = received[0]
    projected = chunks[0]
    for piece in received:
        projected = projected + piece.astype(f32)

    nearby, teacher, row_pick = lax.optimization_barrier((nearby, teacher, row_pick))
    teacher_rows = teacher.shape[0]
    teacher_f = teacher.astype(f32)
    teacher_unit = (
        teacher_f * lax.rsqrt(jnp.sum(teacher_f * teacher_f, axis=-1, keepdims=True) + eps)
    ).astype(bf16)
    local_patch = patch_map - lax.axis_index(("seq", "tea")) * teacher_rows
    patch_hot = (local_patch[:, None] == jnp.arange(teacher_rows, dtype=jnp.int32)[None, :]).astype(bf16)
    row_teacher = jnp.dot(patch_hot, teacher_unit, preferred_element_type=f32).astype(bf16)
    own_teacher = lax.dynamic_slice_in_dim(row_teacher, tp_index * SHARD, SHARD, axis=0)
    key_teacher = to_all(own_teacher).reshape(GROUPS * SHARD, E)
    gram_teacher = lax.dot_general(row_teacher, key_teacher, contract, preferred_element_type=f32)

    picks = row_pick.reshape(GROUPS)
    sent = jnp.broadcast_to(picks.astype(f32)[:, None, None], (GROUPS, 8, 128))
    theirs = lax.all_to_all(sent, "seq", 0, 0, tiled=True)[:, 0, 0]
    table = key_pick.reshape(GROUPS, GROUPS)
    fits = lambda v: (v[:, None].astype(jnp.int32) == block_ids[None, :]).astype(f32)
    row_side = fits(picks)
    key_side = fits(lax.dynamic_index_in_dim(table, seq_index, axis=0, keepdims=False))
    other_row = fits(theirs)
    other_key = fits(lax.dynamic_index_in_dim(table, seq_index, axis=1, keepdims=False))
    counts = row_side.T[:, :, None] * key_side[None] + other_key.T[:, :, None] * other_row[None]
    counts = jnp.pad(
        counts.reshape(RB, GROUPS * RB).astype(bf16), ((0, SHARD - RB), (0, E_WIDE - E - GROUPS * RB))
    )
    key_ids = jnp.arange(GROUPS * SHARD, dtype=jnp.int32)
    key_cell = key_ids // SHARD * RB + (tp_index * SHARD + key_ids % SHARD) // BLK
    spread = (jnp.arange(E_WIDE - E, dtype=jnp.int32)[:, None] == key_cell[None, :]).astype(bf16)

    inv_norm = lax.rsqrt(jnp.sum(projected * projected, axis=-1, keepdims=True) + eps)
    unit_student = projected * inv_norm
    student_bf = unit_student.astype(bf16)
    rows = lax.all_gather(jnp.concatenate([student_bf, counts], axis=1), "tp", axis=0, tiled=True)
    keys = to_all(student_bf).reshape(GROUPS * SHARD, E)

    row_grad = gram_grads(at, rows, keys, gram_teacher, spread)
    unit_grad = row_grad[0]
    for piece in scatter_around(row_grad, shift_tp):
        unit_grad = unit_grad + piece.astype(f32)
    inner = jnp.sum(unit_student * unit_grad, axis=-1, keepdims=True)
    grad_proj = ((unit_grad - unit_student * inner) * inv_norm).astype(bf16)
    pieces = gather_around(grad_proj, shift_tp, NT)

    where = jnp.concatenate([at, tea])
    keep, give, hidden_terms = backward(where, pieces, hidden_states, w_in, w_out, pre_act, activation)
    grad_hidden = lax.psum_scatter(hidden_terms, "tp", scatter_dimension=0, tiled=True).astype(f32)
    chip = (keep + swap_tea(give).astype(f32)).astype(bf16)
    chip = lax.all_to_all(chip, "seq", 0, 0, tiled=True)
    mine = to_all(jnp.sum(chip.astype(f32), axis=0).astype(bf16)).reshape(keep.shape)
    other = swap_tea(mine)
    grad_w_in, grad_w_out = final_layout(tea, mine, other, hidden_states.shape[1])
    return (grad_hidden, grad_w_in, grad_w_out)


def solution(mesh):
    return jax.shard_map(
        on_device,
        mesh=mesh,
        in_specs=(
            P(("seq", "tea"), None),
            P(None, "tp"),
            P("tp", None),
            P(("seq", "tea"), None),
            P(("seq", "tea")),
            P("seq", "tp", "tea", None),
            P(None, "tp", "tea", None),
        ),
        out_specs=(P(("seq", "tea"), "tp"), P(None, "tp"), P("tp", None)),
        check_vma=False,
    )
```

```python
import jax
import jax.numpy as jnp
from jax import lax
from jax.experimental import pallas as pl
from jax.experimental.pallas import tpu as pltpu
from jax.sharding import PartitionSpec as P

E = 1408
BLK = 128
RB = 3
SIDE = 4
NT = 8
GROUPS = SIDE * SIDE
SHARD = 48
ROWS = 384
E_WIDE = 1536
E_PAD = 1536

eps = 1e-06
bf16 = jnp.bfloat16
f32 = jnp.float32


def shift_tp(x, step):
    return lax.ppermute(x, "tp", [(i, (i + step) % NT) for i in range(NT)])


def swap_tea(x):
    return lax.ppermute(x, "tea", [(0, 1), (1, 0)])


def gather_around(x, shift, size):
    order = sorted(range(1, size), key=lambda d: -min(d, size - d))
    got = {0: x}
    for d in order:
        got[size - d] = shift(x, d)
    return [got[d] for d in range(size)]


def scatter_around(pieces, shift, order):
    return [shift(pieces[d], d) for d in order]


def to_all(x):
    return lax.all_to_all(jnp.broadcast_to(x[None], (GROUPS,) + x.shape), "seq", 0, 0, tiled=True)


def in_vmem(count):
    return [pl.BlockSpec(memory_space=pltpu.VMEM)] * count


def in_place(count):
    return [pl.BlockSpec(memory_space=pltpu.HBM)] * count


def hbm(x):
    return pltpu.with_memory_space_constraint(x, pltpu.HBM)


IN_SMEM = pl.BlockSpec(memory_space=pltpu.SMEM)
def scoped(mib):
    return pltpu.CompilerParams(vmem_limit_bytes=mib * 1024 * 1024)


PIECE_ORDER = (0, 1, 7, 2, 6, 3, 5, 4)


def spot_of(at, d):
    return pl.multiple_of(lax.rem(at + d, NT) * SHARD, SHARD)


def chunk_out(total_ref, at, own_hbm, others, stage_ref, sems):
    copies = []
    for d in range(1, NT):
        stage_ref[d - 1] = total_ref[pl.ds(spot_of(at, d), SHARD), :].astype(bf16)
        copies.append(pltpu.make_async_copy(stage_ref.at[d - 1], others[d - 1], sems.at[d]))
        copies[-1].start()
    copies.append(pltpu.make_async_copy(total_ref.at[pl.ds(spot_of(at, 0), SHARD), :], own_hbm, sems.at[0]))
    copies[-1].start()
    return copies


STAGE = [pltpu.VMEM((NT - 1, SHARD, E), bf16), pltpu.SemaphoreType.DMA((NT,))]
CHUNKS = [pltpu.HBM((SHARD, E), f32)] + [pltpu.HBM((SHARD, E), bf16)] * (NT - 1)


def align_body(at_ref, teacher_ref, patch_ref, picks_ref, rows_hbm, send_hbm, rows_ref, own_ref, extra_ref, sems):
    teacher = teacher_ref[...].astype(f32)
    unit = (teacher * lax.rsqrt(jnp.sum(teacher * teacher, axis=-1, keepdims=True) + eps)).astype(bf16)
    ids = lax.broadcasted_iota(jnp.int32, (teacher.shape[0], ROWS), 0)
    hot = (ids == patch_ref[...]).astype(f32).astype(bf16)
    rows_ref[...] = lax.dot_general(
        hot, unit, (((0,), (0,)), ((), ())), preferred_element_type=f32
    ).astype(bf16)
    copies = [pltpu.make_async_copy(rows_ref, rows_hbm, sems.at[GROUPS])]
    copies[0].start()
    own_ref[...] = rows_ref[pl.ds(spot_of(at_ref[0], 0), SHARD), :]
    for j in range(GROUPS):
        copies.append(pltpu.make_async_copy(own_ref, send_hbm.at[j, :, pl.ds(0, E)], sems.at[j]))
        copies[-1].start()
    for j in range(GROUPS):
        extra_ref[j] = jnp.full(extra_ref.shape[1:], picks_ref[j], jnp.int32).astype(f32).astype(bf16)
    copies.append(pltpu.make_async_copy(extra_ref, send_hbm.at[:, :, pl.ds(E, E_WIDE - E)], sems.at[GROUPS + 1]))
    copies[-1].start()
    for copy in copies:
        copy.wait()


def align(at, teacher, patch, picks):
    return pl.pallas_call(
        align_body,
        out_shape=[
            pltpu.HBM((ROWS, E), bf16),
            pltpu.HBM((GROUPS, SHARD, E_WIDE), bf16),
        ],
        in_specs=[IN_SMEM] + in_vmem(2) + [IN_SMEM],
        out_specs=in_place(2),
        scratch_shapes=[
            pltpu.VMEM((ROWS, E), bf16),
            pltpu.VMEM((SHARD, E), bf16),
            pltpu.VMEM((GROUPS, SHARD, E_WIDE - E), bf16),
            pltpu.SemaphoreType.DMA((GROUPS + 2,)),
        ],
        compiler_params=scoped(12),
        cost_estimate=pl.CostEstimate(flops=250_000_000, bytes_accessed=4_000_000, transcendentals=0),
        name="align",
    )(at, teacher, patch, picks)


def forward_body(at_ref, hidden_ref, w_in_ref, w_out_ref, pre_hbm, act_hbm, *refs):
    own_hbm, others = refs[0], refs[1:NT]
    total_ref, pre_ref, act_ref, sems, stage_ref, stage_sems = refs[NT:]
    pre = jnp.dot(hidden_ref[...], w_in_ref[...], preferred_element_type=f32)
    pre_ref[...] = pre
    act = (pre / (1.0 + jnp.exp(-pre))).astype(bf16)
    act_ref[...] = act
    copies = [
        pltpu.make_async_copy(pre_ref, pre_hbm, sems.at[0]),
        pltpu.make_async_copy(act_ref, act_hbm, sems.at[1]),
    ]
    for copy in copies:
        copy.start()
    total_ref[...] = jnp.dot(act, w_out_ref[...], preferred_element_type=f32)
    copies += chunk_out(total_ref, at_ref[0], own_hbm, others, stage_ref, stage_sems)
    for copy in copies:
        copy.wait()


def forward(at, hidden_states, w_in, w_out):
    rows, width = hidden_states.shape[0], w_in.shape[1]
    return pl.pallas_call(
        forward_body,
        out_shape=[pltpu.HBM((rows, width), f32), pltpu.HBM((rows, width), bf16)] + CHUNKS,
        in_specs=[IN_SMEM] + in_vmem(3),
        out_specs=in_place(2 + NT),
        scratch_shapes=[
            pltpu.VMEM((rows, E), f32),
            pltpu.VMEM((rows, width), f32),
            pltpu.VMEM((rows, width), bf16),
            pltpu.SemaphoreType.DMA((2,)),
        ]
        + STAGE,
        compiler_params=scoped(16),
        cost_estimate=pl.CostEstimate(flops=900_000_000, bytes_accessed=8_000_000, transcendentals=100_000),
        name="forward",
    )(at, hidden_states, w_in, w_out)


def normalise_body(local_ref, own_hbm, theirs_hbm, *refs):
    parts, refs = refs[: NT - 1], refs[NT - 1 :]
    unit_hbm, inv_hbm, row_hbm, send_hbm, unit_ref, inv_ref, row_ref, got_ref, theirs_ref, sems = refs
    first = pltpu.make_async_copy(own_hbm, unit_ref, sems.at[NT])
    first.start()
    copies = [pltpu.make_async_copy(parts[i], got_ref.at[i], sems.at[i]) for i in range(NT - 1)]
    picks = pltpu.make_async_copy(
        theirs_hbm.at[:, pl.ds(0, 16), pl.ds(E, E_WIDE - E)], theirs_ref, sems.at[NT - 1]
    )
    for copy in copies:
        copy.start()
    picks.start()
    first.wait()
    total = unit_ref[...]
    for i in range(NT - 1):
        copies[i].wait()
        total = total + got_ref[i].astype(f32)
    inv = lax.rsqrt(jnp.sum(total * total, axis=-1, keepdims=True) + eps)
    unit = total * inv
    row_ref[:, :E] = unit.astype(bf16)
    copies = [
        pltpu.make_async_copy(row_ref.at[:, pl.ds(0, E)], send_hbm.at[j], sems.at[NT + 3 + j]) for j in range(GROUPS)
    ]
    for copy in copies:
        copy.start()
    unit_ref[...] = unit
    inv_ref[...] = jnp.broadcast_to(inv, inv_ref.shape)
    copies.append(pltpu.make_async_copy(unit_ref, unit_hbm, sems.at[NT]))
    copies[-1].start()
    copies.append(pltpu.make_async_copy(inv_ref, inv_hbm, sems.at[NT + 1]))
    copies[-1].start()
    shape = (16, E_WIDE - E)
    lane = lax.broadcasted_iota(jnp.int32, shape, 1)
    block = lax.broadcasted_iota(jnp.int32, shape, 0)
    group, end = lane // RB, lane % RB
    picks.wait()
    other = jnp.zeros(shape, f32)
    for j in range(GROUPS):
        other = other + jnp.where(group == j, theirs_ref[j].astype(f32), 0.0)
    as_row = (local_ref[0:1, :] == block) & (local_ref[1:2, :] == end)
    as_key = (local_ref[2:3, :] == block) & (other.astype(jnp.int32) == end)
    counts = as_row.astype(f32) + as_key.astype(f32)
    counts = jnp.where((group < GROUPS) & (block < RB), counts, 0.0)
    row_ref[:, E:] = jnp.concatenate([counts, jnp.zeros((SHARD - 16, E_WIDE - E), f32)], axis=0).astype(bf16)
    copies.append(pltpu.make_async_copy(row_ref, row_hbm, sems.at[NT + 2]))
    copies[-1].start()
    for copy in copies:
        copy.wait()


def normalise(own, local, theirs, parts):
    return pl.pallas_call(
        normalise_body,
        out_shape=[
            pltpu.HBM((SHARD, E), f32),
            pltpu.HBM((SHARD, BLK), f32),
            pltpu.HBM((SHARD, E_WIDE), bf16),
            pltpu.HBM((GROUPS, SHARD, E), bf16),
        ],
        in_specs=in_vmem(1) + in_place(NT + 1),
        out_specs=in_place(4),
        scratch_shapes=[
            pltpu.VMEM((SHARD, E), f32),
            pltpu.VMEM((SHARD, BLK), f32),
            pltpu.VMEM((SHARD, E_WIDE), bf16),
            pltpu.VMEM((NT - 1, SHARD, E), bf16),
            pltpu.VMEM((GROUPS, 16, E_WIDE - E), bf16),
            pltpu.SemaphoreType.DMA((NT + 3 + GROUPS,)),
        ],
        compiler_params=scoped(12),
        cost_estimate=pl.CostEstimate(flops=1_000_000, bytes_accessed=4_000_000, transcendentals=0),
        name="normalise",
    )(local, hbm(own), hbm(theirs), *[hbm(part) for part in parts])


def gram_body(at_ref, rows_hbm, keys_hbm, teacher_hbm, spread_ref, own_hbm, *refs):
    others = refs[: NT - 1]
    row_ref, key_ref, teacher_ref, grad_ref, total_ref, sems, stage_ref, stage_sems = refs[NT - 1 :]
    contract = (((1,), (1,)), ((), ()))
    step = 256
    spans = [pl.ds(k, step) for k in range(0, GROUPS * SHARD, step)]
    row_copy = pltpu.make_async_copy(rows_hbm, row_ref, sems.at[0])
    row_copy.start()
    copies = []
    for i, span in enumerate(spans):
        pair = (
            pltpu.make_async_copy(keys_hbm.at[span, :], key_ref.at[span, :], sems.at[1 + 2 * i]),
            pltpu.make_async_copy(teacher_hbm.at[:, span], teacher_ref.at[:, span], sems.at[2 + 2 * i]),
        )
        pair[0].start()
        pair[1].start()
        copies.append(pair)
    row_copy.wait()
    counts = jnp.zeros((16, E_WIDE - E), f32)
    for d in range(NT):
        counts = counts + row_ref[pl.ds(d * SHARD, 16), E:].astype(f32)
    tile = jnp.dot(counts.astype(bf16), spread_ref[...], preferred_element_type=f32) * (E / 8.0)
    for i, span in enumerate(spans):
        copies[i][0].wait()
        copies[i][1].wait()
        diff = (
            lax.dot_general(row_ref[:, :E], key_ref[span, :], contract, preferred_element_type=f32)
            - teacher_ref[:, span]
        )
        for a in range(RB):
            grad_ref[pl.ds(a * BLK, BLK), span] = (
                diff[a * BLK : (a + 1) * BLK] * tile[a : a + 1, i * step : (i + 1) * step]
            ).astype(bf16)
    for c, wide in ((0, 768), (768, 640)):
        total_ref[:, pl.ds(c, wide)] = jnp.dot(
            grad_ref[...], key_ref[:, pl.ds(c, wide)], preferred_element_type=f32
        )
    for copy in chunk_out(total_ref, at_ref[0], own_hbm, others, stage_ref, stage_sems):
        copy.wait()


def gram_grads(at, rows, keys, gram_teacher, spread):
    steps = GROUPS * SHARD // 256
    return pl.pallas_call(
        gram_body,
        out_shape=CHUNKS,
        in_specs=[IN_SMEM] + in_place(3) + in_vmem(1),
        out_specs=in_place(NT),
        scratch_shapes=[
            pltpu.VMEM((ROWS, E_WIDE), bf16),
            pltpu.VMEM((GROUPS * SHARD, E), bf16),
            pltpu.VMEM((ROWS, GROUPS * SHARD), f32),
            pltpu.VMEM((ROWS, GROUPS * SHARD), bf16),
            pltpu.VMEM((ROWS, E), f32),
            pltpu.SemaphoreType.DMA((1 + 2 * steps,)),
        ]
        + STAGE,
        compiler_params=scoped(20),
        cost_estimate=pl.CostEstimate(flops=1_700_000_000, bytes_accessed=9_000_000, transcendentals=0),
        name="gram_grads",
    )(at, hbm(rows), hbm(keys), hbm(gram_teacher), spread)


def backward_body(at_ref, *refs):
    pieces, refs = dict(zip(PIECE_ORDER, refs[:NT])), refs[NT:]
    hidden_ref, w_out_ref, pre_ref, act_ref = refs[:4]
    keep_hbm, give_hbm, grad_pre_hbm, keep_ref, give_ref, grad_pre_ref, proj_ref, sems = refs[4:]
    at, tea = at_ref[0], at_ref[1]
    contract = (((1,), (1,)), ((), ()))
    over_rows = (((0,), (0,)), ((), ()))
    copies = [
        pltpu.make_async_copy(pieces[d], proj_ref.at[pl.ds(spot_of(at, d), SHARD), pl.ds(0, E)], sems.at[d])
        for d in range(NT)
    ]
    for copy in copies:
        copy.start()
    proj_ref[:, E:] = jnp.zeros((ROWS, E_PAD - E), bf16)
    pre = pre_ref[...]
    sigma = 1.0 / (1.0 + jnp.exp(-pre))
    slope = sigma * (1.0 + pre * (1.0 - sigma))
    for copy in copies:
        copy.wait()
    grad_act = lax.dot_general(proj_ref[:, :E], w_out_ref[...], contract, preferred_element_type=f32)
    grad_pre = (grad_act * slope).astype(bf16)
    grad_pre_ref[...] = grad_pre
    copies = [pltpu.make_async_copy(grad_pre_ref, grad_pre_hbm, sems.at[0])]
    copies[0].start()
    d_half, e_half = hidden_ref.shape[1] // 2, E_PAD // 2
    in_rows, out_rows = d_half // GROUPS, e_half // GROUPS
    for n, (ref, target, side) in enumerate(((give_ref, give_hbm, 1 - tea), (keep_ref, keep_hbm, tea))):
        part = hidden_ref[:, pl.ds(pl.multiple_of(side * d_half, d_half), d_half)]
        grad = lax.dot_general(part, grad_pre, over_rows, preferred_element_type=f32)
        for c in range(GROUPS):
            ref[c, pl.ds(0, in_rows), :] = grad[c * in_rows : (c + 1) * in_rows].astype(ref.dtype)
        part = proj_ref[:, pl.ds(pl.multiple_of(side * e_half, e_half), e_half)]
        grad = lax.dot_general(part, act_ref[...], over_rows, preferred_element_type=f32)
        for c in range(GROUPS):
            ref[c, pl.ds(in_rows, out_rows), :] = grad[c * out_rows : (c + 1) * out_rows].astype(ref.dtype)
        copies.append(pltpu.make_async_copy(ref, target, sems.at[n + 1]))
        copies[-1].start()
    for copy in copies:
        copy.wait()


def backward(where, pieces, hidden_states, w_out, pre_act, activation):
    rows, d_model = hidden_states.shape
    width = activation.shape[1]
    halves = (GROUPS, (d_model + E_PAD) // 2 // GROUPS, width)
    return pl.pallas_call(
        backward_body,
        out_shape=[pltpu.HBM(halves, f32), pltpu.HBM(halves, bf16), pltpu.HBM((rows, width), bf16)],
        in_specs=[IN_SMEM] + in_place(NT) + in_vmem(4),
        out_specs=in_place(3),
        scratch_shapes=[
            pltpu.VMEM(halves, f32),
            pltpu.VMEM(halves, bf16),
            pltpu.VMEM((rows, width), bf16),
            pltpu.VMEM((ROWS, E_PAD), bf16),
            pltpu.SemaphoreType.DMA((NT,)),
        ],
        compiler_params=scoped(20),
        cost_estimate=pl.CostEstimate(flops=1_200_000_000, bytes_accessed=9_000_000, transcendentals=100_000),
        name="backward",
    )(where, *[pieces[d] for d in PIECE_ORDER], hidden_states, w_out, pre_act, activation)


def hidden_body(grad_pre_ref, w_in_ref, terms_hbm, terms_ref, sems):
    contract = (((1,), (1,)), ((), ()))
    share = w_in_ref.shape[0] // NT
    copies = []
    for d in range(NT):
        span = pl.ds(d * ROWS, ROWS)
        terms_ref[span, :] = lax.dot_general(
            grad_pre_ref[...], w_in_ref[pl.ds(d * share, share), :], contract, preferred_element_type=f32
        ).astype(bf16)
        copies.append(pltpu.make_async_copy(terms_ref.at[span, :], terms_hbm.at[span, :], sems.at[d]))
        copies[-1].start()
    for copy in copies:
        copy.wait()


def hidden_grads(grad_pre, w_in):
    shape = (NT * ROWS, w_in.shape[0] // NT)
    return pl.pallas_call(
        hidden_body,
        out_shape=pltpu.HBM(shape, bf16),
        in_specs=in_vmem(2),
        out_specs=in_place(1)[0],
        scratch_shapes=[pltpu.VMEM(shape, bf16), pltpu.SemaphoreType.DMA((NT,))],
        compiler_params=scoped(12),
        cost_estimate=pl.CostEstimate(flops=600_000_000, bytes_accessed=4_000_000, transcendentals=0),
        name="hidden_grads",
    )(grad_pre, w_in)


def final_body(tea_ref, mine_ref, other_ref, hidden_hbm, w_in_ref, w_out_ref, hidden_ref, flat_ref, got_ref, sem):
    tea = tea_ref[0]
    copy = pltpu.make_async_copy(hidden_hbm, got_ref, sem)
    copy.start()
    d_half, e_half = w_in_ref.shape[0] // 2, E_PAD // 2
    in_rows, out_rows = d_half // GROUPS, e_half // GROUPS
    for ref, side in ((mine_ref, tea), (other_ref, 1 - tea)):
        d_at = pl.multiple_of(side * d_half, d_half)
        e_at = pl.multiple_of(side * e_half, e_half)
        for c in range(GROUPS):
            w_in_ref[pl.ds(d_at + c * in_rows, in_rows), :] = ref[c, pl.ds(0, in_rows), :].astype(f32)
            flat_ref[pl.ds(e_at + c * out_rows, out_rows), :] = ref[c, pl.ds(in_rows, out_rows), :].astype(f32)
    for c in range(0, E, BLK):
        w_out_ref[:, pl.ds(c, BLK)] = flat_ref[pl.ds(c, BLK), :].T
    copy.wait()
    hidden_ref[...] = got_ref[...].astype(f32)


def final_layout(tea, mine, other, hidden, d_model):
    width = mine.shape[-1]
    return pl.pallas_call(
        final_body,
        out_shape=[
            jax.ShapeDtypeStruct((d_model, width), f32),
            jax.ShapeDtypeStruct((width, E), f32),
            jax.ShapeDtypeStruct(hidden.shape, f32),
        ],
        in_specs=[IN_SMEM] + in_vmem(2) + in_place(1),
        out_specs=in_vmem(3),
        scratch_shapes=[
            pltpu.VMEM((E_PAD, width), f32),
            pltpu.VMEM(hidden.shape, bf16),
            pltpu.SemaphoreType.DMA,
        ],
        compiler_params=scoped(12),
        cost_estimate=pl.CostEstimate(flops=0, bytes_accessed=7_000_000, transcendentals=0),
        name="final_layout",
    )(tea, mine, other, hbm(hidden))


def on_device(hidden_states, w_in, w_out, teacher, patch_map, row_pick, key_pick):
    seq_index = lax.axis_index("seq")
    tp_index = lax.axis_index("tp")
    tea_index = lax.axis_index("tea")
    at = jnp.full((1,), tp_index, jnp.int32)
    tea = jnp.full((1,), tea_index, jnp.int32)
    contract = (((1,), (1,)), ((), ()))

    picks = row_pick.reshape(GROUPS)
    local_patch = patch_map - lax.axis_index(("seq", "tea")) * teacher.shape[0]
    row_teacher, teacher_send = align(at, teacher, local_patch.reshape(1, ROWS), picks)
    teacher_send, at_next = lax.optimization_barrier((teacher_send, at))
    teacher_got = lax.all_to_all(teacher_send, "seq", 0, 0, tiled=True)

    pre_act, activation, *chunks = forward(at_next, hidden_states, w_in, w_out)
    activation, key_pick, picks = lax.optimization_barrier((activation, key_pick, picks))
    received = scatter_around(chunks, shift_tp, (1, 7, 2, 6, 4, 3, 5))

    table = key_pick.reshape(GROUPS, GROUPS)
    of_rows = lax.dynamic_index_in_dim(table, seq_index, axis=0, keepdims=False)
    of_keys = lax.dynamic_index_in_dim(table, seq_index, axis=1, keepdims=False)
    local = jnp.repeat(jnp.stack([picks, of_rows, of_keys]), RB, axis=1)
    local = jnp.pad(local, ((0, 8 - 3), (0, E_WIDE - E - GROUPS * RB)))
    key_ids = jnp.arange(GROUPS * SHARD, dtype=jnp.int32)
    key_cell = key_ids // SHARD * RB + (tp_index * SHARD + key_ids % SHARD) // BLK
    spread = (jnp.arange(E_WIDE - E, dtype=jnp.int32)[:, None] == key_cell[None, :]).astype(bf16)

    *received, teacher_got = lax.optimization_barrier((*received, teacher_got))
    unit_student, inv_norm, row_send, key_send = normalise(chunks[0], local, teacher_got, received)
    rows = lax.all_gather(row_send, "tp", axis=0, tiled=True)
    keys = lax.all_to_all(key_send, "seq", 0, 0, tiled=True).reshape(GROUPS * SHARD, E)
    teacher_got, inv_norm = lax.optimization_barrier((teacher_got, inv_norm))
    inv_norm = inv_norm[:, :1]
    key_teacher = teacher_got[:, :, :E].reshape(GROUPS * SHARD, E)
    gram_teacher = lax.dot_general(row_teacher, key_teacher, contract, preferred_element_type=f32)

    row_grad = gram_grads(at, rows, keys, gram_teacher, spread)
    unit_grad = row_grad[0]
    for piece in scatter_around(row_grad, shift_tp, (4, 3, 5, 2, 6, 1, 7)):
        unit_grad = unit_grad + piece.astype(f32)
    inner = jnp.sum(unit_student * unit_grad, axis=-1, keepdims=True)
    grad_proj = ((unit_grad - unit_student * inner) * inv_norm).astype(bf16)
    pieces = gather_around(grad_proj, shift_tp, NT)

    where = jnp.concatenate([at, tea])
    keep, give, grad_pre = backward(where, pieces, hidden_states, w_out, pre_act, activation)
    grad_hidden = lax.psum_scatter(hidden_grads(grad_pre, w_in), "tp", scatter_dimension=0, tiled=True)
    chip = (keep + swap_tea(give).astype(f32)).astype(bf16)
    chip = lax.all_to_all(chip, "seq", 0, 0, tiled=True)
    mine = to_all(jnp.sum(chip.astype(f32), axis=0).astype(bf16)).reshape(keep.shape)
    other = swap_tea(mine)
    grad_w_in, grad_w_out, grad_hidden = final_layout(tea, mine, other, grad_hidden, hidden_states.shape[1])
    return (grad_hidden, grad_w_in, grad_w_out)


def solution(mesh):
    return jax.shard_map(
        on_device,
        mesh=mesh,
        in_specs=(
            P(("seq", "tea"), None),
            P(None, "tp"),
            P("tp", None),
            P(("seq", "tea"), None),
            P(("seq", "tea")),
            P("seq", "tp", "tea", None),
            P(None, "tp", "tea", None),
        ),
        out_specs=(P(("seq", "tea"), "tp"), P(None, "tp"), P("tp", None)),
        check_vma=False,
    )
```

```python
import jax
import jax.numpy as jnp
from jax import lax
from jax.experimental import pallas as pl
from jax.experimental.pallas import tpu as pltpu
from jax.sharding import PartitionSpec as P

E = 1408
BLK = 128
RB = 3
SIDE = 4
NT = 8
GROUPS = SIDE * SIDE
SHARD = 48
ROWS = 384
E_WIDE = 1536
E_PAD = 1536

eps = 1e-06
bf16 = jnp.bfloat16
f32 = jnp.float32


def shift_tp(x, step):
    return lax.ppermute(x, "tp", [(i, (i + step) % NT) for i in range(NT)])


def swap_tea(x):
    return lax.ppermute(x, "tea", [(0, 1), (1, 0)])


LEFT = 768
RIGHT = 640


def gather_ring(x):
    before, after = shift_tp(x, 1), shift_tp(x, -1)
    before2, after2 = shift_tp(x, 2), shift_tp(x, -2)
    before3, after3 = shift_tp(before2, 1), shift_tp(after2, -1)
    left, right = shift_tp(before2[:, :LEFT], 2), shift_tp(after2[:, LEFT:], -2)
    return [x, after, after2, after3, left, right, before3, before2, before]


def sum_ring(own, one, two, three, left, right, five, six, seven):
    three, five = shift_tp(three, 1), shift_tp(five, -1)
    left, right = shift_tp(left, 2), shift_tp(right, -2)
    one, seven = shift_tp(one, 1), shift_tp(seven, -1)
    zeros = jnp.zeros((SHARD, LEFT), f32), jnp.zeros((SHARD, RIGHT), f32)
    two = two + three.astype(f32) + jnp.concatenate([left.astype(f32), zeros[1]], axis=1)
    six = six + five.astype(f32) + jnp.concatenate([zeros[0], right.astype(f32)], axis=1)
    two, six = shift_tp(two.astype(bf16), 2), shift_tp(six.astype(bf16), -2)
    return [one, seven, two, six]


def to_all(x):
    return lax.all_to_all(jnp.broadcast_to(x[None], (GROUPS,) + x.shape), "seq", 0, 0, tiled=True)


def in_vmem(count):
    return [pl.BlockSpec(memory_space=pltpu.VMEM)] * count


def in_place(count):
    return [pl.BlockSpec(memory_space=pltpu.HBM)] * count


def hbm(x):
    return pltpu.with_memory_space_constraint(x, pltpu.HBM)


IN_SMEM = pl.BlockSpec(memory_space=pltpu.SMEM)
def scoped(mib):
    return pltpu.CompilerParams(vmem_limit_bytes=mib * 1024 * 1024)


PIECE_ORDER = (0, 1, 8, 2, 7, 3, 6, 4, 5)


def spot_of(at, d):
    return pl.multiple_of(lax.rem(at + d, NT) * SHARD, SHARD)


def chunk_out(total_ref, at, targets, stage_ref, sems):
    copies = []
    slot = 0
    for n, d, cols in (
        (3, 3, None),
        (6, 5, None),
        (4, 4, pl.ds(0, LEFT)),
        (5, 4, pl.ds(LEFT, RIGHT)),
        (1, 1, None),
        (8, 7, None),
        (2, 2, None),
        (7, 6, None),
        (0, 0, None),
    ):
        rows = pl.ds(spot_of(at, d), SHARD)
        if d in (0, 2, 6):
            source = total_ref.at[rows, :]
        else:
            if n != 5:
                stage_ref[slot] = total_ref[rows, :].astype(bf16)
                slot += 1
            source = stage_ref.at[slot - 1] if cols is None else stage_ref.at[slot - 1, :, cols]
        copies.append(pltpu.make_async_copy(source, targets[n], sems.at[n]))
        copies[-1].start()
    return copies


PARTS = NT + 1
STAGE = [pltpu.VMEM((5, SHARD, E), bf16), pltpu.SemaphoreType.DMA((PARTS,))]
WIDE, FULL = pltpu.HBM((SHARD, E), f32), pltpu.HBM((SHARD, E), bf16)
CHUNKS = [WIDE, FULL, WIDE, FULL, pltpu.HBM((SHARD, LEFT), bf16), pltpu.HBM((SHARD, RIGHT), bf16), FULL, WIDE, FULL]


def align_body(at_ref, teacher_hbm, patch_ref, picks_ref, rows_hbm, send_hbm, teacher_ref, rows_ref, own_ref, extra_ref, sems):
    copy = pltpu.make_async_copy(teacher_hbm, teacher_ref, sems.at[GROUPS])
    copy.start()
    for j in range(GROUPS):
        extra_ref[j] = jnp.full(extra_ref.shape[1:], picks_ref[j], jnp.int32).astype(f32).astype(bf16)
    extra = pltpu.make_async_copy(extra_ref, send_hbm.at[:, :, pl.ds(E, E_WIDE - E)], sems.at[GROUPS + 1])
    extra.start()
    copy.wait()
    teacher = teacher_ref[...].astype(f32)
    unit = (teacher * lax.rsqrt(jnp.sum(teacher * teacher, axis=-1, keepdims=True) + eps)).astype(bf16)
    ids = lax.broadcasted_iota(jnp.int32, (teacher.shape[0], ROWS), 0)
    hot = (ids == patch_ref[...] - at_ref[1] * teacher.shape[0]).astype(f32).astype(bf16)
    rows_ref[...] = lax.dot_general(
        hot, unit, (((0,), (0,)), ((), ())), preferred_element_type=f32
    ).astype(bf16)
    copies = [pltpu.make_async_copy(rows_ref, rows_hbm, sems.at[GROUPS])]
    copies[0].start()
    own_ref[...] = rows_ref[pl.ds(spot_of(at_ref[0], 0), SHARD), :]
    for j in range(GROUPS):
        copies.append(pltpu.make_async_copy(own_ref, send_hbm.at[j, :, pl.ds(0, E)], sems.at[j]))
        copies[-1].start()
    copies.append(extra)
    for copy in copies:
        copy.wait()


def align(at, teacher, patch, picks):
    return pl.pallas_call(
        align_body,
        out_shape=[
            pltpu.HBM((ROWS, E), bf16),
            pltpu.HBM((GROUPS, SHARD, E_WIDE), bf16),
        ],
        in_specs=[IN_SMEM] + in_place(1) + in_vmem(1) + [IN_SMEM],
        out_specs=in_place(2),
        scratch_shapes=[
            pltpu.VMEM(teacher.shape, bf16),
            pltpu.VMEM((ROWS, E), bf16),
            pltpu.VMEM((SHARD, E), bf16),
            pltpu.VMEM((GROUPS, SHARD, E_WIDE - E), bf16),
            pltpu.SemaphoreType.DMA((GROUPS + 2,)),
        ],
        compiler_params=scoped(12),
        cost_estimate=pl.CostEstimate(flops=250_000_000, bytes_accessed=4_000_000, transcendentals=0),
        name="align",
    )(at, hbm(teacher), patch, picks)


def forward_body(at_ref, hidden_ref, w_in_ref, w_out_ref, pre_hbm, act_hbm, *refs):
    targets = refs[:PARTS]
    total_ref, pre_ref, act_ref, sems, stage_ref, stage_sems = refs[PARTS:]
    pre = jnp.dot(hidden_ref[...], w_in_ref[...], preferred_element_type=f32)
    pre_ref[...] = pre
    act = (pre / (1.0 + jnp.exp(-pre))).astype(bf16)
    act_ref[...] = act
    copies = [
        pltpu.make_async_copy(pre_ref, pre_hbm, sems.at[0]),
        pltpu.make_async_copy(act_ref, act_hbm, sems.at[1]),
    ]
    for copy in copies:
        copy.start()
    total_ref[...] = jnp.dot(act, w_out_ref[...], preferred_element_type=f32)
    copies += chunk_out(total_ref, at_ref[0], targets, stage_ref, stage_sems)
    for copy in copies:
        copy.wait()


def forward(at, hidden_states, w_in, w_out):
    rows, width = hidden_states.shape[0], w_in.shape[1]
    return pl.pallas_call(
        forward_body,
        out_shape=[pltpu.HBM((rows, width), f32), pltpu.HBM((rows, width), bf16)] + CHUNKS,
        in_specs=[IN_SMEM] + in_vmem(3),
        out_specs=in_place(2 + PARTS),
        scratch_shapes=[
            pltpu.VMEM((rows, E), f32),
            pltpu.VMEM((rows, width), f32),
            pltpu.VMEM((rows, width), bf16),
            pltpu.SemaphoreType.DMA((2,)),
        ]
        + STAGE,
        compiler_params=scoped(16),
        cost_estimate=pl.CostEstimate(flops=900_000_000, bytes_accessed=8_000_000, transcendentals=100_000),
        name="forward",
    )(at, hidden_states, w_in, w_out)


RECEIVED = 4


def normalise_body(local_ref, own_hbm, theirs_hbm, *refs):
    parts, refs = refs[: RECEIVED], refs[RECEIVED :]
    unit_hbm, inv_hbm, row_hbm, send_hbm, unit_ref, inv_ref, row_ref, got_ref, theirs_ref, sems = refs
    first = pltpu.make_async_copy(own_hbm, unit_ref, sems.at[RECEIVED + 1])
    first.start()
    copies = [pltpu.make_async_copy(parts[i], got_ref.at[i], sems.at[i]) for i in range(RECEIVED)]
    picks = pltpu.make_async_copy(
        theirs_hbm.at[:, pl.ds(0, 16), pl.ds(E, E_WIDE - E)], theirs_ref, sems.at[RECEIVED]
    )
    for copy in copies:
        copy.start()
    picks.start()
    first.wait()
    total = unit_ref[...]
    for i in range(RECEIVED):
        copies[i].wait()
        total = total + got_ref[i].astype(f32)
    inv = lax.rsqrt(jnp.sum(total * total, axis=-1, keepdims=True) + eps)
    unit = total * inv
    row_ref[:, :E] = unit.astype(bf16)
    copies = [
        pltpu.make_async_copy(row_ref.at[:, pl.ds(0, E)], send_hbm.at[j], sems.at[RECEIVED + 4 + j]) for j in range(GROUPS)
    ]
    for copy in copies:
        copy.start()
    unit_ref[...] = unit
    inv_ref[...] = jnp.broadcast_to(inv, inv_ref.shape)
    copies.append(pltpu.make_async_copy(unit_ref, unit_hbm, sems.at[RECEIVED + 1]))
    copies[-1].start()
    copies.append(pltpu.make_async_copy(inv_ref, inv_hbm, sems.at[RECEIVED + 2]))
    copies[-1].start()
    shape = (16, E_WIDE - E)
    lane = lax.broadcasted_iota(jnp.int32, shape, 1)
    block = lax.broadcasted_iota(jnp.int32, shape, 0)
    group, end = lane // RB, lane % RB
    picks.wait()
    other = jnp.zeros(shape, f32)
    for j in range(GROUPS):
        other = other + jnp.where(group == j, theirs_ref[j].astype(f32), 0.0)
    as_row = (local_ref[0:1, :] == block) & (local_ref[1:2, :] == end)
    as_key = (local_ref[2:3, :] == block) & (other.astype(jnp.int32) == end)
    counts = as_row.astype(f32) + as_key.astype(f32)
    counts = jnp.where((group < GROUPS) & (block < RB), counts, 0.0)
    row_ref[:, E:] = jnp.concatenate([counts, jnp.zeros((SHARD - 16, E_WIDE - E), f32)], axis=0).astype(bf16)
    copies.append(pltpu.make_async_copy(row_ref, row_hbm, sems.at[RECEIVED + 3]))
    copies[-1].start()
    for copy in copies:
        copy.wait()


def normalise(own, local, theirs, parts):
    return pl.pallas_call(
        normalise_body,
        out_shape=[
            pltpu.HBM((SHARD, E), f32),
            pltpu.HBM((SHARD, BLK), f32),
            pltpu.HBM((SHARD, E_WIDE), bf16),
            pltpu.HBM((GROUPS, SHARD, E), bf16),
        ],
        in_specs=in_vmem(1) + in_place(RECEIVED + 2),
        out_specs=in_place(4),
        scratch_shapes=[
            pltpu.VMEM((SHARD, E), f32),
            pltpu.VMEM((SHARD, BLK), f32),
            pltpu.VMEM((SHARD, E_WIDE), bf16),
            pltpu.VMEM((RECEIVED, SHARD, E), bf16),
            pltpu.VMEM((GROUPS, 16, E_WIDE - E), bf16),
            pltpu.SemaphoreType.DMA((RECEIVED + 4 + GROUPS,)),
        ],
        compiler_params=scoped(12),
        cost_estimate=pl.CostEstimate(flops=1_000_000, bytes_accessed=4_000_000, transcendentals=0),
        name="normalise",
    )(local, hbm(own), hbm(theirs), *[hbm(part) for part in parts])


def gram_body(at_ref, rows_hbm, keys_hbm, teacher_hbm, spread_ref, *refs):
    targets = refs[:PARTS]
    row_ref, key_ref, teacher_ref, grad_ref, total_ref, sems, stage_ref, stage_sems = refs[PARTS:]
    contract = (((1,), (1,)), ((), ()))
    step = 256
    spans = [pl.ds(k, step) for k in range(0, GROUPS * SHARD, step)]
    row_copy = pltpu.make_async_copy(rows_hbm, row_ref, sems.at[0])
    row_copy.start()
    copies = []
    for i, span in enumerate(spans):
        pair = (
            pltpu.make_async_copy(keys_hbm.at[span, :], key_ref.at[span, :], sems.at[1 + 2 * i]),
            pltpu.make_async_copy(teacher_hbm.at[:, span], teacher_ref.at[:, span], sems.at[2 + 2 * i]),
        )
        pair[0].start()
        pair[1].start()
        copies.append(pair)
    row_copy.wait()
    counts = jnp.zeros((16, E_WIDE - E), f32)
    for d in range(NT):
        counts = counts + row_ref[pl.ds(d * SHARD, 16), E:].astype(f32)
    tile = jnp.dot(counts.astype(bf16), spread_ref[...], preferred_element_type=f32) * (E / 8.0)
    for i, span in enumerate(spans):
        copies[i][0].wait()
        copies[i][1].wait()
        diff = (
            lax.dot_general(row_ref[:, :E], key_ref[span, :], contract, preferred_element_type=f32)
            - teacher_ref[:, span]
        )
        for a in range(RB):
            grad_ref[pl.ds(a * BLK, BLK), span] = (
                diff[a * BLK : (a + 1) * BLK] * tile[a : a + 1, i * step : (i + 1) * step]
            ).astype(bf16)
    for c, wide in ((0, 768), (768, 640)):
        total_ref[:, pl.ds(c, wide)] = jnp.dot(
            grad_ref[...], key_ref[:, pl.ds(c, wide)], preferred_element_type=f32
        )
    for copy in chunk_out(total_ref, at_ref[0], targets, stage_ref, stage_sems):
        copy.wait()


def gram_grads(at, rows, keys, gram_teacher, spread):
    steps = GROUPS * SHARD // 256
    return pl.pallas_call(
        gram_body,
        out_shape=CHUNKS,
        in_specs=[IN_SMEM] + in_place(3) + in_vmem(1),
        out_specs=in_place(PARTS),
        scratch_shapes=[
            pltpu.VMEM((ROWS, E_WIDE), bf16),
            pltpu.VMEM((GROUPS * SHARD, E), bf16),
            pltpu.VMEM((ROWS, GROUPS * SHARD), f32),
            pltpu.VMEM((ROWS, GROUPS * SHARD), bf16),
            pltpu.VMEM((ROWS, E), f32),
            pltpu.SemaphoreType.DMA((1 + 2 * steps,)),
        ]
        + STAGE,
        compiler_params=scoped(20),
        cost_estimate=pl.CostEstimate(flops=1_700_000_000, bytes_accessed=9_000_000, transcendentals=0),
        name="gram_grads",
    )(at, hbm(rows), hbm(keys), hbm(gram_teacher), spread)


def backward_body(at_ref, *refs):
    pieces, refs = dict(zip(PIECE_ORDER, refs[:PARTS])), refs[PARTS:]
    hidden_ref, w_out_ref, pre_ref, act_ref = refs[:4]
    keep_hbm, give_hbm, grad_pre_hbm, keep_ref, give_ref, grad_pre_ref, proj_ref, sems = refs[4:]
    at, tea = at_ref[0], at_ref[1]
    contract = (((1,), (1,)), ((), ()))
    over_rows = (((0,), (0,)), ((), ()))
    copies = []
    for n in range(PARTS):
        d = n if n <= 4 else n - 1
        cols = {4: pl.ds(0, LEFT), 5: pl.ds(LEFT, RIGHT)}.get(n, pl.ds(0, E))
        rows = pl.ds(spot_of(at, d), SHARD)
        copies.append(pltpu.make_async_copy(pieces[n], proj_ref.at[rows, cols], sems.at[n]))
        copies[-1].start()
    proj_ref[:, E:] = jnp.zeros((ROWS, E_PAD - E), bf16)
    pre = pre_ref[...]
    sigma = 1.0 / (1.0 + jnp.exp(-pre))
    slope = sigma * (1.0 + pre * (1.0 - sigma))
    for copy in copies:
        copy.wait()
    grad_act = lax.dot_general(proj_ref[:, :E], w_out_ref[...], contract, preferred_element_type=f32)
    grad_pre = (grad_act * slope).astype(bf16)
    grad_pre_ref[...] = grad_pre
    copies = [pltpu.make_async_copy(grad_pre_ref, grad_pre_hbm, sems.at[0])]
    copies[0].start()
    d_half, e_half = hidden_ref.shape[1] // 2, E_PAD // 2
    in_rows, out_rows = d_half // GROUPS, e_half // GROUPS
    for n, (ref, target, side) in enumerate(((give_ref, give_hbm, 1 - tea), (keep_ref, keep_hbm, tea))):
        part = hidden_ref[:, pl.ds(pl.multiple_of(side * d_half, d_half), d_half)]
        grad = lax.dot_general(part, grad_pre, over_rows, preferred_element_type=f32)
        for c in range(GROUPS):
            ref[c, pl.ds(0, in_rows), :] = grad[c * in_rows : (c + 1) * in_rows].astype(ref.dtype)
        part = proj_ref[:, pl.ds(pl.multiple_of(side * e_half, e_half), e_half)]
        grad = lax.dot_general(part, act_ref[...], over_rows, preferred_element_type=f32)
        for c in range(GROUPS):
            ref[c, pl.ds(in_rows, out_rows), :] = grad[c * out_rows : (c + 1) * out_rows].astype(ref.dtype)
        copies.append(pltpu.make_async_copy(ref, target, sems.at[n + 1]))
        copies[-1].start()
    for copy in copies:
        copy.wait()


def backward(where, pieces, hidden_states, w_out, pre_act, activation):
    rows, d_model = hidden_states.shape
    width = activation.shape[1]
    halves = (GROUPS, (d_model + E_PAD) // 2 // GROUPS, width)
    return pl.pallas_call(
        backward_body,
        out_shape=[pltpu.HBM(halves, f32), pltpu.HBM(halves, bf16), pltpu.HBM((rows, width), bf16)],
        in_specs=[IN_SMEM] + in_place(PARTS) + in_vmem(4),
        out_specs=in_place(3),
        scratch_shapes=[
            pltpu.VMEM(halves, f32),
            pltpu.VMEM(halves, bf16),
            pltpu.VMEM((rows, width), bf16),
            pltpu.VMEM((ROWS, E_PAD), bf16),
            pltpu.SemaphoreType.DMA((PARTS,)),
        ],
        compiler_params=scoped(20),
        cost_estimate=pl.CostEstimate(flops=1_200_000_000, bytes_accessed=9_000_000, transcendentals=100_000),
        name="backward",
    )(where, *[pieces[d] for d in PIECE_ORDER], hidden_states, w_out, pre_act, activation)


def pair_body(keep_hbm, got_hbm, grad_pre_hbm, w_in_ref, sum_ref, terms_hbm, keep_ref, got_ref, grad_pre_ref, terms_ref, sems, out_sems):
    first = pltpu.make_async_copy(grad_pre_hbm, grad_pre_ref, sems.at[2 * NT])
    first.start()
    contract = (((1,), (1,)), ((), ()))
    share = w_in_ref.shape[0] // NT
    parts = GROUPS // NT
    reads, writes = [], []
    for p in range(NT):
        span = pl.ds(p * parts, parts)
        reads.append(
            (
                pltpu.make_async_copy(keep_hbm.at[span], keep_ref.at[span], sems.at[2 * p]),
                pltpu.make_async_copy(got_hbm.at[span], got_ref.at[span], sems.at[2 * p + 1]),
            )
        )
        for copy in reads[-1]:
            copy.start()
    first.wait()
    for p in range(NT):
        span = pl.ds(p * ROWS, ROWS)
        terms_ref[span, :] = lax.dot_general(
            grad_pre_ref[...], w_in_ref[pl.ds(p * share, share), :], contract, preferred_element_type=f32
        ).astype(bf16)
        writes.append(pltpu.make_async_copy(terms_ref.at[span, :], terms_hbm.at[span, :], out_sems.at[p]))
        writes[-1].start()
        span = pl.ds(p * parts, parts)
        for copy in reads[p]:
            copy.wait()
        sum_ref[span] = (keep_ref[span] + got_ref[span].astype(f32)).astype(bf16)
    for copy in writes:
        copy.wait()


def pair_sum(keep, got, grad_pre, w_in):
    terms = (NT * ROWS, w_in.shape[0] // NT)
    return pl.pallas_call(
        pair_body,
        out_shape=[jax.ShapeDtypeStruct(keep.shape, bf16), pltpu.HBM(terms, bf16)],
        in_specs=in_place(3) + in_vmem(1),
        out_specs=in_vmem(1) + in_place(1),
        scratch_shapes=[
            pltpu.VMEM(keep.shape, f32),
            pltpu.VMEM(keep.shape, bf16),
            pltpu.VMEM(grad_pre.shape, bf16),
            pltpu.VMEM(terms, bf16),
            pltpu.SemaphoreType.DMA((2 * NT + 1,)),
            pltpu.SemaphoreType.DMA((NT,)),
        ],
        compiler_params=scoped(14),
        cost_estimate=pl.CostEstimate(flops=600_000_000, bytes_accessed=9_000_000, transcendentals=0),
        name="pair_sum",
    )(hbm(keep), got, hbm(grad_pre), w_in)


def final_body(tea_ref, mine_ref, other_ref, hidden_hbm, w_in_ref, w_out_ref, hidden_ref, flat_ref, got_ref, sem):
    tea = tea_ref[0]
    copy = pltpu.make_async_copy(hidden_hbm, got_ref, sem)
    copy.start()
    d_half, e_half = w_in_ref.shape[0] // 2, E_PAD // 2
    in_rows, out_rows = d_half // GROUPS, e_half // GROUPS
    for ref, side in ((mine_ref, tea), (other_ref, 1 - tea)):
        d_at = pl.multiple_of(side * d_half, d_half)
        e_at = pl.multiple_of(side * e_half, e_half)
        for c in range(GROUPS):
            w_in_ref[pl.ds(d_at + c * in_rows, in_rows), :] = ref[c, pl.ds(0, in_rows), :].astype(f32)
            flat_ref[pl.ds(e_at + c * out_rows, out_rows), :] = ref[c, pl.ds(in_rows, out_rows), :].astype(f32)
    for c in range(0, E, BLK):
        w_out_ref[:, pl.ds(c, BLK)] = flat_ref[pl.ds(c, BLK), :].T
    copy.wait()
    hidden_ref[...] = got_ref[...].astype(f32)


def final_layout(tea, mine, other, hidden, d_model):
    width = mine.shape[-1]
    return pl.pallas_call(
        final_body,
        out_shape=[
            jax.ShapeDtypeStruct((d_model, width), f32),
            jax.ShapeDtypeStruct((width, E), f32),
            jax.ShapeDtypeStruct(hidden.shape, f32),
        ],
        in_specs=[IN_SMEM] + in_vmem(2) + in_place(1),
        out_specs=in_vmem(3),
        scratch_shapes=[
            pltpu.VMEM((E_PAD, width), f32),
            pltpu.VMEM(hidden.shape, bf16),
            pltpu.SemaphoreType.DMA,
        ],
        compiler_params=scoped(12),
        cost_estimate=pl.CostEstimate(flops=0, bytes_accessed=7_000_000, transcendentals=0),
        name="final_layout",
    )(tea, mine, other, hbm(hidden))


def on_device(hidden_states, w_in, w_out, teacher, patch_map, row_pick, key_pick):
    seq_index = lax.axis_index("seq")
    tp_index = lax.axis_index("tp")
    tea_index = lax.axis_index("tea")
    at = jnp.full((1,), tp_index, jnp.int32)
    tea = jnp.full((1,), tea_index, jnp.int32)
    contract = (((1,), (1,)), ((), ()))

    picks = row_pick.reshape(GROUPS)
    group = jnp.full((1,), lax.axis_index(("seq", "tea")), jnp.int32)
    row_teacher, teacher_send = align(jnp.concatenate([at, group]), teacher, patch_map.reshape(1, ROWS), picks)
    teacher_send, at_next = lax.optimization_barrier((teacher_send, at))
    teacher_got = lax.all_to_all(teacher_send, "seq", 0, 0, tiled=True)

    pre_act, activation, *chunks = forward(at_next, hidden_states, w_in, w_out)
    activation, key_pick, picks = lax.optimization_barrier((activation, key_pick, picks))
    received = sum_ring(*chunks)

    table = key_pick.reshape(GROUPS, GROUPS)
    of_rows = lax.dynamic_index_in_dim(table, seq_index, axis=0, keepdims=False)
    of_keys = lax.dynamic_index_in_dim(table, seq_index, axis=1, keepdims=False)
    local = jnp.repeat(jnp.stack([picks, of_rows, of_keys]), RB, axis=1)
    local = jnp.pad(local, ((0, 8 - 3), (0, E_WIDE - E - GROUPS * RB)))
    key_ids = jnp.arange(GROUPS * SHARD, dtype=jnp.int32)
    key_cell = key_ids // SHARD * RB + (tp_index * SHARD + key_ids % SHARD) // BLK
    spread = (jnp.arange(E_WIDE - E, dtype=jnp.int32)[:, None] == key_cell[None, :]).astype(bf16)

    *received, teacher_got = lax.optimization_barrier((*received, teacher_got))
    unit_student, inv_norm, row_send, key_send = normalise(chunks[0], local, teacher_got, received)
    rows = lax.all_gather(row_send, "tp", axis=0, tiled=True)
    keys = lax.all_to_all(key_send, "seq", 0, 0, tiled=True).reshape(GROUPS * SHARD, E)
    teacher_got, inv_norm = lax.optimization_barrier((teacher_got, inv_norm))
    inv_norm = inv_norm[:, :1]
    key_teacher = teacher_got[:, :, :E].reshape(GROUPS * SHARD, E)
    gram_teacher = lax.dot_general(row_teacher, key_teacher, contract, preferred_element_type=f32)

    row_grad = gram_grads(at, rows, keys, gram_teacher, spread)
    unit_grad = row_grad[0]
    for piece in sum_ring(*row_grad):
        unit_grad = unit_grad + piece.astype(f32)
    inner = jnp.sum(unit_student * unit_grad, axis=-1, keepdims=True)
    grad_proj = ((unit_grad - unit_student * inner) * inv_norm).astype(bf16)
    pieces = gather_ring(grad_proj)

    where = jnp.concatenate([at, tea])
    keep, give, grad_pre = backward(where, pieces, hidden_states, w_out, pre_act, activation)
    chip, hidden_terms = pair_sum(keep, swap_tea(give), grad_pre, w_in)
    grad_hidden = lax.psum_scatter(hidden_terms, "tp", scatter_dimension=0, tiled=True)
    chip = lax.all_to_all(chip, "seq", 0, 0, tiled=True)
    mine = to_all(jnp.sum(chip.astype(f32), axis=0).astype(bf16)).reshape(keep.shape)
    other = swap_tea(mine)
    grad_w_in, grad_w_out, grad_hidden = final_layout(tea, mine, other, grad_hidden, hidden_states.shape[1])
    return (grad_hidden, grad_w_in, grad_w_out)


def solution(mesh):
    return jax.shard_map(
        on_device,
        mesh=mesh,
        in_specs=(
            P(("seq", "tea"), None),
            P(None, "tp"),
            P("tp", None),
            P(("seq", "tea"), None),
            P(("seq", "tea")),
            P("seq", "tp", "tea", None),
            P(None, "tp", "tea", None),
        ),
        out_specs=(P(("seq", "tea"), "tp"), P(None, "tp"), P("tp", None)),
        check_vma=False,
    )
```

```python
import jax
import jax.numpy as jnp
from jax import lax
from jax.experimental import pallas as pl
from jax.experimental.pallas import tpu as pltpu
from jax.sharding import PartitionSpec as P

E = 1408
BLK = 128
RB = 3
SIDE = 4
NT = 8
GROUPS = SIDE * SIDE
SHARD = 48
ROWS = 384
E_WIDE = 1536
E_PAD = 1536

eps = 1e-06
bf16 = jnp.bfloat16
f32 = jnp.float32


def shift_tp(x, step):
    return lax.ppermute(x, "tp", [(i, (i + step) % NT) for i in range(NT)])


def swap_tea(x):
    return lax.ppermute(x, "tea", [(0, 1), (1, 0)])


LEFT = 768
RIGHT = 640


def gather_ring(x):
    before, after = shift_tp(x, 1), shift_tp(x, -1)
    before2, after2 = shift_tp(x, 2), shift_tp(x, -2)
    before3, after3 = shift_tp(before2, 1), shift_tp(after2, -1)
    left, right = shift_tp(before2[:, :LEFT], 2), shift_tp(after2[:, LEFT:], -2)
    return [x, after, after2, after3, left, right, before3, before2, before]


def pass_near(own, one, two, three, left, right, five, six, seven, axis=1):
    three, five = shift_tp(three, 1), shift_tp(five, -1)
    left, right = shift_tp(left, 2), shift_tp(right, -2)
    one, seven = shift_tp(one, 1), shift_tp(seven, -1)
    blank = jnp.zeros(left.shape, f32), jnp.zeros(right.shape, f32)
    two = two + three.astype(f32) + jnp.concatenate([left.astype(f32), blank[1]], axis=axis)
    six = six + five.astype(f32) + jnp.concatenate([blank[0], right.astype(f32)], axis=axis)
    return one, seven, two.astype(bf16), six.astype(bf16)


def sum_ring(*terms):
    one, seven, two, six = pass_near(*terms)
    return [one, seven, shift_tp(two, 2), shift_tp(six, -2)]


def to_all(x):
    return lax.all_to_all(jnp.broadcast_to(x[None], (GROUPS,) + x.shape), "seq", 0, 0, tiled=True)


def in_vmem(count):
    return [pl.BlockSpec(memory_space=pltpu.VMEM)] * count


def in_place(count):
    return [pl.BlockSpec(memory_space=pltpu.HBM)] * count


def hbm(x):
    return pltpu.with_memory_space_constraint(x, pltpu.HBM)


IN_SMEM = pl.BlockSpec(memory_space=pltpu.SMEM)
def scoped(mib):
    return pltpu.CompilerParams(vmem_limit_bytes=mib * 1024 * 1024)


PIECE_ORDER = (0, 1, 8, 2, 7, 3, 6, 4, 5)


def spot_of(at, d):
    return pl.multiple_of(lax.rem(at + d, NT) * SHARD, SHARD)


def chunk_out(total_ref, at, targets, stage_ref, sems):
    copies = []
    slot = 0
    for n, d, cols in (
        (3, 3, None),
        (6, 5, None),
        (4, 4, pl.ds(0, LEFT)),
        (5, 4, pl.ds(LEFT, RIGHT)),
        (1, 1, None),
        (8, 7, None),
        (2, 2, None),
        (7, 6, None),
        (0, 0, None),
    ):
        rows = pl.ds(spot_of(at, d), SHARD)
        if d in (0, 2, 6):
            source = total_ref.at[rows, :]
        else:
            if n != 5:
                stage_ref[slot] = total_ref[rows, :].astype(bf16)
                slot += 1
            source = stage_ref.at[slot - 1] if cols is None else stage_ref.at[slot - 1, :, cols]
        copies.append(pltpu.make_async_copy(source, targets[n], sems.at[n]))
        copies[-1].start()
    return copies


PARTS = NT + 1
STAGE = [pltpu.VMEM((5, SHARD, E), bf16), pltpu.SemaphoreType.DMA((PARTS,))]
WIDE, FULL = pltpu.HBM((SHARD, E), f32), pltpu.HBM((SHARD, E), bf16)
CHUNKS = [WIDE, FULL, WIDE, FULL, pltpu.HBM((SHARD, LEFT), bf16), pltpu.HBM((SHARD, RIGHT), bf16), FULL, WIDE, FULL]


def align_body(at_ref, teacher_hbm, patch_ref, picks_ref, rows_hbm, send_hbm, teacher_ref, rows_ref, own_ref, extra_ref, sems):
    copy = pltpu.make_async_copy(teacher_hbm, teacher_ref, sems.at[GROUPS])
    copy.start()
    for j in range(GROUPS):
        extra_ref[j] = jnp.full(extra_ref.shape[1:], picks_ref[j], jnp.int32).astype(f32).astype(bf16)
    extra = pltpu.make_async_copy(extra_ref, send_hbm.at[:, :, pl.ds(E, E_WIDE - E)], sems.at[GROUPS + 1])
    extra.start()
    copy.wait()
    teacher = teacher_ref[...].astype(f32)
    unit = (teacher * lax.rsqrt(jnp.sum(teacher * teacher, axis=-1, keepdims=True) + eps)).astype(bf16)
    ids = lax.broadcasted_iota(jnp.int32, (teacher.shape[0], ROWS), 0)
    hot = (ids == patch_ref[...] - at_ref[1] * teacher.shape[0]).astype(f32).astype(bf16)
    rows_ref[...] = lax.dot_general(
        hot, unit, (((0,), (0,)), ((), ())), preferred_element_type=f32
    ).astype(bf16)
    copies = [pltpu.make_async_copy(rows_ref, rows_hbm, sems.at[GROUPS])]
    copies[0].start()
    own_ref[...] = rows_ref[pl.ds(spot_of(at_ref[0], 0), SHARD), :]
    for j in range(GROUPS):
        copies.append(pltpu.make_async_copy(own_ref, send_hbm.at[j, :, pl.ds(0, E)], sems.at[j]))
        copies[-1].start()
    copies.append(extra)
    for copy in copies:
        copy.wait()


def align(at, teacher, patch, picks):
    return pl.pallas_call(
        align_body,
        out_shape=[
            pltpu.HBM((ROWS, E), bf16),
            pltpu.HBM((GROUPS, SHARD, E_WIDE), bf16),
        ],
        in_specs=[IN_SMEM] + in_place(1) + in_vmem(1) + [IN_SMEM],
        out_specs=in_place(2),
        scratch_shapes=[
            pltpu.VMEM(teacher.shape, bf16),
            pltpu.VMEM((ROWS, E), bf16),
            pltpu.VMEM((SHARD, E), bf16),
            pltpu.VMEM((GROUPS, SHARD, E_WIDE - E), bf16),
            pltpu.SemaphoreType.DMA((GROUPS + 2,)),
        ],
        compiler_params=scoped(12),
        cost_estimate=pl.CostEstimate(flops=250_000_000, bytes_accessed=4_000_000, transcendentals=0),
        name="align",
    )(at, hbm(teacher), patch, picks)


def forward_body(at_ref, hidden_ref, w_in_ref, w_out_ref, pre_hbm, act_hbm, *refs):
    targets = refs[:PARTS]
    total_ref, pre_ref, act_ref, sems, stage_ref, stage_sems = refs[PARTS:]
    pre = jnp.dot(hidden_ref[...], w_in_ref[...], preferred_element_type=f32)
    pre_ref[...] = pre
    act = (pre / (1.0 + jnp.exp(-pre))).astype(bf16)
    act_ref[...] = act
    copies = [
        pltpu.make_async_copy(pre_ref, pre_hbm, sems.at[0]),
        pltpu.make_async_copy(act_ref, act_hbm, sems.at[1]),
    ]
    for copy in copies:
        copy.start()
    total_ref[...] = jnp.dot(act, w_out_ref[...], preferred_element_type=f32)
    copies += chunk_out(total_ref, at_ref[0], targets, stage_ref, stage_sems)
    for copy in copies:
        copy.wait()


def forward(at, hidden_states, w_in, w_out):
    rows, width = hidden_states.shape[0], w_in.shape[1]
    return pl.pallas_call(
        forward_body,
        out_shape=[pltpu.HBM((rows, width), f32), pltpu.HBM((rows, width), bf16)] + CHUNKS,
        in_specs=[IN_SMEM] + in_vmem(3),
        out_specs=in_place(2 + PARTS),
        scratch_shapes=[
            pltpu.VMEM((rows, E), f32),
            pltpu.VMEM((rows, width), f32),
            pltpu.VMEM((rows, width), bf16),
            pltpu.SemaphoreType.DMA((2,)),
        ]
        + STAGE,
        compiler_params=scoped(16),
        cost_estimate=pl.CostEstimate(flops=900_000_000, bytes_accessed=8_000_000, transcendentals=100_000),
        name="forward",
    )(at, hidden_states, w_in, w_out)


RECEIVED = 4


def normalise_body(local_ref, own_hbm, theirs_hbm, *refs):
    parts, refs = refs[: RECEIVED], refs[RECEIVED :]
    unit_hbm, inv_hbm, row_hbm, send_hbm, unit_ref, inv_ref, row_ref, got_ref, theirs_ref, sems = refs
    first = pltpu.make_async_copy(own_hbm, unit_ref, sems.at[RECEIVED + 1])
    first.start()
    copies = [pltpu.make_async_copy(parts[i], got_ref.at[i], sems.at[i]) for i in range(RECEIVED)]
    picks = pltpu.make_async_copy(
        theirs_hbm.at[:, pl.ds(0, 16), pl.ds(E, E_WIDE - E)], theirs_ref, sems.at[RECEIVED]
    )
    for copy in copies:
        copy.start()
    picks.start()
    first.wait()
    total = unit_ref[...]
    for i in range(RECEIVED):
        copies[i].wait()
        total = total + got_ref[i].astype(f32)
    inv = lax.rsqrt(jnp.sum(total * total, axis=-1, keepdims=True) + eps)
    unit = total * inv
    row_ref[:, :E] = unit.astype(bf16)
    copies = [
        pltpu.make_async_copy(row_ref.at[:, pl.ds(0, E)], send_hbm.at[j], sems.at[RECEIVED + 4 + j]) for j in range(GROUPS)
    ]
    for copy in copies:
        copy.start()
    unit_ref[...] = unit
    inv_ref[...] = jnp.broadcast_to(inv, inv_ref.shape)
    copies.append(pltpu.make_async_copy(unit_ref, unit_hbm, sems.at[RECEIVED + 1]))
    copies[-1].start()
    copies.append(pltpu.make_async_copy(inv_ref, inv_hbm, sems.at[RECEIVED + 2]))
    copies[-1].start()
    shape = (16, E_WIDE - E)
    lane = lax.broadcasted_iota(jnp.int32, shape, 1)
    block = lax.broadcasted_iota(jnp.int32, shape, 0)
    group, end = lane // RB, lane % RB
    picks.wait()
    other = jnp.zeros(shape, f32)
    for j in range(GROUPS):
        other = other + jnp.where(group == j, theirs_ref[j].astype(f32), 0.0)
    as_row = (local_ref[0:1, :] == block) & (local_ref[1:2, :] == end)
    as_key = (local_ref[2:3, :] == block) & (other.astype(jnp.int32) == end)
    counts = as_row.astype(f32) + as_key.astype(f32)
    counts = jnp.where((group < GROUPS) & (block < RB), counts, 0.0)
    row_ref[:, E:] = jnp.concatenate([counts, jnp.zeros((SHARD - 16, E_WIDE - E), f32)], axis=0).astype(bf16)
    copies.append(pltpu.make_async_copy(row_ref, row_hbm, sems.at[RECEIVED + 3]))
    copies[-1].start()
    for copy in copies:
        copy.wait()


def normalise(own, local, theirs, parts):
    return pl.pallas_call(
        normalise_body,
        out_shape=[
            pltpu.HBM((SHARD, E), f32),
            pltpu.HBM((SHARD, BLK), f32),
            pltpu.HBM((SHARD, E_WIDE), bf16),
            pltpu.HBM((GROUPS, SHARD, E), bf16),
        ],
        in_specs=in_vmem(1) + in_place(RECEIVED + 2),
        out_specs=in_place(4),
        scratch_shapes=[
            pltpu.VMEM((SHARD, E), f32),
            pltpu.VMEM((SHARD, BLK), f32),
            pltpu.VMEM((SHARD, E_WIDE), bf16),
            pltpu.VMEM((RECEIVED, SHARD, E), bf16),
            pltpu.VMEM((GROUPS, 16, E_WIDE - E), bf16),
            pltpu.SemaphoreType.DMA((RECEIVED + 4 + GROUPS,)),
        ],
        compiler_params=scoped(12),
        cost_estimate=pl.CostEstimate(flops=1_000_000, bytes_accessed=4_000_000, transcendentals=0),
        name="normalise",
    )(local, hbm(own), hbm(theirs), *[hbm(part) for part in parts])


def gather_in(at, pieces, target_ref, wide, sems):
    copies = []
    for n in range(PARTS):
        d = n if n <= 4 else n - 1
        cols = {4: pl.ds(0, LEFT), 5: pl.ds(LEFT, wide - LEFT)}.get(n, pl.ds(0, wide))
        rows = pl.ds(spot_of(at, d), SHARD)
        copies.append(pltpu.make_async_copy(pieces[n], target_ref.at[rows, cols], sems.at[n]))
        copies[-1].start()
    return copies


def gram_body(at_ref, *refs):
    pieces, refs = dict(zip(PIECE_ORDER, refs[:PARTS])), refs[PARTS:]
    keys_hbm, teacher_hbm, spread_ref = refs[:3]
    refs = refs[3:]
    targets = refs[:PARTS]
    row_ref, key_ref, teacher_ref, grad_ref, total_ref, sems, stage_ref, stage_sems = refs[PARTS:]
    contract = (((1,), (1,)), ((), ()))
    step = 256
    spans = [pl.ds(k, step) for k in range(0, GROUPS * SHARD, step)]
    row_copies = gather_in(at_ref[0], pieces, row_ref, E_WIDE, sems)
    copies = []
    for i, span in enumerate(spans):
        pair = (
            pltpu.make_async_copy(keys_hbm.at[span, :], key_ref.at[span, :], sems.at[PARTS + 2 * i]),
            pltpu.make_async_copy(teacher_hbm.at[:, span], teacher_ref.at[:, span], sems.at[PARTS + 1 + 2 * i]),
        )
        pair[0].start()
        pair[1].start()
        copies.append(pair)
    for copy in row_copies:
        copy.wait()
    counts = jnp.zeros((16, E_WIDE - E), f32)
    for d in range(NT):
        counts = counts + row_ref[pl.ds(d * SHARD, 16), E:].astype(f32)
    tile = jnp.dot(counts.astype(bf16), spread_ref[...], preferred_element_type=f32) * (E / 8.0)
    for i, span in enumerate(spans):
        copies[i][0].wait()
        copies[i][1].wait()
        diff = (
            lax.dot_general(row_ref[:, :E], key_ref[span, :], contract, preferred_element_type=f32)
            - teacher_ref[:, span]
        )
        for a in range(RB):
            grad_ref[pl.ds(a * BLK, BLK), span] = (
                diff[a * BLK : (a + 1) * BLK] * tile[a : a + 1, i * step : (i + 1) * step]
            ).astype(bf16)
    for c, wide in ((0, 768), (768, 640)):
        total_ref[:, pl.ds(c, wide)] = jnp.dot(
            grad_ref[...], key_ref[:, pl.ds(c, wide)], preferred_element_type=f32
        )
    for copy in chunk_out(total_ref, at_ref[0], targets, stage_ref, stage_sems):
        copy.wait()


def gram_grads(at, pieces, keys, gram_teacher, spread):
    steps = GROUPS * SHARD // 256
    return pl.pallas_call(
        gram_body,
        out_shape=CHUNKS,
        in_specs=[IN_SMEM] + in_place(PARTS + 2) + in_vmem(1),
        out_specs=in_place(PARTS),
        scratch_shapes=[
            pltpu.VMEM((ROWS, E_WIDE), bf16),
            pltpu.VMEM((GROUPS * SHARD, E), bf16),
            pltpu.VMEM((ROWS, GROUPS * SHARD), f32),
            pltpu.VMEM((ROWS, GROUPS * SHARD), bf16),
            pltpu.VMEM((ROWS, E), f32),
            pltpu.SemaphoreType.DMA((PARTS + 2 * steps,)),
        ]
        + STAGE,
        compiler_params=scoped(20),
        cost_estimate=pl.CostEstimate(flops=1_700_000_000, bytes_accessed=9_000_000, transcendentals=0),
        name="gram_grads",
    )(at, *[hbm(pieces[n]) for n in PIECE_ORDER], hbm(keys), hbm(gram_teacher), spread)


def backward_body(at_ref, *refs):
    pieces, refs = dict(zip(PIECE_ORDER, refs[:PARTS])), refs[PARTS:]
    hidden_ref, w_out_ref, pre_ref, act_ref = refs[:4]
    keep_hbm, give_hbm, grad_pre_hbm, keep_ref, give_ref, grad_pre_ref, proj_ref, sems = refs[4:]
    at, tea = at_ref[0], at_ref[1]
    contract = (((1,), (1,)), ((), ()))
    over_rows = (((0,), (0,)), ((), ()))
    copies = gather_in(at, pieces, proj_ref, E, sems)
    proj_ref[:, E:] = jnp.zeros((ROWS, E_PAD - E), bf16)
    pre = pre_ref[...]
    sigma = 1.0 / (1.0 + jnp.exp(-pre))
    slope = sigma * (1.0 + pre * (1.0 - sigma))
    for copy in copies:
        copy.wait()
    grad_act = lax.dot_general(proj_ref[:, :E], w_out_ref[...], contract, preferred_element_type=f32)
    grad_pre = (grad_act * slope).astype(bf16)
    grad_pre_ref[...] = grad_pre
    copies = [pltpu.make_async_copy(grad_pre_ref, grad_pre_hbm, sems.at[0])]
    copies[0].start()
    d_half, e_half = hidden_ref.shape[1] // 2, E_PAD // 2
    in_rows, out_rows = d_half // GROUPS, e_half // GROUPS
    for n, (ref, target, side) in enumerate(((give_ref, give_hbm, 1 - tea), (keep_ref, keep_hbm, tea))):
        part = hidden_ref[:, pl.ds(pl.multiple_of(side * d_half, d_half), d_half)]
        grad = lax.dot_general(part, grad_pre, over_rows, preferred_element_type=f32)
        for c in range(GROUPS):
            ref[c, pl.ds(0, in_rows), :] = grad[c * in_rows : (c + 1) * in_rows].astype(ref.dtype)
        part = proj_ref[:, pl.ds(pl.multiple_of(side * e_half, e_half), e_half)]
        grad = lax.dot_general(part, act_ref[...], over_rows, preferred_element_type=f32)
        for c in range(GROUPS):
            ref[c, pl.ds(in_rows, out_rows), :] = grad[c * out_rows : (c + 1) * out_rows].astype(ref.dtype)
        copies.append(pltpu.make_async_copy(ref, target, sems.at[n + 1]))
        copies[-1].start()
    for copy in copies:
        copy.wait()


def backward(where, pieces, hidden_states, w_out, pre_act, activation):
    rows, d_model = hidden_states.shape
    width = activation.shape[1]
    halves = (GROUPS, (d_model + E_PAD) // 2 // GROUPS, width)
    return pl.pallas_call(
        backward_body,
        out_shape=[pltpu.HBM(halves, f32), pltpu.HBM(halves, bf16), pltpu.HBM((rows, width), bf16)],
        in_specs=[IN_SMEM] + in_place(PARTS) + in_vmem(4),
        out_specs=in_place(3),
        scratch_shapes=[
            pltpu.VMEM(halves, f32),
            pltpu.VMEM(halves, bf16),
            pltpu.VMEM((rows, width), bf16),
            pltpu.VMEM((ROWS, E_PAD), bf16),
            pltpu.SemaphoreType.DMA((PARTS,)),
        ],
        compiler_params=scoped(20),
        cost_estimate=pl.CostEstimate(flops=1_200_000_000, bytes_accessed=9_000_000, transcendentals=100_000),
        name="backward",
    )(where, *[pieces[d] for d in PIECE_ORDER], hidden_states, w_out, pre_act, activation)


def hidden_body(at_ref, grad_pre_hbm, w_in_ref, *refs):
    targets, refs = refs[:PARTS], refs[PARTS:]
    grad_pre_ref, wide_ref, full_ref, sems, first_sem = refs
    first = pltpu.make_async_copy(grad_pre_hbm, grad_pre_ref, first_sem)
    first.start()
    contract = (((1,), (1,)), ((), ()))
    share = w_in_ref.shape[0] // NT
    half = ROWS // 2
    copies = []
    first.wait()
    for d in (3, 5, 4, 1, 7, 2, 6, 0):
        rows = pl.ds(pl.multiple_of(lax.rem(at_ref[0] + d, NT) * share, share), share)
        terms = lax.dot_general(grad_pre_ref[...], w_in_ref[rows, :], contract, preferred_element_type=f32)
        if d in (0, 2, 6):
            source = wide_ref.at[d // 2 if d < 6 else 2]
        else:
            source = full_ref.at[(1, 3, 4, 5, 7).index(d)]
            terms = terms.astype(bf16)
        source[...] = terms
        if d == 4:
            pairs = [(source.at[pl.ds(0, half), :], 4), (source.at[pl.ds(half, half), :], 5)]
        else:
            pairs = [(source, d if d < 4 else d + 1)]
        for part, n in pairs:
            copies.append(pltpu.make_async_copy(part, targets[n], sems.at[n]))
            copies[-1].start()
    for copy in copies:
        copy.wait()


def hidden_grads(at, grad_pre, w_in):
    share = w_in.shape[0] // NT
    wide, full, half = (pltpu.HBM((rows, share), kind) for rows, kind in ((ROWS, f32), (ROWS, bf16), (ROWS // 2, bf16)))
    return pl.pallas_call(
        hidden_body,
        out_shape=[wide, full, wide, full, half, half, full, wide, full],
        in_specs=[IN_SMEM] + in_place(1) + in_vmem(1),
        out_specs=in_place(PARTS),
        scratch_shapes=[
            pltpu.VMEM(grad_pre.shape, bf16),
            pltpu.VMEM((3, ROWS, share), f32),
            pltpu.VMEM((5, ROWS, share), bf16),
            pltpu.SemaphoreType.DMA((PARTS,)),
            pltpu.SemaphoreType.DMA,
        ],
        compiler_params=scoped(14),
        cost_estimate=pl.CostEstimate(flops=600_000_000, bytes_accessed=5_000_000, transcendentals=0),
        name="hidden_grads",
    )(at, hbm(grad_pre), w_in)


def pair_body(keep_hbm, got_hbm, sum_ref, keep_ref, got_ref, sems):
    parts = keep_ref.shape[0] // 4
    reads = []
    for p in range(4):
        span = pl.ds(p * parts, parts)
        reads.append(
            (
                pltpu.make_async_copy(keep_hbm.at[span], keep_ref.at[span], sems.at[2 * p]),
                pltpu.make_async_copy(got_hbm.at[span], got_ref.at[span], sems.at[2 * p + 1]),
            )
        )
        for copy in reads[-1]:
            copy.start()
    for p in range(4):
        span = pl.ds(p * parts, parts)
        for copy in reads[p]:
            copy.wait()
        sum_ref[span] = (keep_ref[span] + got_ref[span].astype(f32)).astype(bf16)


def pair_sum(keep, got):
    return pl.pallas_call(
        pair_body,
        out_shape=jax.ShapeDtypeStruct(keep.shape, bf16),
        in_specs=in_place(2),
        out_specs=in_vmem(1)[0],
        scratch_shapes=[
            pltpu.VMEM(keep.shape, f32),
            pltpu.VMEM(keep.shape, bf16),
            pltpu.SemaphoreType.DMA((8,)),
        ],
        compiler_params=scoped(12),
        cost_estimate=pl.CostEstimate(flops=600_000, bytes_accessed=5_000_000, transcendentals=0),
        name="pair_sum",
    )(hbm(keep), got)


def final_body(tea_ref, mine_ref, other_ref, own_hbm, *refs):
    parts, refs = refs[:RECEIVED], refs[RECEIVED:]
    w_in_ref, w_out_ref, hidden_ref, flat_ref, own_ref, got_ref, sems = refs
    tea = tea_ref[0]
    copies = [pltpu.make_async_copy(own_hbm, own_ref, sems.at[RECEIVED])]
    for i in range(RECEIVED):
        copies.append(pltpu.make_async_copy(parts[i], got_ref.at[i], sems.at[i]))
    for copy in copies:
        copy.start()
    d_half, e_half = w_in_ref.shape[0] // 2, E_PAD // 2
    in_rows, out_rows = d_half // GROUPS, e_half // GROUPS
    for ref, side in ((mine_ref, tea), (other_ref, 1 - tea)):
        d_at = pl.multiple_of(side * d_half, d_half)
        e_at = pl.multiple_of(side * e_half, e_half)
        for c in range(GROUPS):
            w_in_ref[pl.ds(d_at + c * in_rows, in_rows), :] = ref[c, pl.ds(0, in_rows), :].astype(f32)
            flat_ref[pl.ds(e_at + c * out_rows, out_rows), :] = ref[c, pl.ds(in_rows, out_rows), :].astype(f32)
    for c in range(0, E, BLK):
        w_out_ref[:, pl.ds(c, BLK)] = flat_ref[pl.ds(c, BLK), :].T
    for copy in copies:
        copy.wait()
    total = own_ref[...]
    for i in range(RECEIVED):
        total = total + got_ref[i].astype(f32)
    hidden_ref[...] = total


def final_layout(tea, mine, other, own, parts, d_model):
    width = mine.shape[-1]
    return pl.pallas_call(
        final_body,
        out_shape=[
            jax.ShapeDtypeStruct((d_model, width), f32),
            jax.ShapeDtypeStruct((width, E), f32),
            jax.ShapeDtypeStruct(own.shape, f32),
        ],
        in_specs=[IN_SMEM] + in_vmem(2) + in_place(1 + RECEIVED),
        out_specs=in_vmem(3),
        scratch_shapes=[
            pltpu.VMEM((E_PAD, width), f32),
            pltpu.VMEM(own.shape, f32),
            pltpu.VMEM((RECEIVED,) + own.shape, bf16),
            pltpu.SemaphoreType.DMA((RECEIVED + 1,)),
        ],
        compiler_params=scoped(12),
        cost_estimate=pl.CostEstimate(flops=0, bytes_accessed=7_000_000, transcendentals=0),
        name="final_layout",
    )(tea, mine, other, hbm(own), *parts)


def on_device(hidden_states, w_in, w_out, teacher, patch_map, row_pick, key_pick):
    seq_index = lax.axis_index("seq")
    tp_index = lax.axis_index("tp")
    tea_index = lax.axis_index("tea")
    at = jnp.full((1,), tp_index, jnp.int32)
    tea = jnp.full((1,), tea_index, jnp.int32)
    contract = (((1,), (1,)), ((), ()))

    picks = row_pick.reshape(GROUPS)
    group = jnp.full((1,), lax.axis_index(("seq", "tea")), jnp.int32)
    row_teacher, teacher_send = align(jnp.concatenate([at, group]), teacher, patch_map.reshape(1, ROWS), picks)
    teacher_send, at_next = lax.optimization_barrier((teacher_send, at))
    teacher_got = lax.all_to_all(teacher_send, "seq", 0, 0, tiled=True)

    pre_act, activation, *chunks = forward(at_next, hidden_states, w_in, w_out)
    activation, key_pick, picks = lax.optimization_barrier((activation, key_pick, picks))
    received = sum_ring(*chunks)

    table = key_pick.reshape(GROUPS, GROUPS)
    of_rows = lax.dynamic_index_in_dim(table, seq_index, axis=0, keepdims=False)
    of_keys = lax.dynamic_index_in_dim(table, seq_index, axis=1, keepdims=False)
    local = jnp.repeat(jnp.stack([picks, of_rows, of_keys]), RB, axis=1)
    local = jnp.pad(local, ((0, 8 - 3), (0, E_WIDE - E - GROUPS * RB)))
    key_ids = jnp.arange(GROUPS * SHARD, dtype=jnp.int32)
    key_cell = key_ids // SHARD * RB + (tp_index * SHARD + key_ids % SHARD) // BLK
    spread = (jnp.arange(E_WIDE - E, dtype=jnp.int32)[:, None] == key_cell[None, :]).astype(bf16)

    *received, teacher_got = lax.optimization_barrier((*received, teacher_got))
    unit_student, inv_norm, row_send, key_send = normalise(chunks[0], local, teacher_got, received)
    rows = gather_ring(row_send)
    keys = lax.all_to_all(key_send, "seq", 0, 0, tiled=True).reshape(GROUPS * SHARD, E)
    teacher_got, inv_norm = lax.optimization_barrier((teacher_got, inv_norm))
    inv_norm = inv_norm[:, :1]
    key_teacher = teacher_got[:, :, :E].reshape(GROUPS * SHARD, E)
    gram_teacher = lax.dot_general(row_teacher, key_teacher, contract, preferred_element_type=f32)

    row_grad = gram_grads(at, rows, keys, gram_teacher, spread)
    unit_grad = row_grad[0]
    for piece in sum_ring(*row_grad):
        unit_grad = unit_grad + piece.astype(f32)
    inner = jnp.sum(unit_student * unit_grad, axis=-1, keepdims=True)
    grad_proj = ((unit_grad - unit_student * inner) * inv_norm).astype(bf16)
    pieces = gather_ring(grad_proj)

    where = jnp.concatenate([at, tea])
    keep, give, grad_pre = backward(where, pieces, hidden_states, w_out, pre_act, activation)
    got = swap_tea(give)
    hidden_terms = hidden_grads(at, grad_pre, w_in)
    chip, *hidden_terms = lax.optimization_barrier((pair_sum(keep, got), *hidden_terms))
    one, seven, two, six = pass_near(*hidden_terms, axis=0)
    chip = lax.all_to_all(chip, "seq", 0, 0, tiled=True)
    mine = jnp.sum(chip.astype(f32), axis=0).astype(bf16)
    mine, two, six = lax.optimization_barrier((mine, two, six))
    hidden_got = [one, seven, shift_tp(two, 2), shift_tp(six, -2)]
    mine = to_all(mine).reshape(keep.shape)
    mine, *hidden_got = lax.optimization_barrier((mine, *hidden_got))
    other = swap_tea(mine)
    grad_w_in, grad_w_out, grad_hidden = final_layout(
        tea, mine, other, hidden_terms[0], hidden_got, hidden_states.shape[1]
    )
    return (grad_hidden, grad_w_in, grad_w_out)


def solution(mesh):
    return jax.shard_map(
        on_device,
        mesh=mesh,
        in_specs=(
            P(("seq", "tea"), None),
            P(None, "tp"),
            P("tp", None),
            P(("seq", "tea"), None),
            P(("seq", "tea")),
            P("seq", "tp", "tea", None),
            P(None, "tp", "tea", None),
        ),
        out_specs=(P(("seq", "tea"), "tp"), P(None, "tp"), P("tp", None)),
        check_vma=False,
    )
```

```python
import jax
import jax.numpy as jnp
from jax import lax
from jax.experimental import pallas as pl
from jax.experimental.pallas import tpu as pltpu
from jax.sharding import PartitionSpec as P

E = 1408
BLK = 128
RB = 3
SIDE = 4
NT = 8
GROUPS = SIDE * SIDE
SHARD = 48
ROWS = 384
E_WIDE = 1536
E_PAD = 1536

eps = 1e-06
bf16 = jnp.bfloat16
f32 = jnp.float32


def shift_tp(x, step):
    return lax.ppermute(x, "tp", [(i, (i + step) % NT) for i in range(NT)])


def swap_tea(x):
    return lax.ppermute(x, "tea", [(0, 1), (1, 0)])


LEFT = 768
RIGHT = 640


def gather_ring(x):
    before, after = shift_tp(x, 1), shift_tp(x, -1)
    before2, after2 = shift_tp(x, 2), shift_tp(x, -2)
    before3, after3 = shift_tp(before2, 1), shift_tp(after2, -1)
    left, right = shift_tp(before2[:, :LEFT], 2), shift_tp(after2[:, LEFT:], -2)
    return [x, after, after2, after3, left, right, before3, before2, before]


def pass_near(own, one, two, three, left, right, five, six, seven, axis=1):
    three, five = shift_tp(three, 1), shift_tp(five, -1)
    left, right = shift_tp(left, 2), shift_tp(right, -2)
    one, seven = shift_tp(one, 1), shift_tp(seven, -1)
    blank = jnp.zeros(left.shape, f32), jnp.zeros(right.shape, f32)
    two = two + three.astype(f32) + jnp.concatenate([left.astype(f32), blank[1]], axis=axis)
    six = six + five.astype(f32) + jnp.concatenate([blank[0], right.astype(f32)], axis=axis)
    return one, seven, two.astype(bf16), six.astype(bf16)


def sum_ring(*terms):
    one, seven, two, six = pass_near(*terms)
    return [one, seven, shift_tp(two, 2), shift_tp(six, -2)]


def to_all(x):
    return lax.all_to_all(jnp.broadcast_to(x[None], (GROUPS,) + x.shape), "seq", 0, 0, tiled=True)


def in_vmem(count):
    return [pl.BlockSpec(memory_space=pltpu.VMEM)] * count


def in_place(count):
    return [pl.BlockSpec(memory_space=pltpu.HBM)] * count


def hbm(x):
    return pltpu.with_memory_space_constraint(x, pltpu.HBM)


IN_SMEM = pl.BlockSpec(memory_space=pltpu.SMEM)
def scoped(mib):
    return pltpu.CompilerParams(vmem_limit_bytes=mib * 1024 * 1024)


PIECE_ORDER = (0, 1, 8, 2, 7, 3, 6, 4, 5)


def spot_of(at, d):
    return pl.multiple_of(lax.rem(at + d, NT) * SHARD, SHARD)


def chunk_out(total_ref, at, targets, stage_ref, sems):
    copies = []
    slot = 0
    for n, d, cols in (
        (3, 3, None),
        (6, 5, None),
        (4, 4, pl.ds(0, LEFT)),
        (5, 4, pl.ds(LEFT, RIGHT)),
        (1, 1, None),
        (8, 7, None),
        (2, 2, None),
        (7, 6, None),
        (0, 0, None),
    ):
        rows = pl.ds(spot_of(at, d), SHARD)
        if d in (0, 2, 6):
            source = total_ref.at[rows, :]
        else:
            if n != 5:
                stage_ref[slot] = total_ref[rows, :].astype(bf16)
                slot += 1
            source = stage_ref.at[slot - 1] if cols is None else stage_ref.at[slot - 1, :, cols]
        copies.append(pltpu.make_async_copy(source, targets[n], sems.at[n]))
        copies[-1].start()
    return copies


def chunk_store(total_ref, at, targets):
    for n, target in enumerate(targets):
        d = n if n <= 4 else n - 1
        cols = {4: pl.ds(0, LEFT), 5: pl.ds(LEFT, RIGHT)}.get(n, pl.ds(0, E))
        target[...] = total_ref[pl.ds(spot_of(at, d), SHARD), cols].astype(target.dtype)


PARTS = NT + 1
STAGE = [pltpu.VMEM((5, SHARD, E), bf16), pltpu.SemaphoreType.DMA((PARTS,))]
WIDE, FULL = pltpu.HBM((SHARD, E), f32), pltpu.HBM((SHARD, E), bf16)
CHUNKS = [WIDE, FULL, WIDE, FULL, pltpu.HBM((SHARD, LEFT), bf16), pltpu.HBM((SHARD, RIGHT), bf16), FULL, WIDE, FULL]


def align_body(at_ref, teacher_hbm, patch_ref, picks_ref, rows_hbm, send_hbm, teacher_ref, rows_ref, own_ref, extra_ref, sems):
    copy = pltpu.make_async_copy(teacher_hbm, teacher_ref, sems.at[GROUPS])
    copy.start()
    for j in range(GROUPS):
        extra_ref[j] = jnp.full(extra_ref.shape[1:], picks_ref[j], jnp.int32).astype(f32).astype(bf16)
    extra = pltpu.make_async_copy(extra_ref, send_hbm.at[:, :, pl.ds(E, E_WIDE - E)], sems.at[GROUPS + 1])
    extra.start()
    copy.wait()
    teacher = teacher_ref[...].astype(f32)
    unit = (teacher * lax.rsqrt(jnp.sum(teacher * teacher, axis=-1, keepdims=True) + eps)).astype(bf16)
    ids = lax.broadcasted_iota(jnp.int32, (teacher.shape[0], ROWS), 0)
    hot = (ids == patch_ref[...] - at_ref[1] * teacher.shape[0]).astype(f32).astype(bf16)
    rows_ref[...] = lax.dot_general(
        hot, unit, (((0,), (0,)), ((), ())), preferred_element_type=f32
    ).astype(bf16)
    copies = [pltpu.make_async_copy(rows_ref, rows_hbm, sems.at[GROUPS])]
    copies[0].start()
    own_ref[...] = rows_ref[pl.ds(spot_of(at_ref[0], 0), SHARD), :]
    for j in range(GROUPS):
        copies.append(pltpu.make_async_copy(own_ref, send_hbm.at[j, :, pl.ds(0, E)], sems.at[j]))
        copies[-1].start()
    copies.append(extra)
    for copy in copies:
        copy.wait()


def align(at, teacher, patch, picks):
    return pl.pallas_call(
        align_body,
        out_shape=[
            pltpu.HBM((ROWS, E), bf16),
            pltpu.HBM((GROUPS, SHARD, E_WIDE), bf16),
        ],
        in_specs=[IN_SMEM] + in_place(1) + in_vmem(1) + [IN_SMEM],
        out_specs=in_place(2),
        scratch_shapes=[
            pltpu.VMEM(teacher.shape, bf16),
            pltpu.VMEM((ROWS, E), bf16),
            pltpu.VMEM((SHARD, E), bf16),
            pltpu.VMEM((GROUPS, SHARD, E_WIDE - E), bf16),
            pltpu.SemaphoreType.DMA((GROUPS + 2,)),
        ],
        compiler_params=scoped(12),
        cost_estimate=pl.CostEstimate(flops=250_000_000, bytes_accessed=4_000_000, transcendentals=0),
        name="align",
    )(at, hbm(teacher), patch, picks)


def forward_body(at_ref, hidden_ref, w_in_ref, w_out_ref, pre_hbm, act_hbm, *refs):
    targets = refs[:PARTS]
    total_ref, pre_ref, act_ref, sems, stage_ref, stage_sems = refs[PARTS:]
    pre = jnp.dot(hidden_ref[...], w_in_ref[...], preferred_element_type=f32)
    pre_ref[...] = pre
    act = (pre / (1.0 + jnp.exp(-pre))).astype(bf16)
    act_ref[...] = act
    copies = [
        pltpu.make_async_copy(pre_ref, pre_hbm, sems.at[0]),
        pltpu.make_async_copy(act_ref, act_hbm, sems.at[1]),
    ]
    for copy in copies:
        copy.start()
    total_ref[...] = jnp.dot(act, w_out_ref[...], preferred_element_type=f32)
    copies += chunk_out(total_ref, at_ref[0], targets, stage_ref, stage_sems)
    for copy in copies:
        copy.wait()


def forward(at, hidden_states, w_in, w_out):
    rows, width = hidden_states.shape[0], w_in.shape[1]
    return pl.pallas_call(
        forward_body,
        out_shape=[pltpu.HBM((rows, width), f32), pltpu.HBM((rows, width), bf16)] + CHUNKS,
        in_specs=[IN_SMEM] + in_vmem(3),
        out_specs=in_place(2 + PARTS),
        scratch_shapes=[
            pltpu.VMEM((rows, E), f32),
            pltpu.VMEM((rows, width), f32),
            pltpu.VMEM((rows, width), bf16),
            pltpu.SemaphoreType.DMA((2,)),
        ]
        + STAGE,
        compiler_params=scoped(16),
        cost_estimate=pl.CostEstimate(flops=900_000_000, bytes_accessed=8_000_000, transcendentals=100_000),
        name="forward",
    )(at, hidden_states, w_in, w_out)


RECEIVED = 4


def normalise_body(local_ref, own_hbm, theirs_hbm, *refs):
    parts, refs = refs[: RECEIVED], refs[RECEIVED :]
    unit_hbm, inv_hbm, row_hbm, send_hbm, unit_ref, inv_ref, row_ref, got_ref, theirs_ref, sems = refs
    first = pltpu.make_async_copy(own_hbm, unit_ref, sems.at[RECEIVED + 1])
    first.start()
    copies = [pltpu.make_async_copy(parts[i], got_ref.at[i], sems.at[i]) for i in range(RECEIVED)]
    picks = pltpu.make_async_copy(
        theirs_hbm.at[:, pl.ds(0, 16), pl.ds(E, E_WIDE - E)], theirs_ref, sems.at[RECEIVED]
    )
    for copy in copies:
        copy.start()
    picks.start()
    first.wait()
    total = unit_ref[...]
    for i in range(RECEIVED):
        copies[i].wait()
        total = total + got_ref[i].astype(f32)
    inv = lax.rsqrt(jnp.sum(total * total, axis=-1, keepdims=True) + eps)
    unit = total * inv
    row_ref[:, :E] = unit.astype(bf16)
    copies = [
        pltpu.make_async_copy(row_ref.at[:, pl.ds(0, E)], send_hbm.at[j], sems.at[RECEIVED + 4 + j]) for j in range(GROUPS)
    ]
    for copy in copies:
        copy.start()
    unit_ref[...] = unit
    inv_ref[...] = jnp.broadcast_to(inv, inv_ref.shape)
    copies.append(pltpu.make_async_copy(unit_ref, unit_hbm, sems.at[RECEIVED + 1]))
    copies[-1].start()
    copies.append(pltpu.make_async_copy(inv_ref, inv_hbm, sems.at[RECEIVED + 2]))
    copies[-1].start()
    shape = (16, E_WIDE - E)
    lane = lax.broadcasted_iota(jnp.int32, shape, 1)
    block = lax.broadcasted_iota(jnp.int32, shape, 0)
    group, end = lane // RB, lane % RB
    picks.wait()
    other = jnp.zeros(shape, f32)
    for j in range(GROUPS):
        other = other + jnp.where(group == j, theirs_ref[j].astype(f32), 0.0)
    as_row = (local_ref[0:1, :] == block) & (local_ref[1:2, :] == end)
    as_key = (local_ref[2:3, :] == block) & (other.astype(jnp.int32) == end)
    counts = as_row.astype(f32) + as_key.astype(f32)
    counts = jnp.where((group < GROUPS) & (block < RB), counts, 0.0)
    row_ref[:, E:] = jnp.concatenate([counts, jnp.zeros((SHARD - 16, E_WIDE - E), f32)], axis=0).astype(bf16)
    copies.append(pltpu.make_async_copy(row_ref, row_hbm, sems.at[RECEIVED + 3]))
    copies[-1].start()
    for copy in copies:
        copy.wait()


def normalise(own, local, theirs, parts):
    return pl.pallas_call(
        normalise_body,
        out_shape=[
            pltpu.HBM((SHARD, E), f32),
            pltpu.HBM((SHARD, BLK), f32),
            pltpu.HBM((SHARD, E_WIDE), bf16),
            pltpu.HBM((GROUPS, SHARD, E), bf16),
        ],
        in_specs=in_vmem(1) + in_place(RECEIVED + 2),
        out_specs=in_place(4),
        scratch_shapes=[
            pltpu.VMEM((SHARD, E), f32),
            pltpu.VMEM((SHARD, BLK), f32),
            pltpu.VMEM((SHARD, E_WIDE), bf16),
            pltpu.VMEM((RECEIVED, SHARD, E), bf16),
            pltpu.VMEM((GROUPS, 16, E_WIDE - E), bf16),
            pltpu.SemaphoreType.DMA((RECEIVED + 4 + GROUPS,)),
        ],
        compiler_params=scoped(12),
        cost_estimate=pl.CostEstimate(flops=1_000_000, bytes_accessed=4_000_000, transcendentals=0),
        name="normalise",
    )(local, hbm(own), hbm(theirs), *[hbm(part) for part in parts])


def gather_in(at, pieces, target_ref, wide, sems):
    copies = []
    for n in range(PARTS):
        d = n if n <= 4 else n - 1
        cols = {4: pl.ds(0, LEFT), 5: pl.ds(LEFT, wide - LEFT)}.get(n, pl.ds(0, wide))
        rows = pl.ds(spot_of(at, d), SHARD)
        copies.append(pltpu.make_async_copy(pieces[n], target_ref.at[rows, cols], sems.at[n]))
        copies[-1].start()
    return copies


def gram_body(at_ref, *refs):
    pieces, refs = dict(zip(PIECE_ORDER, refs[:PARTS])), refs[PARTS:]
    keys_hbm, teacher_hbm, spread_ref = refs[:3]
    refs = refs[3:]
    targets = refs[:PARTS]
    row_ref, key_ref, teacher_ref, grad_ref, total_ref, sems = refs[PARTS:]
    contract = (((1,), (1,)), ((), ()))
    step = 256
    spans = [pl.ds(k, step) for k in range(0, GROUPS * SHARD, step)]
    row_copies = gather_in(at_ref[0], pieces, row_ref, E_WIDE, sems)
    copies = []
    for i, span in enumerate(spans):
        pair = (
            pltpu.make_async_copy(keys_hbm.at[span, :], key_ref.at[span, :], sems.at[PARTS + 2 * i]),
            pltpu.make_async_copy(teacher_hbm.at[:, span], teacher_ref.at[:, span], sems.at[PARTS + 1 + 2 * i]),
        )
        pair[0].start()
        pair[1].start()
        copies.append(pair)
    for copy in row_copies:
        copy.wait()
    counts = jnp.zeros((16, E_WIDE - E), f32)
    for d in range(NT):
        counts = counts + row_ref[pl.ds(d * SHARD, 16), E:].astype(f32)
    tile = jnp.dot(counts.astype(bf16), spread_ref[...], preferred_element_type=f32) * (E / 8.0)
    for i, span in enumerate(spans):
        copies[i][0].wait()
        copies[i][1].wait()
        diff = (
            lax.dot_general(row_ref[:, :E], key_ref[span, :], contract, preferred_element_type=f32)
            - teacher_ref[:, span]
        )
        for a in range(RB):
            grad_ref[pl.ds(a * BLK, BLK), span] = (
                diff[a * BLK : (a + 1) * BLK] * tile[a : a + 1, i * step : (i + 1) * step]
            ).astype(bf16)
    for c, wide in ((0, 768), (768, 640)):
        total_ref[:, pl.ds(c, wide)] = jnp.dot(
            grad_ref[...], key_ref[:, pl.ds(c, wide)], preferred_element_type=f32
        )
    chunk_store(total_ref, at_ref[0], targets)


def gram_grads(at, pieces, keys, gram_teacher, spread):
    steps = GROUPS * SHARD // 256
    return pl.pallas_call(
        gram_body,
        out_shape=[jax.ShapeDtypeStruct(chunk.shape, chunk.dtype) for chunk in CHUNKS],
        in_specs=[IN_SMEM] + in_place(PARTS + 2) + in_vmem(1),
        out_specs=in_vmem(PARTS),
        scratch_shapes=[
            pltpu.VMEM((ROWS, E_WIDE), bf16),
            pltpu.VMEM((GROUPS * SHARD, E), bf16),
            pltpu.VMEM((ROWS, GROUPS * SHARD), f32),
            pltpu.VMEM((ROWS, GROUPS * SHARD), bf16),
            pltpu.VMEM((ROWS, E), f32),
            pltpu.SemaphoreType.DMA((PARTS + 2 * steps,)),
        ],
        compiler_params=scoped(20),
        cost_estimate=pl.CostEstimate(flops=1_700_000_000, bytes_accessed=9_000_000, transcendentals=0),
        name="gram_grads",
    )(at, *[hbm(pieces[n]) for n in PIECE_ORDER], hbm(keys), hbm(gram_teacher), spread)


def backward_body(at_ref, *refs):
    pieces, refs = dict(zip(PIECE_ORDER, refs[:PARTS])), refs[PARTS:]
    hidden_ref, w_out_ref, pre_ref, act_ref = refs[:4]
    keep_ref, give_ref, grad_pre_hbm, grad_pre_ref, proj_ref, sems = refs[4:]
    at, tea = at_ref[0], at_ref[1]
    contract = (((1,), (1,)), ((), ()))
    over_rows = (((0,), (0,)), ((), ()))
    copies = gather_in(at, pieces, proj_ref, E, sems)
    proj_ref[:, E:] = jnp.zeros((ROWS, E_PAD - E), bf16)
    pre = pre_ref[...]
    sigma = 1.0 / (1.0 + jnp.exp(-pre))
    slope = sigma * (1.0 + pre * (1.0 - sigma))
    for copy in copies:
        copy.wait()
    grad_act = lax.dot_general(proj_ref[:, :E], w_out_ref[...], contract, preferred_element_type=f32)
    grad_pre = (grad_act * slope).astype(bf16)
    grad_pre_ref[...] = grad_pre
    copy = pltpu.make_async_copy(grad_pre_ref, grad_pre_hbm, sems.at[0])
    copy.start()
    d_half, e_half = hidden_ref.shape[1] // 2, E_PAD // 2
    in_rows, out_rows = d_half // GROUPS, e_half // GROUPS
    for ref, side in ((give_ref, 1 - tea), (keep_ref, tea)):
        part = hidden_ref[:, pl.ds(pl.multiple_of(side * d_half, d_half), d_half)]
        grad = lax.dot_general(part, grad_pre, over_rows, preferred_element_type=f32)
        for c in range(GROUPS):
            ref[c, pl.ds(0, in_rows), :] = grad[c * in_rows : (c + 1) * in_rows].astype(ref.dtype)
        part = proj_ref[:, pl.ds(pl.multiple_of(side * e_half, e_half), e_half)]
        grad = lax.dot_general(part, act_ref[...], over_rows, preferred_element_type=f32)
        for c in range(GROUPS):
            ref[c, pl.ds(in_rows, out_rows), :] = grad[c * out_rows : (c + 1) * out_rows].astype(ref.dtype)
    copy.wait()


def backward(where, pieces, hidden_states, w_out, pre_act, activation):
    rows, d_model = hidden_states.shape
    width = activation.shape[1]
    halves = (GROUPS, (d_model + E_PAD) // 2 // GROUPS, width)
    return pl.pallas_call(
        backward_body,
        out_shape=[
            jax.ShapeDtypeStruct(halves, f32),
            jax.ShapeDtypeStruct(halves, bf16),
            pltpu.HBM((rows, width), bf16),
        ],
        in_specs=[IN_SMEM] + in_place(PARTS) + in_vmem(4),
        out_specs=in_vmem(2) + in_place(1),
        scratch_shapes=[
            pltpu.VMEM((rows, width), bf16),
            pltpu.VMEM((ROWS, E_PAD), bf16),
            pltpu.SemaphoreType.DMA((PARTS,)),
        ],
        compiler_params=scoped(20),
        cost_estimate=pl.CostEstimate(flops=1_200_000_000, bytes_accessed=9_000_000, transcendentals=100_000),
        name="backward",
    )(where, *[pieces[d] for d in PIECE_ORDER], hidden_states, w_out, pre_act, activation)


def hidden_body(at_ref, grad_pre_hbm, w_in_ref, *refs):
    targets, refs = refs[:PARTS], refs[PARTS:]
    grad_pre_ref, wide_ref, full_ref, sems, first_sem = refs
    first = pltpu.make_async_copy(grad_pre_hbm, grad_pre_ref, first_sem)
    first.start()
    contract = (((1,), (1,)), ((), ()))
    share = w_in_ref.shape[0] // NT
    half = ROWS // 2
    copies = []
    first.wait()
    for d in (3, 5, 4, 1, 7, 2, 6, 0):
        rows = pl.ds(pl.multiple_of(lax.rem(at_ref[0] + d, NT) * share, share), share)
        terms = lax.dot_general(grad_pre_ref[...], w_in_ref[rows, :], contract, preferred_element_type=f32)
        if d in (0, 2, 6):
            source = wide_ref.at[d // 2 if d < 6 else 2]
        else:
            source = full_ref.at[(1, 3, 4, 5, 7).index(d)]
            terms = terms.astype(bf16)
        source[...] = terms
        if d == 4:
            pairs = [(source.at[pl.ds(0, half), :], 4), (source.at[pl.ds(half, half), :], 5)]
        else:
            pairs = [(source, d if d < 4 else d + 1)]
        for part, n in pairs:
            copies.append(pltpu.make_async_copy(part, targets[n], sems.at[n]))
            copies[-1].start()
    for copy in copies:
        copy.wait()


def hidden_grads(at, grad_pre, w_in):
    share = w_in.shape[0] // NT
    wide, full, half = (pltpu.HBM((rows, share), kind) for rows, kind in ((ROWS, f32), (ROWS, bf16), (ROWS // 2, bf16)))
    return pl.pallas_call(
        hidden_body,
        out_shape=[wide, full, wide, full, half, half, full, wide, full],
        in_specs=[IN_SMEM] + in_place(1) + in_vmem(1),
        out_specs=in_place(PARTS),
        scratch_shapes=[
            pltpu.VMEM(grad_pre.shape, bf16),
            pltpu.VMEM((3, ROWS, share), f32),
            pltpu.VMEM((5, ROWS, share), bf16),
            pltpu.SemaphoreType.DMA((PARTS,)),
            pltpu.SemaphoreType.DMA,
        ],
        compiler_params=scoped(14),
        cost_estimate=pl.CostEstimate(flops=600_000_000, bytes_accessed=5_000_000, transcendentals=0),
        name="hidden_grads",
    )(at, hbm(grad_pre), w_in)


def pair_body(keep_ref, got_ref, sum_ref):
    sum_ref[...] = (keep_ref[...] + got_ref[...].astype(f32)).astype(bf16)


def pair_sum(keep, got):
    return pl.pallas_call(
        pair_body,
        out_shape=jax.ShapeDtypeStruct(keep.shape, bf16),
        in_specs=in_vmem(2),
        out_specs=in_vmem(1)[0],
        compiler_params=scoped(8),
        cost_estimate=pl.CostEstimate(flops=600_000, bytes_accessed=5_000_000, transcendentals=0),
        name="pair_sum",
    )(keep, got)


def half_out(ref, side, w_in_hbm, w_out_hbm, w_in_ref, w_out_ref, flat_ref, sems):
    d_half, e_half = w_in_ref.shape[0], E_PAD // 2
    in_rows, out_rows = d_half // GROUPS, e_half // GROUPS
    for c in range(GROUPS):
        w_in_ref[pl.ds(c * in_rows, in_rows), :] = ref[c, pl.ds(0, in_rows), :].astype(f32)
    copy = pltpu.make_async_copy(
        w_in_ref, w_in_hbm.at[pl.ds(pl.multiple_of(side * d_half, d_half), d_half), :], sems.at[0]
    )
    copy.start()
    for c in range(GROUPS):
        flat_ref[pl.ds(c * out_rows, out_rows), :] = ref[c, pl.ds(in_rows, out_rows), :].astype(f32)
    for c in range(0, e_half, BLK):
        w_out_ref[:, pl.ds(c, BLK)] = flat_ref[pl.ds(c, BLK), :].T
    for which, start, size in ((0, 0, e_half), (1, e_half, E - e_half)):

        @pl.when(side == which)
        def _():
            part = pltpu.make_async_copy(
                w_out_ref.at[:, pl.ds(0, size)], w_out_hbm.at[:, pl.ds(start, size)], sems.at[1]
            )
            part.start()
            part.wait()

    copy.wait()


def first_body(tea_ref, mine_ref, own_hbm, *refs):
    parts, refs = refs[:RECEIVED], refs[RECEIVED:]
    w_in_hbm, w_out_hbm, hidden_ref, w_in_ref, w_out_ref, flat_ref, own_ref, got_ref, sems = refs
    copies = [pltpu.make_async_copy(own_hbm, own_ref, sems.at[RECEIVED + 2])]
    for i in range(RECEIVED):
        copies.append(pltpu.make_async_copy(parts[i], got_ref.at[i], sems.at[2 + i]))
    for copy in copies:
        copy.start()
    half_out(mine_ref, tea_ref[0], w_in_hbm, w_out_hbm, w_in_ref, w_out_ref, flat_ref, sems)
    for copy in copies:
        copy.wait()
    total = own_ref[...]
    for i in range(RECEIVED):
        total = total + got_ref[i].astype(f32)
    hidden_ref[...] = total


def second_body(tea_ref, other_ref, w_in_old, w_out_old, w_in_hbm, w_out_hbm, w_in_ref, w_out_ref, flat_ref, sems):
    half_out(other_ref, 1 - tea_ref[0], w_in_hbm, w_out_hbm, w_in_ref, w_out_ref, flat_ref, sems)


def half_scratch(d_model, width):
    return [
        pltpu.VMEM((d_model // 2, width), f32),
        pltpu.VMEM((width, E_PAD // 2), f32),
        pltpu.VMEM((E_PAD // 2, width), f32),
    ]


def first_half(tea, mine, own, parts, d_model):
    width = mine.shape[-1]
    return pl.pallas_call(
        first_body,
        out_shape=[
            pltpu.HBM((d_model, width), f32),
            pltpu.HBM((width, E), f32),
            jax.ShapeDtypeStruct(own.shape, f32),
        ],
        in_specs=[IN_SMEM] + in_vmem(1) + in_place(1 + RECEIVED),
        out_specs=in_place(2) + in_vmem(1),
        scratch_shapes=half_scratch(d_model, width)
        + [
            pltpu.VMEM(own.shape, f32),
            pltpu.VMEM((RECEIVED,) + own.shape, bf16),
            pltpu.SemaphoreType.DMA((RECEIVED + 3,)),
        ],
        compiler_params=scoped(12),
        cost_estimate=pl.CostEstimate(flops=0, bytes_accessed=5_000_000, transcendentals=0),
        name="first_half",
    )(tea, mine, hbm(own), *parts)


def second_half(tea, other, w_in, w_out):
    return pl.pallas_call(
        second_body,
        out_shape=[pltpu.HBM(w_in.shape, f32), pltpu.HBM(w_out.shape, f32)],
        in_specs=[IN_SMEM] + in_vmem(1) + in_place(2),
        out_specs=in_place(2),
        scratch_shapes=half_scratch(w_in.shape[0], w_in.shape[1]) + [pltpu.SemaphoreType.DMA((2,))],
        input_output_aliases={2: 0, 3: 1},
        compiler_params=scoped(12),
        cost_estimate=pl.CostEstimate(flops=0, bytes_accessed=4_000_000, transcendentals=0),
        name="second_half",
    )(tea, other, hbm(w_in), hbm(w_out))


def on_device(hidden_states, w_in, w_out, teacher, patch_map, row_pick, key_pick):
    seq_index = lax.axis_index("seq")
    tp_index = lax.axis_index("tp")
    tea_index = lax.axis_index("tea")
    at = jnp.full((1,), tp_index, jnp.int32)
    tea = jnp.full((1,), tea_index, jnp.int32)
    contract = (((1,), (1,)), ((), ()))

    picks = row_pick.reshape(GROUPS)
    group = jnp.full((1,), lax.axis_index(("seq", "tea")), jnp.int32)
    row_teacher, teacher_send = align(jnp.concatenate([at, group]), teacher, patch_map.reshape(1, ROWS), picks)
    teacher_send, at_next = lax.optimization_barrier((teacher_send, at))
    teacher_got = lax.all_to_all(teacher_send, "seq", 0, 0, tiled=True)

    pre_act, activation, *chunks = forward(at_next, hidden_states, w_in, w_out)
    activation, key_pick, picks = lax.optimization_barrier((activation, key_pick, picks))
    received = sum_ring(*chunks)

    table = key_pick.reshape(GROUPS, GROUPS)
    of_rows = lax.dynamic_index_in_dim(table, seq_index, axis=0, keepdims=False)
    of_keys = lax.dynamic_index_in_dim(table, seq_index, axis=1, keepdims=False)
    local = jnp.repeat(jnp.stack([picks, of_rows, of_keys]), RB, axis=1)
    local = jnp.pad(local, ((0, 8 - 3), (0, E_WIDE - E - GROUPS * RB)))
    key_ids = jnp.arange(GROUPS * SHARD, dtype=jnp.int32)
    key_cell = key_ids // SHARD * RB + (tp_index * SHARD + key_ids % SHARD) // BLK
    spread = (jnp.arange(E_WIDE - E, dtype=jnp.int32)[:, None] == key_cell[None, :]).astype(bf16)

    *received, teacher_got = lax.optimization_barrier((*received, teacher_got))
    unit_student, inv_norm, row_send, key_send = normalise(chunks[0], local, teacher_got, received)
    rows = gather_ring(row_send)
    keys = lax.all_to_all(key_send, "seq", 0, 0, tiled=True).reshape(GROUPS * SHARD, E)
    teacher_got, inv_norm = lax.optimization_barrier((teacher_got, inv_norm))
    inv_norm = inv_norm[:, :1]
    key_teacher = teacher_got[:, :, :E].reshape(GROUPS * SHARD, E)
    gram_teacher = lax.dot_general(row_teacher, key_teacher, contract, preferred_element_type=f32)

    row_grad = gram_grads(at, rows, keys, gram_teacher, spread)
    unit_grad = row_grad[0]
    for piece in sum_ring(*row_grad):
        unit_grad = unit_grad + piece.astype(f32)
    inner = jnp.sum(unit_student * unit_grad, axis=-1, keepdims=True)
    grad_proj = ((unit_grad - unit_student * inner) * inv_norm).astype(bf16)
    pieces = gather_ring(grad_proj)

    where = jnp.concatenate([at, tea])
    keep, give, grad_pre = backward(where, pieces, hidden_states, w_out, pre_act, activation)
    got = swap_tea(give)
    hidden_terms = hidden_grads(at, grad_pre, w_in)
    chip, *hidden_terms = lax.optimization_barrier((pair_sum(keep, got), *hidden_terms))
    one, seven, two, six = pass_near(*hidden_terms, axis=0)
    chip = lax.all_to_all(chip, "seq", 0, 0, tiled=True)
    mine = jnp.sum(chip.astype(f32), axis=0).astype(bf16)
    mine, one, seven, two, six = lax.optimization_barrier((mine, one, seven, two, six))
    hidden_got = [one, seven, shift_tp(two, 2), shift_tp(six, -2)]
    mine = to_all(mine).reshape(keep.shape)
    mine, *hidden_got = lax.optimization_barrier((mine, *hidden_got))
    other = swap_tea(mine)
    grad_w_in, grad_w_out, grad_hidden = first_half(tea, mine, hidden_terms[0], hidden_got, hidden_states.shape[1])
    grad_w_in, grad_w_out = second_half(tea, other, grad_w_in, grad_w_out)
    return (grad_hidden, grad_w_in, grad_w_out)


def solution(mesh):
    return jax.shard_map(
        on_device,
        mesh=mesh,
        in_specs=(
            P(("seq", "tea"), None),
            P(None, "tp"),
            P("tp", None),
            P(("seq", "tea"), None),
            P(("seq", "tea")),
            P("seq", "tp", "tea", None),
            P(None, "tp", "tea", None),
        ),
        out_specs=(P(("seq", "tea"), "tp"), P(None, "tp"), P("tp", None)),
        check_vma=False,
    )
```

```python
import jax
import jax.numpy as jnp
from jax import lax
from jax.experimental import pallas as pl
from jax.experimental.pallas import tpu as pltpu
from jax.sharding import PartitionSpec as P

E = 1408
BLK = 128
RB = 3
SIDE = 4
NT = 8
GROUPS = SIDE * SIDE
SHARD = 48
ROWS = 384
E_WIDE = 1536
E_PAD = 1536

eps = 1e-06
bf16 = jnp.bfloat16
f32 = jnp.float32


def shift_tp(x, step):
    return lax.ppermute(x, "tp", [(i, (i + step) % NT) for i in range(NT)])


def swap_tea(x):
    return lax.ppermute(x, "tea", [(0, 1), (1, 0)])


LEFT = 768
RIGHT = 640


def gather_ring(x):
    before, after = shift_tp(x, 1), shift_tp(x, -1)
    before2, after2 = shift_tp(x, 2), shift_tp(x, -2)
    before3, after3 = shift_tp(before2, 1), shift_tp(after2, -1)
    left, right = shift_tp(before2[:, :LEFT], 2), shift_tp(after2[:, LEFT:], -2)
    return [x, after, after2, after3, left, right, before3, before2, before]


def pass_near(own, one, two, three, left, right, five, six, seven):
    three, five = shift_tp(three, 1), shift_tp(five, -1)
    left, right = shift_tp(left, 2), shift_tp(right, -2)
    one, seven = shift_tp(one, 1), shift_tp(seven, -1)
    blank = jnp.zeros(left.shape, f32), jnp.zeros(right.shape, f32)
    two = two + three.astype(f32) + jnp.concatenate([left.astype(f32), blank[1]], axis=1)
    six = six + five.astype(f32) + jnp.concatenate([blank[0], right.astype(f32)], axis=1)
    return one, seven, two.astype(bf16), six.astype(bf16)


def sum_ring(*terms):
    one, seven, two, six = pass_near(*terms)
    return [one, seven, shift_tp(two, 2), shift_tp(six, -2)]


def to_all(x):
    return lax.all_to_all(jnp.broadcast_to(x[None], (GROUPS,) + x.shape), "seq", 0, 0, tiled=True)


def in_vmem(count):
    return [pl.BlockSpec(memory_space=pltpu.VMEM)] * count


def in_place(count):
    return [pl.BlockSpec(memory_space=pltpu.HBM)] * count


def hbm(x):
    return pltpu.with_memory_space_constraint(x, pltpu.HBM)


IN_SMEM = pl.BlockSpec(memory_space=pltpu.SMEM)
def scoped(mib):
    return pltpu.CompilerParams(vmem_limit_bytes=mib * 1024 * 1024)


PIECE_ORDER = (0, 1, 8, 2, 7, 3, 6, 4, 5)


def spot_of(at, d):
    return pl.multiple_of(lax.rem(at + d, NT) * SHARD, SHARD)


def chunk_out(total_ref, at, targets, stage_ref, sems):
    copies = []
    slot = 0
    for n, d, cols in (
        (3, 3, None),
        (6, 5, None),
        (4, 4, pl.ds(0, LEFT)),
        (5, 4, pl.ds(LEFT, RIGHT)),
        (1, 1, None),
        (8, 7, None),
        (2, 2, None),
        (7, 6, None),
        (0, 0, None),
    ):
        rows = pl.ds(spot_of(at, d), SHARD)
        if d in (0, 2, 6):
            source = total_ref.at[rows, :]
        else:
            if n != 5:
                stage_ref[slot] = total_ref[rows, :].astype(bf16)
                slot += 1
            source = stage_ref.at[slot - 1] if cols is None else stage_ref.at[slot - 1, :, cols]
        copies.append(pltpu.make_async_copy(source, targets[n], sems.at[n]))
        copies[-1].start()
    return copies


def chunk_store(total_ref, at, targets):
    for n, target in enumerate(targets):
        d = n if n <= 4 else n - 1
        cols = {4: pl.ds(0, LEFT), 5: pl.ds(LEFT, RIGHT)}.get(n, pl.ds(0, E))
        target[...] = total_ref[pl.ds(spot_of(at, d), SHARD), cols].astype(target.dtype)


PARTS = NT + 1
STAGE = [pltpu.VMEM((5, SHARD, E), bf16), pltpu.SemaphoreType.DMA((PARTS,))]
WIDE, FULL = pltpu.HBM((SHARD, E), f32), pltpu.HBM((SHARD, E), bf16)
CHUNKS = [WIDE, FULL, WIDE, FULL, pltpu.HBM((SHARD, LEFT), bf16), pltpu.HBM((SHARD, RIGHT), bf16), FULL, WIDE, FULL]


def align_body(at_ref, teacher_hbm, patch_ref, picks_ref, rows_hbm, send_hbm, teacher_ref, rows_ref, own_ref, extra_ref, sems):
    copy = pltpu.make_async_copy(teacher_hbm, teacher_ref, sems.at[GROUPS])
    copy.start()
    for j in range(GROUPS):
        extra_ref[j] = jnp.full(extra_ref.shape[1:], picks_ref[j], jnp.int32).astype(f32).astype(bf16)
    extra = pltpu.make_async_copy(extra_ref, send_hbm.at[:, :, pl.ds(E, E_WIDE - E)], sems.at[GROUPS + 1])
    extra.start()
    copy.wait()
    teacher = teacher_ref[...].astype(f32)
    unit = (teacher * lax.rsqrt(jnp.sum(teacher * teacher, axis=-1, keepdims=True) + eps)).astype(bf16)
    ids = lax.broadcasted_iota(jnp.int32, (teacher.shape[0], ROWS), 0)
    hot = (ids == patch_ref[...] - at_ref[1] * teacher.shape[0]).astype(f32).astype(bf16)
    rows_ref[...] = lax.dot_general(
        hot, unit, (((0,), (0,)), ((), ())), preferred_element_type=f32
    ).astype(bf16)
    copies = [pltpu.make_async_copy(rows_ref, rows_hbm, sems.at[GROUPS])]
    copies[0].start()
    own_ref[...] = rows_ref[pl.ds(spot_of(at_ref[0], 0), SHARD), :]
    for j in range(GROUPS):
        copies.append(pltpu.make_async_copy(own_ref, send_hbm.at[j, :, pl.ds(0, E)], sems.at[j]))
        copies[-1].start()
    copies.append(extra)
    for copy in copies:
        copy.wait()


def align(at, teacher, patch, picks):
    return pl.pallas_call(
        align_body,
        out_shape=[
            pltpu.HBM((ROWS, E), bf16),
            pltpu.HBM((GROUPS, SHARD, E_WIDE), bf16),
        ],
        in_specs=[IN_SMEM] + in_place(1) + in_vmem(1) + [IN_SMEM],
        out_specs=in_place(2),
        scratch_shapes=[
            pltpu.VMEM(teacher.shape, bf16),
            pltpu.VMEM((ROWS, E), bf16),
            pltpu.VMEM((SHARD, E), bf16),
            pltpu.VMEM((GROUPS, SHARD, E_WIDE - E), bf16),
            pltpu.SemaphoreType.DMA((GROUPS + 2,)),
        ],
        compiler_params=scoped(12),
        cost_estimate=pl.CostEstimate(flops=250_000_000, bytes_accessed=4_000_000, transcendentals=0),
        name="align",
    )(at, hbm(teacher), patch, picks)


def forward_body(at_ref, hidden_ref, w_in_ref, w_out_ref, pre_hbm, act_hbm, *refs):
    targets = refs[:PARTS]
    total_ref, pre_ref, act_ref, sems, stage_ref, stage_sems = refs[PARTS:]
    pre = jnp.dot(hidden_ref[...], w_in_ref[...], preferred_element_type=f32)
    pre_ref[...] = pre
    act = (pre / (1.0 + jnp.exp(-pre))).astype(bf16)
    act_ref[...] = act
    copies = [
        pltpu.make_async_copy(pre_ref, pre_hbm, sems.at[0]),
        pltpu.make_async_copy(act_ref, act_hbm, sems.at[1]),
    ]
    for copy in copies:
        copy.start()
    total_ref[...] = jnp.dot(act, w_out_ref[...], preferred_element_type=f32)
    copies += chunk_out(total_ref, at_ref[0], targets, stage_ref, stage_sems)
    for copy in copies:
        copy.wait()


def forward(at, hidden_states, w_in, w_out):
    rows, width = hidden_states.shape[0], w_in.shape[1]
    return pl.pallas_call(
        forward_body,
        out_shape=[pltpu.HBM((rows, width), f32), pltpu.HBM((rows, width), bf16)] + CHUNKS,
        in_specs=[IN_SMEM] + in_vmem(3),
        out_specs=in_place(2 + PARTS),
        scratch_shapes=[
            pltpu.VMEM((rows, E), f32),
            pltpu.VMEM((rows, width), f32),
            pltpu.VMEM((rows, width), bf16),
            pltpu.SemaphoreType.DMA((2,)),
        ]
        + STAGE,
        compiler_params=scoped(16),
        cost_estimate=pl.CostEstimate(flops=900_000_000, bytes_accessed=8_000_000, transcendentals=100_000),
        name="forward",
    )(at, hidden_states, w_in, w_out)


RECEIVED = 4


def normalise_body(local_ref, own_hbm, theirs_hbm, *refs):
    parts, refs = refs[: RECEIVED], refs[RECEIVED :]
    unit_hbm, inv_hbm, row_hbm, send_hbm, unit_ref, inv_ref, row_ref, got_ref, theirs_ref, sems = refs
    first = pltpu.make_async_copy(own_hbm, unit_ref, sems.at[RECEIVED + 1])
    first.start()
    copies = [pltpu.make_async_copy(parts[i], got_ref.at[i], sems.at[i]) for i in range(RECEIVED)]
    picks = pltpu.make_async_copy(
        theirs_hbm.at[:, pl.ds(0, 16), pl.ds(E, E_WIDE - E)], theirs_ref, sems.at[RECEIVED]
    )
    for copy in copies:
        copy.start()
    picks.start()
    first.wait()
    total = unit_ref[...]
    for i in range(RECEIVED):
        copies[i].wait()
        total = total + got_ref[i].astype(f32)
    inv = lax.rsqrt(jnp.sum(total * total, axis=-1, keepdims=True) + eps)
    unit = total * inv
    row_ref[:, :E] = unit.astype(bf16)
    copies = [
        pltpu.make_async_copy(row_ref.at[:, pl.ds(0, E)], send_hbm.at[j], sems.at[RECEIVED + 4 + j]) for j in range(GROUPS)
    ]
    for copy in copies:
        copy.start()
    unit_ref[...] = unit
    inv_ref[...] = jnp.broadcast_to(inv, inv_ref.shape)
    copies.append(pltpu.make_async_copy(unit_ref, unit_hbm, sems.at[RECEIVED + 1]))
    copies[-1].start()
    copies.append(pltpu.make_async_copy(inv_ref, inv_hbm, sems.at[RECEIVED + 2]))
    copies[-1].start()
    shape = (16, E_WIDE - E)
    lane = lax.broadcasted_iota(jnp.int32, shape, 1)
    block = lax.broadcasted_iota(jnp.int32, shape, 0)
    group, end = lane // RB, lane % RB
    picks.wait()
    other = jnp.zeros(shape, f32)
    for j in range(GROUPS):
        other = other + jnp.where(group == j, theirs_ref[j].astype(f32), 0.0)
    as_row = (local_ref[0:1, :] == block) & (local_ref[1:2, :] == end)
    as_key = (local_ref[2:3, :] == block) & (other.astype(jnp.int32) == end)
    counts = as_row.astype(f32) + as_key.astype(f32)
    counts = jnp.where((group < GROUPS) & (block < RB), counts, 0.0)
    row_ref[:, E:] = jnp.concatenate([counts, jnp.zeros((SHARD - 16, E_WIDE - E), f32)], axis=0).astype(bf16)
    copies.append(pltpu.make_async_copy(row_ref, row_hbm, sems.at[RECEIVED + 3]))
    copies[-1].start()
    for copy in copies:
        copy.wait()


def normalise(own, local, theirs, parts):
    return pl.pallas_call(
        normalise_body,
        out_shape=[
            pltpu.HBM((SHARD, E), f32),
            pltpu.HBM((SHARD, BLK), f32),
            pltpu.HBM((SHARD, E_WIDE), bf16),
            pltpu.HBM((GROUPS, SHARD, E), bf16),
        ],
        in_specs=in_vmem(1) + in_place(RECEIVED + 2),
        out_specs=in_place(4),
        scratch_shapes=[
            pltpu.VMEM((SHARD, E), f32),
            pltpu.VMEM((SHARD, BLK), f32),
            pltpu.VMEM((SHARD, E_WIDE), bf16),
            pltpu.VMEM((RECEIVED, SHARD, E), bf16),
            pltpu.VMEM((GROUPS, 16, E_WIDE - E), bf16),
            pltpu.SemaphoreType.DMA((RECEIVED + 4 + GROUPS,)),
        ],
        compiler_params=scoped(12),
        cost_estimate=pl.CostEstimate(flops=1_000_000, bytes_accessed=4_000_000, transcendentals=0),
        name="normalise",
    )(local, hbm(own), hbm(theirs), *[hbm(part) for part in parts])


def gather_in(at, pieces, target_ref, wide, sems):
    copies = []
    for n in range(PARTS):
        d = n if n <= 4 else n - 1
        cols = {4: pl.ds(0, LEFT), 5: pl.ds(LEFT, wide - LEFT)}.get(n, pl.ds(0, wide))
        rows = pl.ds(spot_of(at, d), SHARD)
        copies.append(pltpu.make_async_copy(pieces[n], target_ref.at[rows, cols], sems.at[n]))
        copies[-1].start()
    return copies


def gram_body(at_ref, *refs):
    pieces, refs = dict(zip(PIECE_ORDER, refs[:PARTS])), refs[PARTS:]
    keys_hbm, teacher_hbm, spread_ref = refs[:3]
    refs = refs[3:]
    targets = refs[:PARTS]
    row_ref, key_ref, teacher_ref, grad_ref, total_ref, sems = refs[PARTS:]
    contract = (((1,), (1,)), ((), ()))
    step = 256
    spans = [pl.ds(k, step) for k in range(0, GROUPS * SHARD, step)]
    row_copies = gather_in(at_ref[0], pieces, row_ref, E_WIDE, sems)
    copies = []
    for i, span in enumerate(spans):
        pair = (
            pltpu.make_async_copy(keys_hbm.at[span, :], key_ref.at[span, :], sems.at[PARTS + 2 * i]),
            pltpu.make_async_copy(teacher_hbm.at[:, span], teacher_ref.at[:, span], sems.at[PARTS + 1 + 2 * i]),
        )
        pair[0].start()
        pair[1].start()
        copies.append(pair)
    for copy in row_copies:
        copy.wait()
    counts = jnp.zeros((16, E_WIDE - E), f32)
    for d in range(NT):
        counts = counts + row_ref[pl.ds(d * SHARD, 16), E:].astype(f32)
    tile = jnp.dot(counts.astype(bf16), spread_ref[...], preferred_element_type=f32) * (E / 8.0)
    for i, span in enumerate(spans):
        copies[i][0].wait()
        copies[i][1].wait()
        diff = (
            lax.dot_general(row_ref[:, :E], key_ref[span, :], contract, preferred_element_type=f32)
            - teacher_ref[:, span]
        )
        for a in range(RB):
            grad_ref[pl.ds(a * BLK, BLK), span] = (
                diff[a * BLK : (a + 1) * BLK] * tile[a : a + 1, i * step : (i + 1) * step]
            ).astype(bf16)
    for c, wide in ((0, 768), (768, 640)):
        total_ref[:, pl.ds(c, wide)] = jnp.dot(
            grad_ref[...], key_ref[:, pl.ds(c, wide)], preferred_element_type=f32
        )
    chunk_store(total_ref, at_ref[0], targets)


def gram_grads(at, pieces, keys, gram_teacher, spread):
    steps = GROUPS * SHARD // 256
    return pl.pallas_call(
        gram_body,
        out_shape=[jax.ShapeDtypeStruct(chunk.shape, chunk.dtype) for chunk in CHUNKS],
        in_specs=[IN_SMEM] + in_place(PARTS + 2) + in_vmem(1),
        out_specs=in_vmem(PARTS),
        scratch_shapes=[
            pltpu.VMEM((ROWS, E_WIDE), bf16),
            pltpu.VMEM((GROUPS * SHARD, E), bf16),
            pltpu.VMEM((ROWS, GROUPS * SHARD), f32),
            pltpu.VMEM((ROWS, GROUPS * SHARD), bf16),
            pltpu.VMEM((ROWS, E), f32),
            pltpu.SemaphoreType.DMA((PARTS + 2 * steps,)),
        ],
        compiler_params=scoped(20),
        cost_estimate=pl.CostEstimate(flops=1_700_000_000, bytes_accessed=9_000_000, transcendentals=0),
        name="gram_grads",
    )(at, *[hbm(pieces[n]) for n in PIECE_ORDER], hbm(keys), hbm(gram_teacher), spread)


def backward_body(at_ref, *refs):
    pieces, refs = dict(zip(PIECE_ORDER, refs[:PARTS])), refs[PARTS:]
    hidden_ref, w_out_ref, pre_ref, act_ref = refs[:4]
    keep_hbm, give_hbm, grad_pre_hbm, keep_ref, give_ref, grad_pre_ref, proj_ref, sems = refs[4:]
    at, tea = at_ref[0], at_ref[1]
    contract = (((1,), (1,)), ((), ()))
    over_rows = (((0,), (0,)), ((), ()))
    copies = gather_in(at, pieces, proj_ref, E, sems)
    proj_ref[:, E:] = jnp.zeros((ROWS, E_PAD - E), bf16)
    pre = pre_ref[...]
    sigma = 1.0 / (1.0 + jnp.exp(-pre))
    slope = sigma * (1.0 + pre * (1.0 - sigma))
    for copy in copies:
        copy.wait()
    grad_act = lax.dot_general(proj_ref[:, :E], w_out_ref[...], contract, preferred_element_type=f32)
    grad_pre = (grad_act * slope).astype(bf16)
    grad_pre_ref[...] = grad_pre
    copies = [pltpu.make_async_copy(grad_pre_ref, grad_pre_hbm, sems.at[0])]
    copies[0].start()
    d_half, e_half = hidden_ref.shape[1] // 2, E_PAD // 2
    in_rows, out_rows = d_half // GROUPS, e_half // GROUPS
    for n, (ref, target, side) in enumerate(((keep_ref, keep_hbm, tea), (give_ref, give_hbm, 1 - tea))):
        part = hidden_ref[:, pl.ds(pl.multiple_of(side * d_half, d_half), d_half)]
        grad = lax.dot_general(part, grad_pre, over_rows, preferred_element_type=f32)
        for c in range(GROUPS):
            ref[c, pl.ds(0, in_rows), :] = grad[c * in_rows : (c + 1) * in_rows].astype(ref.dtype)
        part = proj_ref[:, pl.ds(pl.multiple_of(side * e_half, e_half), e_half)]
        grad = lax.dot_general(part, act_ref[...], over_rows, preferred_element_type=f32)
        for c in range(GROUPS):
            ref[c, pl.ds(in_rows, out_rows), :] = grad[c * out_rows : (c + 1) * out_rows].astype(ref.dtype)
        copies.append(pltpu.make_async_copy(ref, target, sems.at[n + 1]))
        copies[-1].start()
    for copy in copies:
        copy.wait()


def backward(where, pieces, hidden_states, w_out, pre_act, activation):
    rows, d_model = hidden_states.shape
    width = activation.shape[1]
    halves = (GROUPS, (d_model + E_PAD) // 2 // GROUPS, width)
    return pl.pallas_call(
        backward_body,
        out_shape=[
            pltpu.HBM(halves, bf16),
            pltpu.HBM(halves, bf16),
            pltpu.HBM((rows, width), bf16),
        ],
        in_specs=[IN_SMEM] + in_place(PARTS) + in_vmem(4),
        out_specs=in_place(3),
        scratch_shapes=[
            pltpu.VMEM(halves, bf16),
            pltpu.VMEM(halves, bf16),
            pltpu.VMEM((rows, width), bf16),
            pltpu.VMEM((ROWS, E_PAD), bf16),
            pltpu.SemaphoreType.DMA((PARTS,)),
        ],
        compiler_params=scoped(14),
        cost_estimate=pl.CostEstimate(flops=1_200_000_000, bytes_accessed=9_000_000, transcendentals=100_000),
        name="backward",
    )(where, *[pieces[d] for d in PIECE_ORDER], hidden_states, w_out, pre_act, activation)


def hidden_body(grad_pre_hbm, w_in_ref, terms_hbm, grad_pre_ref, terms_ref, sems):
    first = pltpu.make_async_copy(grad_pre_hbm, grad_pre_ref, sems.at[NT])
    first.start()
    contract = (((1,), (1,)), ((), ()))
    share = w_in_ref.shape[0] // NT
    copies = []
    first.wait()
    for d in range(NT):
        span = pl.ds(d * ROWS, ROWS)
        terms_ref[span, :] = lax.dot_general(
            grad_pre_ref[...], w_in_ref[pl.ds(d * share, share), :], contract, preferred_element_type=f32
        ).astype(bf16)
        copies.append(pltpu.make_async_copy(terms_ref.at[span, :], terms_hbm.at[span, :], sems.at[d]))
        copies[-1].start()
    for copy in copies:
        copy.wait()


def hidden_grads(grad_pre, w_in):
    shape = (NT * ROWS, w_in.shape[0] // NT)
    return pl.pallas_call(
        hidden_body,
        out_shape=pltpu.HBM(shape, bf16),
        in_specs=in_place(1) + in_vmem(1),
        out_specs=in_place(1)[0],
        scratch_shapes=[
            pltpu.VMEM(grad_pre.shape, bf16),
            pltpu.VMEM(shape, bf16),
            pltpu.SemaphoreType.DMA((NT + 1,)),
        ],
        compiler_params=scoped(6),
        cost_estimate=pl.CostEstimate(flops=600_000_000, bytes_accessed=4_000_000, transcendentals=0),
        name="hidden_grads",
    )(hbm(grad_pre), w_in)


def pair_body(keep_ref, got_ref, sum_ref):
    sum_ref[...] = (keep_ref[...].astype(f32) + got_ref[...].astype(f32)).astype(bf16)


def pair_sum(keep, got):
    return pl.pallas_call(
        pair_body,
        out_shape=jax.ShapeDtypeStruct(keep.shape, bf16),
        in_specs=in_vmem(2),
        out_specs=in_vmem(1)[0],
        compiler_params=scoped(8),
        cost_estimate=pl.CostEstimate(flops=600_000, bytes_accessed=5_000_000, transcendentals=0),
        name="pair_sum",
    )(keep, got)


def half_out(ref, side, w_in_hbm, w_out_hbm, w_in_ref, w_out_ref, flat_ref, sems):
    d_half, e_half = w_in_ref.shape[0], E_PAD // 2
    in_rows, out_rows = d_half // GROUPS, e_half // GROUPS
    for c in range(GROUPS):
        w_in_ref[pl.ds(c * in_rows, in_rows), :] = ref[c, pl.ds(0, in_rows), :].astype(f32)
    copy = pltpu.make_async_copy(
        w_in_ref, w_in_hbm.at[pl.ds(pl.multiple_of(side * d_half, d_half), d_half), :], sems.at[0]
    )
    copy.start()
    for c in range(GROUPS):
        flat_ref[pl.ds(c * out_rows, out_rows), :] = ref[c, pl.ds(in_rows, out_rows), :].astype(f32)
    for c in range(0, e_half, BLK):
        w_out_ref[:, pl.ds(c, BLK)] = flat_ref[pl.ds(c, BLK), :].T
    for which, start, size in ((0, 0, e_half), (1, e_half, E - e_half)):

        @pl.when(side == which)
        def _():
            part = pltpu.make_async_copy(
                w_out_ref.at[:, pl.ds(0, size)], w_out_hbm.at[:, pl.ds(start, size)], sems.at[1]
            )
            part.start()
            part.wait()

    copy.wait()


def first_body(tea_ref, mine_ref, sum_hbm, w_in_hbm, w_out_hbm, hidden_ref, w_in_ref, w_out_ref, flat_ref, sum_ref, sems):
    copy = pltpu.make_async_copy(sum_hbm, sum_ref, sems.at[2])
    copy.start()
    half_out(mine_ref, tea_ref[0], w_in_hbm, w_out_hbm, w_in_ref, w_out_ref, flat_ref, sems)
    copy.wait()
    hidden_ref[...] = sum_ref[...].astype(f32)


def second_body(tea_ref, other_ref, w_in_old, w_out_old, w_in_hbm, w_out_hbm, w_in_ref, w_out_ref, flat_ref, sems):
    half_out(other_ref, 1 - tea_ref[0], w_in_hbm, w_out_hbm, w_in_ref, w_out_ref, flat_ref, sems)


def half_scratch(d_model, width):
    return [
        pltpu.VMEM((d_model // 2, width), f32),
        pltpu.VMEM((width, E_PAD // 2), f32),
        pltpu.VMEM((E_PAD // 2, width), f32),
    ]


def first_half(tea, mine, hidden, d_model):
    width = mine.shape[-1]
    return pl.pallas_call(
        first_body,
        out_shape=[
            pltpu.HBM((d_model, width), f32),
            pltpu.HBM((width, E), f32),
            jax.ShapeDtypeStruct(hidden.shape, f32),
        ],
        in_specs=[IN_SMEM] + in_vmem(1) + in_place(1),
        out_specs=in_place(2) + in_vmem(1),
        scratch_shapes=half_scratch(d_model, width)
        + [pltpu.VMEM(hidden.shape, bf16), pltpu.SemaphoreType.DMA((3,))],
        compiler_params=scoped(12),
        cost_estimate=pl.CostEstimate(flops=0, bytes_accessed=5_000_000, transcendentals=0),
        name="first_half",
    )(tea, mine, hbm(hidden))


def second_half(tea, other, w_in, w_out):
    return pl.pallas_call(
        second_body,
        out_shape=[pltpu.HBM(w_in.shape, f32), pltpu.HBM(w_out.shape, f32)],
        in_specs=[IN_SMEM] + in_vmem(1) + in_place(2),
        out_specs=in_place(2),
        scratch_shapes=half_scratch(w_in.shape[0], w_in.shape[1]) + [pltpu.SemaphoreType.DMA((2,))],
        input_output_aliases={2: 0, 3: 1},
        compiler_params=scoped(12),
        cost_estimate=pl.CostEstimate(flops=0, bytes_accessed=4_000_000, transcendentals=0),
        name="second_half",
    )(tea, other, hbm(w_in), hbm(w_out))


def on_device(hidden_states, w_in, w_out, teacher, patch_map, row_pick, key_pick):
    seq_index = lax.axis_index("seq")
    tp_index = lax.axis_index("tp")
    tea_index = lax.axis_index("tea")
    at = jnp.full((1,), tp_index, jnp.int32)
    tea = jnp.full((1,), tea_index, jnp.int32)
    contract = (((1,), (1,)), ((), ()))

    picks = row_pick.reshape(GROUPS)
    group = jnp.full((1,), lax.axis_index(("seq", "tea")), jnp.int32)
    row_teacher, teacher_send = align(jnp.concatenate([at, group]), teacher, patch_map.reshape(1, ROWS), picks)
    teacher_send, at_next = lax.optimization_barrier((teacher_send, at))
    teacher_got = lax.all_to_all(teacher_send, "seq", 0, 0, tiled=True)

    pre_act, activation, *chunks = forward(at_next, hidden_states, w_in, w_out)
    activation, key_pick, picks = lax.optimization_barrier((activation, key_pick, picks))
    received = sum_ring(*chunks)

    table = key_pick.reshape(GROUPS, GROUPS)
    of_rows = lax.dynamic_index_in_dim(table, seq_index, axis=0, keepdims=False)
    of_keys = lax.dynamic_index_in_dim(table, seq_index, axis=1, keepdims=False)
    local = jnp.repeat(jnp.stack([picks, of_rows, of_keys]), RB, axis=1)
    local = jnp.pad(local, ((0, 8 - 3), (0, E_WIDE - E - GROUPS * RB)))
    key_ids = jnp.arange(GROUPS * SHARD, dtype=jnp.int32)
    key_cell = key_ids // SHARD * RB + (tp_index * SHARD + key_ids % SHARD) // BLK
    spread = (jnp.arange(E_WIDE - E, dtype=jnp.int32)[:, None] == key_cell[None, :]).astype(bf16)

    *received, teacher_got = lax.optimization_barrier((*received, teacher_got))
    unit_student, inv_norm, row_send, key_send = normalise(chunks[0], local, teacher_got, received)
    rows = gather_ring(row_send)
    keys = lax.all_to_all(key_send, "seq", 0, 0, tiled=True).reshape(GROUPS * SHARD, E)
    teacher_got, inv_norm = lax.optimization_barrier((teacher_got, inv_norm))
    inv_norm = inv_norm[:, :1]
    key_teacher = teacher_got[:, :, :E].reshape(GROUPS * SHARD, E)
    gram_teacher = lax.dot_general(row_teacher, key_teacher, contract, preferred_element_type=f32)

    row_grad = gram_grads(at, rows, keys, gram_teacher, spread)
    unit_grad = row_grad[0]
    for piece in sum_ring(*row_grad):
        unit_grad = unit_grad + piece.astype(f32)
    inner = jnp.sum(unit_student * unit_grad, axis=-1, keepdims=True)
    grad_proj = ((unit_grad - unit_student * inner) * inv_norm).astype(bf16)
    pieces = gather_ring(grad_proj)

    where = jnp.concatenate([at, tea])
    keep, give, grad_pre = backward(where, pieces, hidden_states, w_out, pre_act, activation)
    got = swap_tea(give)
    hidden_terms = hidden_grads(grad_pre, w_in)
    chip, hidden_terms = lax.optimization_barrier((pair_sum(keep, got), hidden_terms))
    hidden_sum = lax.psum_scatter(hidden_terms, "tp", scatter_dimension=0, tiled=True)
    chip = lax.all_to_all(chip, "seq", 0, 0, tiled=True)
    mine = to_all(jnp.sum(chip.astype(f32), axis=0).astype(bf16)).reshape(keep.shape)
    other = swap_tea(mine)
    grad_w_in, grad_w_out, grad_hidden = first_half(tea, mine, hidden_sum, hidden_states.shape[1])
    grad_w_in, grad_w_out = second_half(tea, other, grad_w_in, grad_w_out)
    return (grad_hidden, grad_w_in, grad_w_out)


def solution(mesh):
    return jax.shard_map(
        on_device,
        mesh=mesh,
        in_specs=(
            P(("seq", "tea"), None),
            P(None, "tp"),
            P("tp", None),
            P(("seq", "tea"), None),
            P(("seq", "tea")),
            P("seq", "tp", "tea", None),
            P(None, "tp", "tea", None),
        ),
        out_specs=(P(("seq", "tea"), "tp"), P(None, "tp"), P("tp", None)),
        check_vma=False,
    )
```

```python
import jax
import jax.numpy as jnp
from jax import lax
from jax.experimental import pallas as pl
from jax.experimental.pallas import tpu as pltpu
from jax.sharding import PartitionSpec as P

E = 1408
BLK = 128
RB = 3
SIDE = 4
NT = 8
GROUPS = SIDE * SIDE
SHARD = 48
ROWS = 384
E_WIDE = 1536
E_PAD = 1536

eps = 1e-06
bf16 = jnp.bfloat16
f32 = jnp.float32


def shift_tp(x, step):
    return lax.ppermute(x, "tp", [(i, (i + step) % NT) for i in range(NT)])


def swap_tea(x):
    return lax.ppermute(x, "tea", [(0, 1), (1, 0)])


LEFT = 768
RIGHT = 640


def gather_ring(x):
    before, after = shift_tp(x, 1), shift_tp(x, -1)
    before2, after2 = shift_tp(x, 2), shift_tp(x, -2)
    far_after = shift_tp(jnp.concatenate([after, after2[:, LEFT:]], axis=1), -2)
    far_before = shift_tp(jnp.concatenate([before, before2[:, :LEFT]], axis=1), 2)
    return [x, after, after2, far_after, before2, before, far_before]


def sum_ring(own, one, two, far_after, six, seven, far_before):
    far_after, far_before = shift_tp(far_after, 2).astype(f32), shift_tp(far_before, -2).astype(f32)
    one, seven = one + far_after[:, :E], seven + far_before[:, :E]
    two = two + jnp.concatenate([far_after[:, E:], jnp.zeros((SHARD, RIGHT), f32)], axis=1)
    six = six + jnp.concatenate([jnp.zeros((SHARD, LEFT), f32), far_before[:, E:]], axis=1)
    one, two, six, seven = (v.astype(bf16) for v in (one, two, six, seven))
    return [shift_tp(two, 2), shift_tp(six, -2), shift_tp(one, 1), shift_tp(seven, -1)]


def pass_split(own, one, two, three, left, right, five, six, seven):
    three, five = shift_tp(three, 1), shift_tp(five, -1)
    left, right = shift_tp(left, 2), shift_tp(right, -2)
    one, seven = shift_tp(one, 1), shift_tp(seven, -1)
    blank = jnp.zeros(left.shape, f32), jnp.zeros(right.shape, f32)
    two = two + three.astype(f32) + jnp.concatenate([left.astype(f32), blank[1]], axis=1)
    six = six + five.astype(f32) + jnp.concatenate([blank[0], right.astype(f32)], axis=1)
    return one, seven, two.astype(bf16), six.astype(bf16)


def sum_split(*terms):
    one, seven, two, six = pass_split(*terms)
    return [one, seven, shift_tp(two, 2), shift_tp(six, -2)]


def to_all(x):
    return lax.all_to_all(jnp.broadcast_to(x[None], (GROUPS,) + x.shape), "seq", 0, 0, tiled=True)


def in_vmem(count):
    return [pl.BlockSpec(memory_space=pltpu.VMEM)] * count


def in_place(count):
    return [pl.BlockSpec(memory_space=pltpu.HBM)] * count


def hbm(x):
    return pltpu.with_memory_space_constraint(x, pltpu.HBM)


IN_SMEM = pl.BlockSpec(memory_space=pltpu.SMEM)
def scoped(mib):
    return pltpu.CompilerParams(vmem_limit_bytes=mib * 1024 * 1024)


PIECE_ORDER = (0, 1, 5, 2, 4, 3, 6)


def spot_of(at, d):
    return pl.multiple_of(lax.rem(at + d, NT) * SHARD, SHARD)


PARTS = 7
PLACES = (0, 1, 2, 3, 6, 7, 5)
STAGE = [pltpu.VMEM((5, SHARD, E), bf16), pltpu.SemaphoreType.DMA((NT + 1,))]
WIDE, FULL = pltpu.HBM((SHARD, E), f32), pltpu.HBM((SHARD, E), bf16)
SPLIT = [WIDE, FULL, WIDE, FULL, pltpu.HBM((SHARD, LEFT), bf16), pltpu.HBM((SHARD, RIGHT), bf16), FULL, WIDE, FULL]
CHUNKS = [
    WIDE,
    WIDE,
    WIDE,
    pltpu.HBM((SHARD, E + LEFT), bf16),
    WIDE,
    WIDE,
    pltpu.HBM((SHARD, E + RIGHT), bf16),
]


def far_parts(total_ref, at, after_ref, before_ref):
    half = total_ref[pl.ds(spot_of(at, 4), SHARD), :].astype(bf16)
    after_ref[:, :E] = total_ref[pl.ds(spot_of(at, 3), SHARD), :].astype(bf16)
    after_ref[:, E:] = half[:, :LEFT]
    before_ref[:, :E] = total_ref[pl.ds(spot_of(at, 5), SHARD), :].astype(bf16)
    before_ref[:, E:] = half[:, LEFT:]


def chunk_out(total_ref, at, targets, stage_ref, sems):
    copies = []
    slot = 0
    for n, d, cols in (
        (3, 3, None),
        (6, 5, None),
        (4, 4, pl.ds(0, LEFT)),
        (5, 4, pl.ds(LEFT, RIGHT)),
        (1, 1, None),
        (8, 7, None),
        (2, 2, None),
        (7, 6, None),
        (0, 0, None),
    ):
        rows = pl.ds(spot_of(at, d), SHARD)
        if d in (0, 2, 6):
            source = total_ref.at[rows, :]
        else:
            if n != 5:
                stage_ref[slot] = total_ref[rows, :].astype(bf16)
                slot += 1
            source = stage_ref.at[slot - 1] if cols is None else stage_ref.at[slot - 1, :, cols]
        copies.append(pltpu.make_async_copy(source, targets[n], sems.at[n]))
        copies[-1].start()
    return copies


def chunk_store(total_ref, at, targets):
    far_parts(total_ref, at, targets[3], targets[6])
    for n in (0, 1, 2, 4, 5):
        targets[n][...] = total_ref[pl.ds(spot_of(at, PLACES[n]), SHARD), :]


def align_body(at_ref, teacher_hbm, patch_ref, picks_ref, rows_hbm, send_hbm, teacher_ref, rows_ref, own_ref, extra_ref, sems):
    copy = pltpu.make_async_copy(teacher_hbm, teacher_ref, sems.at[GROUPS])
    copy.start()
    for j in range(GROUPS):
        extra_ref[j] = jnp.full(extra_ref.shape[1:], picks_ref[j], jnp.int32).astype(f32).astype(bf16)
    extra = pltpu.make_async_copy(extra_ref, send_hbm.at[:, :, pl.ds(E, E_WIDE - E)], sems.at[GROUPS + 1])
    extra.start()
    copy.wait()
    teacher = teacher_ref[...].astype(f32)
    unit = (teacher * lax.rsqrt(jnp.sum(teacher * teacher, axis=-1, keepdims=True) + eps)).astype(bf16)
    ids = lax.broadcasted_iota(jnp.int32, (teacher.shape[0], ROWS), 0)
    hot = (ids == patch_ref[...] - at_ref[1] * teacher.shape[0]).astype(f32).astype(bf16)
    rows_ref[...] = lax.dot_general(
        hot, unit, (((0,), (0,)), ((), ())), preferred_element_type=f32
    ).astype(bf16)
    copies = [pltpu.make_async_copy(rows_ref, rows_hbm, sems.at[GROUPS])]
    copies[0].start()
    own_ref[...] = rows_ref[pl.ds(spot_of(at_ref[0], 0), SHARD), :]
    for j in range(GROUPS):
        copies.append(pltpu.make_async_copy(own_ref, send_hbm.at[j, :, pl.ds(0, E)], sems.at[j]))
        copies[-1].start()
    copies.append(extra)
    for copy in copies:
        copy.wait()


def align(at, teacher, patch, picks):
    return pl.pallas_call(
        align_body,
        out_shape=[
            pltpu.HBM((ROWS, E), bf16),
            pltpu.HBM((GROUPS, SHARD, E_WIDE), bf16),
        ],
        in_specs=[IN_SMEM] + in_place(1) + in_vmem(1) + [IN_SMEM],
        out_specs=in_place(2),
        scratch_shapes=[
            pltpu.VMEM(teacher.shape, bf16),
            pltpu.VMEM((ROWS, E), bf16),
            pltpu.VMEM((SHARD, E), bf16),
            pltpu.VMEM((GROUPS, SHARD, E_WIDE - E), bf16),
            pltpu.SemaphoreType.DMA((GROUPS + 2,)),
        ],
        compiler_params=scoped(12),
        cost_estimate=pl.CostEstimate(flops=250_000_000, bytes_accessed=4_000_000, transcendentals=0),
        name="align",
    )(at, hbm(teacher), patch, picks)


def forward_body(at_ref, hidden_ref, w_in_ref, w_out_ref, pre_hbm, act_hbm, *refs):
    targets = refs[: NT + 1]
    total_ref, pre_ref, act_ref, sems, stage_ref, stage_sems = refs[NT + 1 :]
    pre = jnp.dot(hidden_ref[...], w_in_ref[...], preferred_element_type=f32)
    pre_ref[...] = pre
    act = (pre / (1.0 + jnp.exp(-pre))).astype(bf16)
    act_ref[...] = act
    copies = [
        pltpu.make_async_copy(pre_ref, pre_hbm, sems.at[0]),
        pltpu.make_async_copy(act_ref, act_hbm, sems.at[1]),
    ]
    for copy in copies:
        copy.start()
    total_ref[...] = jnp.dot(act, w_out_ref[...], preferred_element_type=f32)
    copies += chunk_out(total_ref, at_ref[0], targets, stage_ref, stage_sems)
    for copy in copies:
        copy.wait()


def forward(at, hidden_states, w_in, w_out):
    rows, width = hidden_states.shape[0], w_in.shape[1]
    return pl.pallas_call(
        forward_body,
        out_shape=[pltpu.HBM((rows, width), f32), pltpu.HBM((rows, width), bf16)] + SPLIT,
        in_specs=[IN_SMEM] + in_vmem(3),
        out_specs=in_place(3 + NT),
        scratch_shapes=[
            pltpu.VMEM((rows, E), f32),
            pltpu.VMEM((rows, width), f32),
            pltpu.VMEM((rows, width), bf16),
            pltpu.SemaphoreType.DMA((2,)),
        ]
        + STAGE,
        compiler_params=scoped(16),
        cost_estimate=pl.CostEstimate(flops=900_000_000, bytes_accessed=8_000_000, transcendentals=100_000),
        name="forward",
    )(at, hidden_states, w_in, w_out)


RECEIVED = 4


def normalise_body(local_ref, own_hbm, theirs_hbm, *refs):
    parts, refs = refs[: RECEIVED], refs[RECEIVED :]
    unit_hbm, inv_hbm, row_hbm, send_hbm, unit_ref, inv_ref, row_ref, got_ref, theirs_ref, sems = refs
    first = pltpu.make_async_copy(own_hbm, unit_ref, sems.at[RECEIVED + 1])
    first.start()
    copies = [pltpu.make_async_copy(parts[i], got_ref.at[i], sems.at[i]) for i in range(RECEIVED)]
    picks = pltpu.make_async_copy(
        theirs_hbm.at[:, pl.ds(0, 16), pl.ds(E, E_WIDE - E)], theirs_ref, sems.at[RECEIVED]
    )
    for copy in copies:
        copy.start()
    picks.start()
    first.wait()
    total = unit_ref[...]
    for i in range(RECEIVED):
        copies[i].wait()
        total = total + got_ref[i].astype(f32)
    inv = lax.rsqrt(jnp.sum(total * total, axis=-1, keepdims=True) + eps)
    unit = total * inv
    row_ref[:, :E] = unit.astype(bf16)
    copies = [
        pltpu.make_async_copy(row_ref.at[:, pl.ds(0, E)], send_hbm.at[j], sems.at[RECEIVED + 4 + j]) for j in range(GROUPS)
    ]
    for copy in copies:
        copy.start()
    unit_ref[...] = unit
    inv_ref[...] = jnp.broadcast_to(inv, inv_ref.shape)
    copies.append(pltpu.make_async_copy(unit_ref, unit_hbm, sems.at[RECEIVED + 1]))
    copies[-1].start()
    copies.append(pltpu.make_async_copy(inv_ref, inv_hbm, sems.at[RECEIVED + 2]))
    copies[-1].start()
    shape = (16, E_WIDE - E)
    lane = lax.broadcasted_iota(jnp.int32, shape, 1)
    block = lax.broadcasted_iota(jnp.int32, shape, 0)
    group, end = lane // RB, lane % RB
    picks.wait()
    other = jnp.zeros(shape, f32)
    for j in range(GROUPS):
        other = other + jnp.where(group == j, theirs_ref[j].astype(f32), 0.0)
    as_row = (local_ref[0:1, :] == block) & (local_ref[1:2, :] == end)
    as_key = (local_ref[2:3, :] == block) & (other.astype(jnp.int32) == end)
    counts = as_row.astype(f32) + as_key.astype(f32)
    counts = jnp.where((group < GROUPS) & (block < RB), counts, 0.0)
    row_ref[:, E:] = jnp.concatenate([counts, jnp.zeros((SHARD - 16, E_WIDE - E), f32)], axis=0).astype(bf16)
    copies.append(pltpu.make_async_copy(row_ref, row_hbm, sems.at[RECEIVED + 3]))
    copies[-1].start()
    for copy in copies:
        copy.wait()


def normalise(own, local, theirs, parts):
    return pl.pallas_call(
        normalise_body,
        out_shape=[
            pltpu.HBM((SHARD, E), f32),
            pltpu.HBM((SHARD, BLK), f32),
            pltpu.HBM((SHARD, E_WIDE), bf16),
            pltpu.HBM((GROUPS, SHARD, E), bf16),
        ],
        in_specs=in_vmem(1) + in_place(RECEIVED + 2),
        out_specs=in_place(4),
        scratch_shapes=[
            pltpu.VMEM((SHARD, E), f32),
            pltpu.VMEM((SHARD, BLK), f32),
            pltpu.VMEM((SHARD, E_WIDE), bf16),
            pltpu.VMEM((RECEIVED, SHARD, E), bf16),
            pltpu.VMEM((GROUPS, 16, E_WIDE - E), bf16),
            pltpu.SemaphoreType.DMA((RECEIVED + 4 + GROUPS,)),
        ],
        compiler_params=scoped(12),
        cost_estimate=pl.CostEstimate(flops=1_000_000, bytes_accessed=4_000_000, transcendentals=0),
        name="normalise",
    )(local, hbm(own), theirs, *[hbm(part) for part in parts])


def gather_in(at, pieces, target_ref, wide, sems):
    copies = []

    def bring(source, d, start, size):
        rows = pl.ds(spot_of(at, d), SHARD)
        copies.append(pltpu.make_async_copy(source, target_ref.at[rows, pl.ds(start, size)], sems.at[len(copies)]))
        copies[-1].start()

    for n in range(PARTS):
        source = pieces[n]
        if n in (3, 6):
            start, size = (LEFT, wide - LEFT) if n == 3 else (0, LEFT)
            bring(source.at[:, pl.ds(wide, size)], 4, start, size)
            source = source.at[:, pl.ds(0, wide)]
        bring(source, PLACES[n], 0, wide)
    return copies


def gram_body(at_ref, *refs):
    pieces, refs = dict(zip(PIECE_ORDER, refs[:PARTS])), refs[PARTS:]
    keys_hbm, teacher_hbm, spread_ref = refs[:3]
    refs = refs[3:]
    targets = refs[:PARTS]
    row_ref, key_ref, teacher_ref, grad_ref, total_ref, sems = refs[PARTS:]
    contract = (((1,), (1,)), ((), ()))
    step = 256
    spans = [pl.ds(k, step) for k in range(0, GROUPS * SHARD, step)]
    row_copies = gather_in(at_ref[0], pieces, row_ref, E_WIDE, sems)
    copies = []
    for i, span in enumerate(spans):
        pair = (
            pltpu.make_async_copy(keys_hbm.at[span, :], key_ref.at[span, :], sems.at[PARTS + 2 + 2 * i]),
            pltpu.make_async_copy(teacher_hbm.at[:, span], teacher_ref.at[:, span], sems.at[PARTS + 3 + 2 * i]),
        )
        pair[0].start()
        pair[1].start()
        copies.append(pair)
    for copy in row_copies:
        copy.wait()
    counts = jnp.zeros((16, E_WIDE - E), f32)
    for d in range(NT):
        counts = counts + row_ref[pl.ds(d * SHARD, 16), E:].astype(f32)
    tile = jnp.dot(counts.astype(bf16), spread_ref[...], preferred_element_type=f32) * (E / 8.0)
    for i, span in enumerate(spans):
        copies[i][0].wait()
        copies[i][1].wait()
        diff = (
            lax.dot_general(row_ref[:, :E], key_ref[span, :], contract, preferred_element_type=f32)
            - teacher_ref[:, span]
        )
        for a in range(RB):
            grad_ref[pl.ds(a * BLK, BLK), span] = (
                diff[a * BLK : (a + 1) * BLK] * tile[a : a + 1, i * step : (i + 1) * step]
            ).astype(bf16)
    for c, wide in ((0, 768), (768, 640)):
        total_ref[:, pl.ds(c, wide)] = jnp.dot(
            grad_ref[...], key_ref[:, pl.ds(c, wide)], preferred_element_type=f32
        )
    chunk_store(total_ref, at_ref[0], targets)


def gram_grads(at, pieces, keys, gram_teacher, spread):
    steps = GROUPS * SHARD // 256
    return pl.pallas_call(
        gram_body,
        out_shape=[jax.ShapeDtypeStruct(chunk.shape, chunk.dtype) for chunk in CHUNKS],
        in_specs=[IN_SMEM] + in_place(PARTS + 2) + in_vmem(1),
        out_specs=in_vmem(PARTS),
        scratch_shapes=[
            pltpu.VMEM((ROWS, E_WIDE), bf16),
            pltpu.VMEM((GROUPS * SHARD, E), bf16),
            pltpu.VMEM((ROWS, GROUPS * SHARD), f32),
            pltpu.VMEM((ROWS, GROUPS * SHARD), bf16),
            pltpu.VMEM((ROWS, E), f32),
            pltpu.SemaphoreType.DMA((PARTS + 2 + 2 * steps,)),
        ],
        compiler_params=scoped(20),
        cost_estimate=pl.CostEstimate(flops=1_700_000_000, bytes_accessed=9_000_000, transcendentals=0),
        name="gram_grads",
    )(at, *[hbm(pieces[n]) for n in PIECE_ORDER], keys, hbm(gram_teacher), spread)


def backward_body(at_ref, *refs):
    pieces, refs = dict(zip(PIECE_ORDER, refs[:PARTS])), refs[PARTS:]
    hidden_ref, w_out_ref, pre_ref, act_ref = refs[:4]
    keep_hbm, give_hbm, grad_pre_hbm, keep_ref, give_ref, grad_pre_ref, proj_ref, sems = refs[4:]
    at, tea = at_ref[0], at_ref[1]
    contract = (((1,), (1,)), ((), ()))
    over_rows = (((0,), (0,)), ((), ()))
    copies = gather_in(at, pieces, proj_ref, E, sems)
    proj_ref[:, E:] = jnp.zeros((ROWS, E_PAD - E), bf16)
    pre = pre_ref[...]
    sigma = 1.0 / (1.0 + jnp.exp(-pre))
    slope = sigma * (1.0 + pre * (1.0 - sigma))
    for copy in copies:
        copy.wait()
    grad_act = lax.dot_general(proj_ref[:, :E], w_out_ref[...], contract, preferred_element_type=f32)
    grad_pre = (grad_act * slope).astype(bf16)
    grad_pre_ref[...] = grad_pre
    copies = [pltpu.make_async_copy(grad_pre_ref, grad_pre_hbm, sems.at[0])]
    copies[0].start()
    d_half, e_half = hidden_ref.shape[1] // 2, E_PAD // 2
    in_rows, out_rows = d_half // GROUPS, e_half // GROUPS
    for n, (ref, target, side) in enumerate(((keep_ref, keep_hbm, tea), (give_ref, give_hbm, 1 - tea))):
        part = hidden_ref[:, pl.ds(pl.multiple_of(side * d_half, d_half), d_half)]
        grad = lax.dot_general(part, grad_pre, over_rows, preferred_element_type=f32)
        for c in range(GROUPS):
            ref[c, pl.ds(0, in_rows), :] = grad[c * in_rows : (c + 1) * in_rows].astype(ref.dtype)
        part = proj_ref[:, pl.ds(pl.multiple_of(side * e_half, e_half), e_half)]
        grad = lax.dot_general(part, act_ref[...], over_rows, preferred_element_type=f32)
        for c in range(GROUPS):
            ref[c, pl.ds(in_rows, out_rows), :] = grad[c * out_rows : (c + 1) * out_rows].astype(ref.dtype)
        copies.append(pltpu.make_async_copy(ref, target, sems.at[n + 1]))
        copies[-1].start()
    for copy in copies:
        copy.wait()


def backward(where, pieces, hidden_states, w_out, pre_act, activation):
    rows, d_model = hidden_states.shape
    width = activation.shape[1]
    halves = (GROUPS, (d_model + E_PAD) // 2 // GROUPS, width)
    return pl.pallas_call(
        backward_body,
        out_shape=[
            pltpu.HBM(halves, bf16),
            pltpu.HBM(halves, bf16),
            pltpu.HBM((rows, width), bf16),
        ],
        in_specs=[IN_SMEM] + in_place(PARTS) + in_vmem(4),
        out_specs=in_place(3),
        scratch_shapes=[
            pltpu.VMEM(halves, bf16),
            pltpu.VMEM(halves, bf16),
            pltpu.VMEM((rows, width), bf16),
            pltpu.VMEM((ROWS, E_PAD), bf16),
            pltpu.SemaphoreType.DMA((PARTS + 2,)),
        ],
        compiler_params=scoped(14),
        cost_estimate=pl.CostEstimate(flops=1_200_000_000, bytes_accessed=9_000_000, transcendentals=100_000),
        name="backward",
    )(where, *[pieces[d] for d in PIECE_ORDER], hidden_states, w_out, pre_act, activation)


def hidden_body(grad_pre_hbm, w_in_ref, terms_hbm, grad_pre_ref, terms_ref, sems):
    first = pltpu.make_async_copy(grad_pre_hbm, grad_pre_ref, sems.at[NT])
    first.start()
    contract = (((1,), (1,)), ((), ()))
    share = w_in_ref.shape[0] // NT
    copies = []
    first.wait()
    for d in range(NT):
        span = pl.ds(d * ROWS, ROWS)
        terms_ref[span, :] = lax.dot_general(
            grad_pre_ref[...], w_in_ref[pl.ds(d * share, share), :], contract, preferred_element_type=f32
        ).astype(bf16)
        copies.append(pltpu.make_async_copy(terms_ref.at[span, :], terms_hbm.at[span, :], sems.at[d]))
        copies[-1].start()
    for copy in copies:
        copy.wait()


def hidden_grads(grad_pre, w_in):
    shape = (NT * ROWS, w_in.shape[0] // NT)
    return pl.pallas_call(
        hidden_body,
        out_shape=pltpu.HBM(shape, bf16),
        in_specs=in_place(1) + in_vmem(1),
        out_specs=in_place(1)[0],
        scratch_shapes=[
            pltpu.VMEM(grad_pre.shape, bf16),
            pltpu.VMEM(shape, bf16),
            pltpu.SemaphoreType.DMA((NT + 1,)),
        ],
        compiler_params=scoped(6),
        cost_estimate=pl.CostEstimate(flops=600_000_000, bytes_accessed=4_000_000, transcendentals=0),
        name="hidden_grads",
    )(hbm(grad_pre), w_in)


def pair_body(keep_ref, got_ref, sum_ref):
    sum_ref[...] = (keep_ref[...].astype(f32) + got_ref[...].astype(f32)).astype(bf16)


def pair_sum(keep, got):
    return pl.pallas_call(
        pair_body,
        out_shape=jax.ShapeDtypeStruct(keep.shape, bf16),
        in_specs=in_vmem(2),
        out_specs=in_vmem(1)[0],
        compiler_params=scoped(8),
        cost_estimate=pl.CostEstimate(flops=600_000, bytes_accessed=5_000_000, transcendentals=0),
        name="pair_sum",
    )(keep, got)


def half_out(ref, side, w_in_hbm, w_out_hbm, w_in_ref, w_out_ref, flat_ref, sems):
    d_half, e_half = w_in_ref.shape[0], E_PAD // 2
    in_rows, out_rows = d_half // GROUPS, e_half // GROUPS
    for c in range(GROUPS):
        w_in_ref[pl.ds(c * in_rows, in_rows), :] = ref[c, pl.ds(0, in_rows), :].astype(f32)
    copy = pltpu.make_async_copy(
        w_in_ref, w_in_hbm.at[pl.ds(pl.multiple_of(side * d_half, d_half), d_half), :], sems.at[0]
    )
    copy.start()
    for c in range(GROUPS):
        flat_ref[pl.ds(c * out_rows, out_rows), :] = ref[c, pl.ds(in_rows, out_rows), :].astype(f32)
    for c in range(0, e_half, BLK):
        w_out_ref[:, pl.ds(c, BLK)] = flat_ref[pl.ds(c, BLK), :].T
    for which, start, size in ((0, 0, e_half), (1, e_half, E - e_half)):

        @pl.when(side == which)
        def _():
            part = pltpu.make_async_copy(
                w_out_ref.at[:, pl.ds(0, size)], w_out_hbm.at[:, pl.ds(start, size)], sems.at[1]
            )
            part.start()
            part.wait()

    copy.wait()


def first_body(tea_ref, mine_ref, sum_hbm, w_in_hbm, w_out_hbm, hidden_ref, w_in_ref, w_out_ref, flat_ref, sum_ref, sems):
    copy = pltpu.make_async_copy(sum_hbm, sum_ref, sems.at[2])
    copy.start()
    half_out(mine_ref, tea_ref[0], w_in_hbm, w_out_hbm, w_in_ref, w_out_ref, flat_ref, sems)
    copy.wait()
    hidden_ref[...] = sum_ref[...].astype(f32)


def second_body(tea_ref, other_ref, w_in_old, w_out_old, w_in_hbm, w_out_hbm, w_in_ref, w_out_ref, flat_ref, sems):
    half_out(other_ref, 1 - tea_ref[0], w_in_hbm, w_out_hbm, w_in_ref, w_out_ref, flat_ref, sems)


def half_scratch(d_model, width):
    return [
        pltpu.VMEM((d_model // 2, width), f32),
        pltpu.VMEM((width, E_PAD // 2), f32),
        pltpu.VMEM((E_PAD // 2, width), f32),
    ]


def first_half(tea, mine, hidden, d_model):
    width = mine.shape[-1]
    return pl.pallas_call(
        first_body,
        out_shape=[
            pltpu.HBM((d_model, width), f32),
            pltpu.HBM((width, E), f32),
            jax.ShapeDtypeStruct(hidden.shape, f32),
        ],
        in_specs=[IN_SMEM] + in_vmem(1) + in_place(1),
        out_specs=in_place(2) + in_vmem(1),
        scratch_shapes=half_scratch(d_model, width)
        + [pltpu.VMEM(hidden.shape, bf16), pltpu.SemaphoreType.DMA((3,))],
        compiler_params=scoped(12),
        cost_estimate=pl.CostEstimate(flops=0, bytes_accessed=5_000_000, transcendentals=0),
        name="first_half",
    )(tea, mine, hbm(hidden))


def second_half(tea, other, w_in, w_out):
    return pl.pallas_call(
        second_body,
        out_shape=[pltpu.HBM(w_in.shape, f32), pltpu.HBM(w_out.shape, f32)],
        in_specs=[IN_SMEM] + in_vmem(1) + in_place(2),
        out_specs=in_place(2),
        scratch_shapes=half_scratch(w_in.shape[0], w_in.shape[1]) + [pltpu.SemaphoreType.DMA((2,))],
        input_output_aliases={2: 0, 3: 1},
        compiler_params=scoped(12),
        cost_estimate=pl.CostEstimate(flops=0, bytes_accessed=4_000_000, transcendentals=0),
        name="second_half",
    )(tea, other, hbm(w_in), hbm(w_out))


def on_device(hidden_states, w_in, w_out, teacher, patch_map, row_pick, key_pick):
    seq_index = lax.axis_index("seq")
    tp_index = lax.axis_index("tp")
    tea_index = lax.axis_index("tea")
    at = jnp.full((1,), tp_index, jnp.int32)
    tea = jnp.full((1,), tea_index, jnp.int32)
    contract = (((1,), (1,)), ((), ()))

    picks = row_pick.reshape(GROUPS)
    group = jnp.full((1,), lax.axis_index(("seq", "tea")), jnp.int32)
    row_teacher, teacher_send = align(jnp.concatenate([at, group]), teacher, patch_map.reshape(1, ROWS), picks)
    teacher_send, at_next = lax.optimization_barrier((teacher_send, at))
    teacher_got = lax.all_to_all(teacher_send, "seq", 0, 0, tiled=True)

    pre_act, activation, *chunks = forward(at_next, hidden_states, w_in, w_out)
    activation, key_pick, picks = lax.optimization_barrier((activation, key_pick, picks))
    received = sum_split(*chunks)

    table = key_pick.reshape(GROUPS, GROUPS)
    of_rows = lax.dynamic_index_in_dim(table, seq_index, axis=0, keepdims=False)
    of_keys = lax.dynamic_index_in_dim(table, seq_index, axis=1, keepdims=False)
    local = jnp.repeat(jnp.stack([picks, of_rows, of_keys]), RB, axis=1)
    local = jnp.pad(local, ((0, 8 - 3), (0, E_WIDE - E - GROUPS * RB)))
    key_ids = jnp.arange(GROUPS * SHARD, dtype=jnp.int32)
    key_cell = key_ids // SHARD * RB + (tp_index * SHARD + key_ids % SHARD) // BLK
    spread = (jnp.arange(E_WIDE - E, dtype=jnp.int32)[:, None] == key_cell[None, :]).astype(bf16)

    *received, teacher_got = lax.optimization_barrier((*received, teacher_got))
    unit_student, inv_norm, row_send, key_send = normalise(chunks[0], local, teacher_got, received)
    rows = gather_ring(row_send)
    keys = lax.all_to_all(key_send, "seq", 0, 0, tiled=True).reshape(GROUPS * SHARD, E)
    teacher_got, inv_norm = lax.optimization_barrier((teacher_got, inv_norm))
    inv_norm = inv_norm[:, :1]
    key_teacher = teacher_got[:, :, :E].reshape(GROUPS * SHARD, E)
    gram_teacher = lax.dot_general(row_teacher, key_teacher, contract, preferred_element_type=f32)

    row_grad = gram_grads(at, rows, keys, gram_teacher, spread)
    unit_grad = row_grad[0]
    for piece in sum_ring(*row_grad):
        unit_grad = unit_grad + piece.astype(f32)
    inner = jnp.sum(unit_student * unit_grad, axis=-1, keepdims=True)
    grad_proj = ((unit_grad - unit_student * inner) * inv_norm).astype(bf16)
    pieces = gather_ring(grad_proj)

    where = jnp.concatenate([at, tea])
    keep, give, grad_pre = backward(where, pieces, hidden_states, w_out, pre_act, activation)
    got = swap_tea(give)
    hidden_terms = hidden_grads(grad_pre, w_in)
    chip, hidden_terms = lax.optimization_barrier((pair_sum(keep, got), hidden_terms))
    hidden_sum = lax.psum_scatter(hidden_terms, "tp", scatter_dimension=0, tiled=True)
    chip = lax.all_to_all(chip, "seq", 0, 0, tiled=True)
    mine = to_all(jnp.sum(chip.astype(f32), axis=0).astype(bf16)).reshape(keep.shape)
    other = swap_tea(mine)
    grad_w_in, grad_w_out, grad_hidden = first_half(tea, mine, hidden_sum, hidden_states.shape[1])
    grad_w_in, grad_w_out = second_half(tea, other, grad_w_in, grad_w_out)
    return (grad_hidden, grad_w_in, grad_w_out)


def solution(mesh):
    return jax.shard_map(
        on_device,
        mesh=mesh,
        in_specs=(
            P(("seq", "tea"), None),
            P(None, "tp"),
            P("tp", None),
            P(("seq", "tea"), None),
            P(("seq", "tea")),
            P("seq", "tp", "tea", None),
            P(None, "tp", "tea", None),
        ),
        out_specs=(P(("seq", "tea"), "tp"), P(None, "tp"), P("tp", None)),
        check_vma=False,
    )
```

```python
import jax
import jax.numpy as jnp
from jax import lax
from jax.experimental import pallas as pl
from jax.experimental.pallas import tpu as pltpu
from jax.sharding import PartitionSpec as P

E = 1408
BLK = 128
RB = 3
SIDE = 4
NT = 8
GROUPS = SIDE * SIDE
SHARD = 48
ROWS = 384
E_WIDE = 1536
E_PAD = 1536

eps = 1e-06
bf16 = jnp.bfloat16
f32 = jnp.float32


def shift_tp(x, step):
    return lax.ppermute(x, "tp", [(i, (i + step) % NT) for i in range(NT)])


def swap_tea(x):
    return lax.ppermute(x, "tea", [(0, 1), (1, 0)])


LEFT = 768
RIGHT = 640


def gather_ring(x):
    before, after = shift_tp(x, 1), shift_tp(x, -1)
    before2, after2 = shift_tp(x, 2), shift_tp(x, -2)
    far_after = shift_tp(jnp.concatenate([after, after2[:, LEFT:]], axis=1), -2)
    far_before = shift_tp(jnp.concatenate([before, before2[:, :LEFT]], axis=1), 2)
    return [x, after, after2, far_after, before2, before, far_before]


def sum_ring(own, one, two, far_after, six, seven, far_before):
    far_after, far_before = shift_tp(far_after, 2).astype(f32), shift_tp(far_before, -2).astype(f32)
    one, seven = one + far_after[:, :E], seven + far_before[:, :E]
    two = two + jnp.concatenate([far_after[:, E:], jnp.zeros((SHARD, RIGHT), f32)], axis=1)
    six = six + jnp.concatenate([jnp.zeros((SHARD, LEFT), f32), far_before[:, E:]], axis=1)
    one, two, six, seven = (v.astype(bf16) for v in (one, two, six, seven))
    return [shift_tp(two, 2), shift_tp(six, -2), shift_tp(one, 1), shift_tp(seven, -1)]


def gather_split(x):
    before, after = shift_tp(x, 1), shift_tp(x, -1)
    before2, after2 = shift_tp(x, 2), shift_tp(x, -2)
    before3, after3 = shift_tp(before2, 1), shift_tp(after2, -1)
    left, right = shift_tp(before2[:, :LEFT], 2), shift_tp(after2[:, LEFT:], -2)
    return [x, after, after2, after3, left, right, before3, before2, before]


def pass_split(own, one, two, three, left, right, five, six, seven):
    three, five = shift_tp(three, 1), shift_tp(five, -1)
    left, right = shift_tp(left, 2), shift_tp(right, -2)
    one, seven = shift_tp(one, 1), shift_tp(seven, -1)
    blank = jnp.zeros(left.shape, f32), jnp.zeros(right.shape, f32)
    two = two + three.astype(f32) + jnp.concatenate([left.astype(f32), blank[1]], axis=1)
    six = six + five.astype(f32) + jnp.concatenate([blank[0], right.astype(f32)], axis=1)
    return one, seven, two.astype(bf16), six.astype(bf16)


def sum_split(*terms):
    one, seven, two, six = pass_split(*terms)
    return [one, seven, shift_tp(two, 2), shift_tp(six, -2)]


def to_all(x):
    return lax.all_to_all(jnp.broadcast_to(x[None], (GROUPS,) + x.shape), "seq", 0, 0, tiled=True)


def in_vmem(count):
    return [pl.BlockSpec(memory_space=pltpu.VMEM)] * count


def in_place(count):
    return [pl.BlockSpec(memory_space=pltpu.HBM)] * count


def hbm(x):
    return pltpu.with_memory_space_constraint(x, pltpu.HBM)


IN_SMEM = pl.BlockSpec(memory_space=pltpu.SMEM)
def scoped(mib):
    return pltpu.CompilerParams(vmem_limit_bytes=mib * 1024 * 1024)


PIECE_ORDER = (0, 1, 5, 2, 4, 3, 6)


def spot_of(at, d):
    return pl.multiple_of(lax.rem(at + d, NT) * SHARD, SHARD)


PARTS = 7
PLACES = (0, 1, 2, 3, 6, 7, 5)
STAGE = [pltpu.VMEM((5, SHARD, E), bf16), pltpu.SemaphoreType.DMA((NT + 1,))]
WIDE, FULL = pltpu.HBM((SHARD, E), f32), pltpu.HBM((SHARD, E), bf16)
SPLIT = [WIDE, FULL, WIDE, FULL, pltpu.HBM((SHARD, LEFT), bf16), pltpu.HBM((SHARD, RIGHT), bf16), FULL, WIDE, FULL]
CHUNKS = [
    WIDE,
    WIDE,
    WIDE,
    pltpu.HBM((SHARD, E + LEFT), bf16),
    WIDE,
    WIDE,
    pltpu.HBM((SHARD, E + RIGHT), bf16),
]


def far_parts(total_ref, at, after_ref, before_ref):
    half = total_ref[pl.ds(spot_of(at, 4), SHARD), :].astype(bf16)
    after_ref[:, :E] = total_ref[pl.ds(spot_of(at, 3), SHARD), :].astype(bf16)
    after_ref[:, E:] = half[:, :LEFT]
    before_ref[:, :E] = total_ref[pl.ds(spot_of(at, 5), SHARD), :].astype(bf16)
    before_ref[:, E:] = half[:, LEFT:]


def chunk_out(total_ref, at, targets, stage_ref, sems):
    copies = []
    slot = 0
    for n, d, cols in (
        (3, 3, None),
        (6, 5, None),
        (4, 4, pl.ds(0, LEFT)),
        (5, 4, pl.ds(LEFT, RIGHT)),
        (1, 1, None),
        (8, 7, None),
        (2, 2, None),
        (7, 6, None),
        (0, 0, None),
    ):
        rows = pl.ds(spot_of(at, d), SHARD)
        if d in (0, 2, 6):
            source = total_ref.at[rows, :]
        else:
            if n != 5:
                stage_ref[slot] = total_ref[rows, :].astype(bf16)
                slot += 1
            source = stage_ref.at[slot - 1] if cols is None else stage_ref.at[slot - 1, :, cols]
        copies.append(pltpu.make_async_copy(source, targets[n], sems.at[n]))
        copies[-1].start()
    return copies


def chunk_store(total_ref, at, targets):
    far_parts(total_ref, at, targets[3], targets[6])
    for n in (0, 1, 2, 4, 5):
        targets[n][...] = total_ref[pl.ds(spot_of(at, PLACES[n]), SHARD), :]


def align_body(at_ref, teacher_hbm, patch_ref, picks_ref, rows_hbm, send_hbm, teacher_ref, rows_ref, own_ref, extra_ref, sems):
    copy = pltpu.make_async_copy(teacher_hbm, teacher_ref, sems.at[GROUPS])
    copy.start()
    for j in range(GROUPS):
        extra_ref[j] = jnp.full(extra_ref.shape[1:], picks_ref[j], jnp.int32).astype(f32).astype(bf16)
    extra = pltpu.make_async_copy(extra_ref, send_hbm.at[:, :, pl.ds(E, E_WIDE - E)], sems.at[GROUPS + 1])
    extra.start()
    copy.wait()
    teacher = teacher_ref[...].astype(f32)
    unit = (teacher * lax.rsqrt(jnp.sum(teacher * teacher, axis=-1, keepdims=True) + eps)).astype(bf16)
    ids = lax.broadcasted_iota(jnp.int32, (teacher.shape[0], ROWS), 0)
    hot = (ids == patch_ref[...] - at_ref[1] * teacher.shape[0]).astype(f32).astype(bf16)
    rows_ref[...] = lax.dot_general(
        hot, unit, (((0,), (0,)), ((), ())), preferred_element_type=f32
    ).astype(bf16)
    copies = [pltpu.make_async_copy(rows_ref, rows_hbm, sems.at[GROUPS])]
    copies[0].start()
    own_ref[...] = rows_ref[pl.ds(spot_of(at_ref[0], 0), SHARD), :]
    for j in range(GROUPS):
        copies.append(pltpu.make_async_copy(own_ref, send_hbm.at[j, :, pl.ds(0, E)], sems.at[j]))
        copies[-1].start()
    copies.append(extra)
    for copy in copies:
        copy.wait()


def align(at, teacher, patch, picks):
    return pl.pallas_call(
        align_body,
        out_shape=[
            pltpu.HBM((ROWS, E), bf16),
            pltpu.HBM((GROUPS, SHARD, E_WIDE), bf16),
        ],
        in_specs=[IN_SMEM] + in_place(1) + in_vmem(1) + [IN_SMEM],
        out_specs=in_place(2),
        scratch_shapes=[
            pltpu.VMEM(teacher.shape, bf16),
            pltpu.VMEM((ROWS, E), bf16),
            pltpu.VMEM((SHARD, E), bf16),
            pltpu.VMEM((GROUPS, SHARD, E_WIDE - E), bf16),
            pltpu.SemaphoreType.DMA((GROUPS + 2,)),
        ],
        compiler_params=scoped(12),
        cost_estimate=pl.CostEstimate(flops=250_000_000, bytes_accessed=4_000_000, transcendentals=0),
        name="align",
    )(at, hbm(teacher), patch, picks)


def forward_body(at_ref, hidden_ref, w_in_ref, w_out_ref, pre_hbm, act_hbm, *refs):
    targets = refs[: NT + 1]
    total_ref, pre_ref, act_ref, sems, stage_ref, stage_sems = refs[NT + 1 :]
    pre = jnp.dot(hidden_ref[...], w_in_ref[...], preferred_element_type=f32)
    pre_ref[...] = pre
    act = (pre / (1.0 + jnp.exp(-pre))).astype(bf16)
    act_ref[...] = act
    copies = [
        pltpu.make_async_copy(pre_ref, pre_hbm, sems.at[0]),
        pltpu.make_async_copy(act_ref, act_hbm, sems.at[1]),
    ]
    for copy in copies:
        copy.start()
    total_ref[...] = jnp.dot(act, w_out_ref[...], preferred_element_type=f32)
    copies += chunk_out(total_ref, at_ref[0], targets, stage_ref, stage_sems)
    for copy in copies:
        copy.wait()


def forward(at, hidden_states, w_in, w_out):
    rows, width = hidden_states.shape[0], w_in.shape[1]
    return pl.pallas_call(
        forward_body,
        out_shape=[pltpu.HBM((rows, width), f32), pltpu.HBM((rows, width), bf16)] + SPLIT,
        in_specs=[IN_SMEM] + in_vmem(3),
        out_specs=in_place(3 + NT),
        scratch_shapes=[
            pltpu.VMEM((rows, E), f32),
            pltpu.VMEM((rows, width), f32),
            pltpu.VMEM((rows, width), bf16),
            pltpu.SemaphoreType.DMA((2,)),
        ]
        + STAGE,
        compiler_params=scoped(16),
        cost_estimate=pl.CostEstimate(flops=900_000_000, bytes_accessed=8_000_000, transcendentals=100_000),
        name="forward",
    )(at, hidden_states, w_in, w_out)


RECEIVED = 4


def normalise_body(local_ref, own_hbm, theirs_hbm, *refs):
    parts, refs = refs[: RECEIVED], refs[RECEIVED :]
    unit_hbm, inv_hbm, row_hbm, send_hbm, unit_ref, inv_ref, row_ref, got_ref, theirs_ref, sems = refs
    first = pltpu.make_async_copy(own_hbm, unit_ref, sems.at[RECEIVED + 1])
    first.start()
    copies = [pltpu.make_async_copy(parts[i], got_ref.at[i], sems.at[i]) for i in range(RECEIVED)]
    picks = pltpu.make_async_copy(
        theirs_hbm.at[:, pl.ds(0, 16), pl.ds(E, E_WIDE - E)], theirs_ref, sems.at[RECEIVED]
    )
    for copy in copies:
        copy.start()
    picks.start()
    first.wait()
    total = unit_ref[...]
    for i in range(RECEIVED):
        copies[i].wait()
        total = total + got_ref[i].astype(f32)
    inv = lax.rsqrt(jnp.sum(total * total, axis=-1, keepdims=True) + eps)
    unit = total * inv
    row_ref[:, :E] = unit.astype(bf16)
    copies = [
        pltpu.make_async_copy(row_ref.at[:, pl.ds(0, E)], send_hbm.at[j], sems.at[RECEIVED + 4 + j]) for j in range(GROUPS)
    ]
    for copy in copies:
        copy.start()
    unit_ref[...] = unit
    inv_ref[...] = jnp.broadcast_to(inv, inv_ref.shape)
    copies.append(pltpu.make_async_copy(unit_ref, unit_hbm, sems.at[RECEIVED + 1]))
    copies[-1].start()
    copies.append(pltpu.make_async_copy(inv_ref, inv_hbm, sems.at[RECEIVED + 2]))
    copies[-1].start()
    shape = (16, E_WIDE - E)
    lane = lax.broadcasted_iota(jnp.int32, shape, 1)
    block = lax.broadcasted_iota(jnp.int32, shape, 0)
    group, end = lane // RB, lane % RB
    picks.wait()
    other = jnp.zeros(shape, f32)
    for j in range(GROUPS):
        other = other + jnp.where(group == j, theirs_ref[j].astype(f32), 0.0)
    as_row = (local_ref[0:1, :] == block) & (local_ref[1:2, :] == end)
    as_key = (local_ref[2:3, :] == block) & (other.astype(jnp.int32) == end)
    counts = as_row.astype(f32) + as_key.astype(f32)
    counts = jnp.where((group < GROUPS) & (block < RB), counts, 0.0)
    row_ref[:, E:] = jnp.concatenate([counts, jnp.zeros((SHARD - 16, E_WIDE - E), f32)], axis=0).astype(bf16)
    copies.append(pltpu.make_async_copy(row_ref, row_hbm, sems.at[RECEIVED + 3]))
    copies[-1].start()
    for copy in copies:
        copy.wait()


def normalise(own, local, theirs, parts):
    return pl.pallas_call(
        normalise_body,
        out_shape=[
            pltpu.HBM((SHARD, E), f32),
            pltpu.HBM((SHARD, BLK), f32),
            pltpu.HBM((SHARD, E_WIDE), bf16),
            pltpu.HBM((GROUPS, SHARD, E), bf16),
        ],
        in_specs=in_vmem(1) + in_place(RECEIVED + 2),
        out_specs=in_place(4),
        scratch_shapes=[
            pltpu.VMEM((SHARD, E), f32),
            pltpu.VMEM((SHARD, BLK), f32),
            pltpu.VMEM((SHARD, E_WIDE), bf16),
            pltpu.VMEM((RECEIVED, SHARD, E), bf16),
            pltpu.VMEM((GROUPS, 16, E_WIDE - E), bf16),
            pltpu.SemaphoreType.DMA((RECEIVED + 4 + GROUPS,)),
        ],
        compiler_params=scoped(12),
        cost_estimate=pl.CostEstimate(flops=1_000_000, bytes_accessed=4_000_000, transcendentals=0),
        name="normalise",
    )(local, hbm(own), theirs, *[hbm(part) for part in parts])


def gather_in(at, pieces, target_ref, wide, sems):
    copies = []

    def bring(source, d, start, size):
        rows = pl.ds(spot_of(at, d), SHARD)
        copies.append(pltpu.make_async_copy(source, target_ref.at[rows, pl.ds(start, size)], sems.at[len(copies)]))
        copies[-1].start()

    for n in range(PARTS):
        source = pieces[n]
        if n in (3, 6):
            start, size = (LEFT, wide - LEFT) if n == 3 else (0, LEFT)
            bring(source.at[:, pl.ds(wide, size)], 4, start, size)
            source = source.at[:, pl.ds(0, wide)]
        bring(source, PLACES[n], 0, wide)
    return copies


def gram_body(at_ref, *refs):
    pieces, refs = dict(zip(PIECE_ORDER, refs[:PARTS])), refs[PARTS:]
    keys_hbm, teacher_hbm, spread_ref = refs[:3]
    refs = refs[3:]
    targets = refs[:PARTS]
    row_ref, key_ref, teacher_ref, grad_ref, total_ref, sems = refs[PARTS:]
    contract = (((1,), (1,)), ((), ()))
    step = 256
    spans = [pl.ds(k, step) for k in range(0, GROUPS * SHARD, step)]
    row_copies = gather_in(at_ref[0], pieces, row_ref, E_WIDE, sems)
    copies = []
    for i, span in enumerate(spans):
        pair = (
            pltpu.make_async_copy(keys_hbm.at[span, :], key_ref.at[span, :], sems.at[PARTS + 2 + 2 * i]),
            pltpu.make_async_copy(teacher_hbm.at[:, span], teacher_ref.at[:, span], sems.at[PARTS + 3 + 2 * i]),
        )
        pair[0].start()
        pair[1].start()
        copies.append(pair)
    for copy in row_copies:
        copy.wait()
    counts = jnp.zeros((16, E_WIDE - E), f32)
    for d in range(NT):
        counts = counts + row_ref[pl.ds(d * SHARD, 16), E:].astype(f32)
    tile = jnp.dot(counts.astype(bf16), spread_ref[...], preferred_element_type=f32) * (E / 8.0)
    for i, span in enumerate(spans):
        copies[i][0].wait()
        copies[i][1].wait()
        diff = (
            lax.dot_general(row_ref[:, :E], key_ref[span, :], contract, preferred_element_type=f32)
            - teacher_ref[:, span]
        )
        for a in range(RB):
            grad_ref[pl.ds(a * BLK, BLK), span] = (
                diff[a * BLK : (a + 1) * BLK] * tile[a : a + 1, i * step : (i + 1) * step]
            ).astype(bf16)
    for c, wide in ((0, 768), (768, 640)):
        total_ref[:, pl.ds(c, wide)] = jnp.dot(
            grad_ref[...], key_ref[:, pl.ds(c, wide)], preferred_element_type=f32
        )
    chunk_store(total_ref, at_ref[0], targets)


def gram_grads(at, pieces, keys, gram_teacher, spread):
    steps = GROUPS * SHARD // 256
    return pl.pallas_call(
        gram_body,
        out_shape=[jax.ShapeDtypeStruct(chunk.shape, chunk.dtype) for chunk in CHUNKS],
        in_specs=[IN_SMEM] + in_place(PARTS + 2) + in_vmem(1),
        out_specs=in_vmem(PARTS),
        scratch_shapes=[
            pltpu.VMEM((ROWS, E_WIDE), bf16),
            pltpu.VMEM((GROUPS * SHARD, E), bf16),
            pltpu.VMEM((ROWS, GROUPS * SHARD), f32),
            pltpu.VMEM((ROWS, GROUPS * SHARD), bf16),
            pltpu.VMEM((ROWS, E), f32),
            pltpu.SemaphoreType.DMA((PARTS + 2 + 2 * steps,)),
        ],
        compiler_params=scoped(20),
        cost_estimate=pl.CostEstimate(flops=1_700_000_000, bytes_accessed=9_000_000, transcendentals=0),
        name="gram_grads",
    )(at, *[hbm(pieces[n]) for n in PIECE_ORDER], keys, hbm(gram_teacher), spread)


def split_in(at, pieces, target_ref, wide, sems):
    copies = []
    for n in range(NT + 1):
        d = n if n <= 4 else n - 1
        cols = {4: pl.ds(0, LEFT), 5: pl.ds(LEFT, wide - LEFT)}.get(n, pl.ds(0, wide))
        rows = pl.ds(spot_of(at, d), SHARD)
        copies.append(pltpu.make_async_copy(pieces[n], target_ref.at[rows, cols], sems.at[n]))
        copies[-1].start()
    return copies


SPLIT_ORDER = (0, 1, 8, 2, 7, 3, 6, 4, 5)


def backward_body(at_ref, *refs):
    pieces, refs = dict(zip(SPLIT_ORDER, refs[: NT + 1])), refs[NT + 1 :]
    hidden_ref, w_out_ref, pre_ref, act_ref = refs[:4]
    keep_hbm, give_hbm, grad_pre_hbm, keep_ref, give_ref, grad_pre_ref, proj_ref, sems = refs[4:]
    at, tea = at_ref[0], at_ref[1]
    contract = (((1,), (1,)), ((), ()))
    over_rows = (((0,), (0,)), ((), ()))
    copies = split_in(at, pieces, proj_ref, E, sems)
    proj_ref[:, E:] = jnp.zeros((ROWS, E_PAD - E), bf16)
    pre = pre_ref[...]
    sigma = 1.0 / (1.0 + jnp.exp(-pre))
    slope = sigma * (1.0 + pre * (1.0 - sigma))
    for copy in copies:
        copy.wait()
    grad_act = lax.dot_general(proj_ref[:, :E], w_out_ref[...], contract, preferred_element_type=f32)
    grad_pre = (grad_act * slope).astype(bf16)
    grad_pre_ref[...] = grad_pre
    copies = [pltpu.make_async_copy(grad_pre_ref, grad_pre_hbm, sems.at[0])]
    copies[0].start()
    d_half, e_half = hidden_ref.shape[1] // 2, E_PAD // 2
    in_rows, out_rows = d_half // GROUPS, e_half // GROUPS
    for n, (ref, target, side) in enumerate(((keep_ref, keep_hbm, tea), (give_ref, give_hbm, 1 - tea))):
        part = hidden_ref[:, pl.ds(pl.multiple_of(side * d_half, d_half), d_half)]
        grad = lax.dot_general(part, grad_pre, over_rows, preferred_element_type=f32)
        for c in range(GROUPS):
            ref[c, pl.ds(0, in_rows), :] = grad[c * in_rows : (c + 1) * in_rows].astype(ref.dtype)
        part = proj_ref[:, pl.ds(pl.multiple_of(side * e_half, e_half), e_half)]
        grad = lax.dot_general(part, act_ref[...], over_rows, preferred_element_type=f32)
        for c in range(GROUPS):
            ref[c, pl.ds(in_rows, out_rows), :] = grad[c * out_rows : (c + 1) * out_rows].astype(ref.dtype)
        copies.append(pltpu.make_async_copy(ref, target, sems.at[n + 1]))
        copies[-1].start()
    for copy in copies:
        copy.wait()


def backward(where, pieces, hidden_states, w_out, pre_act, activation):
    rows, d_model = hidden_states.shape
    width = activation.shape[1]
    halves = (GROUPS, (d_model + E_PAD) // 2 // GROUPS, width)
    return pl.pallas_call(
        backward_body,
        out_shape=[
            pltpu.HBM(halves, bf16),
            pltpu.HBM(halves, bf16),
            pltpu.HBM((rows, width), bf16),
        ],
        in_specs=[IN_SMEM] + in_place(NT + 1) + in_vmem(4),
        out_specs=in_place(3),
        scratch_shapes=[
            pltpu.VMEM(halves, bf16),
            pltpu.VMEM(halves, bf16),
            pltpu.VMEM((rows, width), bf16),
            pltpu.VMEM((ROWS, E_PAD), bf16),
            pltpu.SemaphoreType.DMA((NT + 1,)),
        ],
        compiler_params=scoped(14),
        cost_estimate=pl.CostEstimate(flops=1_200_000_000, bytes_accessed=9_000_000, transcendentals=100_000),
        name="backward",
    )(where, *[pieces[d] for d in SPLIT_ORDER], hidden_states, w_out, pre_act, activation)


def hidden_body(grad_pre_hbm, w_in_ref, terms_hbm, grad_pre_ref, terms_ref, sems):
    first = pltpu.make_async_copy(grad_pre_hbm, grad_pre_ref, sems.at[NT])
    first.start()
    contract = (((1,), (1,)), ((), ()))
    share = w_in_ref.shape[0] // NT
    copies = []
    first.wait()
    for d in range(NT):
        span = pl.ds(d * ROWS, ROWS)
        terms_ref[span, :] = lax.dot_general(
            grad_pre_ref[...], w_in_ref[pl.ds(d * share, share), :], contract, preferred_element_type=f32
        ).astype(bf16)
        copies.append(pltpu.make_async_copy(terms_ref.at[span, :], terms_hbm.at[span, :], sems.at[d]))
        copies[-1].start()
    for copy in copies:
        copy.wait()


def hidden_grads(grad_pre, w_in):
    shape = (NT * ROWS, w_in.shape[0] // NT)
    return pl.pallas_call(
        hidden_body,
        out_shape=pltpu.HBM(shape, bf16),
        in_specs=in_place(1) + in_vmem(1),
        out_specs=in_place(1)[0],
        scratch_shapes=[
            pltpu.VMEM(grad_pre.shape, bf16),
            pltpu.VMEM(shape, bf16),
            pltpu.SemaphoreType.DMA((NT + 1,)),
        ],
        compiler_params=scoped(6),
        cost_estimate=pl.CostEstimate(flops=600_000_000, bytes_accessed=4_000_000, transcendentals=0),
        name="hidden_grads",
    )(hbm(grad_pre), w_in)


def pair_body(keep_ref, got_ref, sum_ref):
    sum_ref[...] = (keep_ref[...].astype(f32) + got_ref[...].astype(f32)).astype(bf16)


def pair_sum(keep, got):
    return pl.pallas_call(
        pair_body,
        out_shape=jax.ShapeDtypeStruct(keep.shape, bf16),
        in_specs=in_vmem(2),
        out_specs=in_vmem(1)[0],
        compiler_params=scoped(8),
        cost_estimate=pl.CostEstimate(flops=600_000, bytes_accessed=5_000_000, transcendentals=0),
        name="pair_sum",
    )(keep, got)


def half_out(ref, side, w_in_hbm, w_out_hbm, w_in_ref, w_out_ref, flat_ref, sems):
    d_half, e_half = w_in_ref.shape[0], E_PAD // 2
    in_rows, out_rows = d_half // GROUPS, e_half // GROUPS
    for c in range(GROUPS):
        w_in_ref[pl.ds(c * in_rows, in_rows), :] = ref[c, pl.ds(0, in_rows), :].astype(f32)
    copy = pltpu.make_async_copy(
        w_in_ref, w_in_hbm.at[pl.ds(pl.multiple_of(side * d_half, d_half), d_half), :], sems.at[0]
    )
    copy.start()
    for c in range(GROUPS):
        flat_ref[pl.ds(c * out_rows, out_rows), :] = ref[c, pl.ds(in_rows, out_rows), :].astype(f32)
    for c in range(0, e_half, BLK):
        w_out_ref[:, pl.ds(c, BLK)] = flat_ref[pl.ds(c, BLK), :].T
    for which, start, size in ((0, 0, e_half), (1, e_half, E - e_half)):

        @pl.when(side == which)
        def _():
            part = pltpu.make_async_copy(
                w_out_ref.at[:, pl.ds(0, size)], w_out_hbm.at[:, pl.ds(start, size)], sems.at[1]
            )
            part.start()
            part.wait()

    copy.wait()


def first_body(tea_ref, mine_ref, sum_hbm, w_in_hbm, w_out_hbm, hidden_ref, w_in_ref, w_out_ref, flat_ref, sum_ref, sems):
    copy = pltpu.make_async_copy(sum_hbm, sum_ref, sems.at[2])
    copy.start()
    half_out(mine_ref, tea_ref[0], w_in_hbm, w_out_hbm, w_in_ref, w_out_ref, flat_ref, sems)
    copy.wait()
    hidden_ref[...] = sum_ref[...].astype(f32)


def second_body(tea_ref, other_ref, w_in_old, w_out_old, w_in_hbm, w_out_hbm, w_in_ref, w_out_ref, flat_ref, sems):
    half_out(other_ref, 1 - tea_ref[0], w_in_hbm, w_out_hbm, w_in_ref, w_out_ref, flat_ref, sems)


def half_scratch(d_model, width):
    return [
        pltpu.VMEM((d_model // 2, width), f32),
        pltpu.VMEM((width, E_PAD // 2), f32),
        pltpu.VMEM((E_PAD // 2, width), f32),
    ]


def first_half(tea, mine, hidden, d_model):
    width = mine.shape[-1]
    return pl.pallas_call(
        first_body,
        out_shape=[
            pltpu.HBM((d_model, width), f32),
            pltpu.HBM((width, E), f32),
            jax.ShapeDtypeStruct(hidden.shape, f32),
        ],
        in_specs=[IN_SMEM] + in_vmem(1) + in_place(1),
        out_specs=in_place(2) + in_vmem(1),
        scratch_shapes=half_scratch(d_model, width)
        + [pltpu.VMEM(hidden.shape, bf16), pltpu.SemaphoreType.DMA((3,))],
        compiler_params=scoped(12),
        cost_estimate=pl.CostEstimate(flops=0, bytes_accessed=5_000_000, transcendentals=0),
        name="first_half",
    )(tea, mine, hbm(hidden))


def second_half(tea, other, w_in, w_out):
    return pl.pallas_call(
        second_body,
        out_shape=[pltpu.HBM(w_in.shape, f32), pltpu.HBM(w_out.shape, f32)],
        in_specs=[IN_SMEM] + in_vmem(1) + in_place(2),
        out_specs=in_place(2),
        scratch_shapes=half_scratch(w_in.shape[0], w_in.shape[1]) + [pltpu.SemaphoreType.DMA((2,))],
        input_output_aliases={2: 0, 3: 1},
        compiler_params=scoped(12),
        cost_estimate=pl.CostEstimate(flops=0, bytes_accessed=4_000_000, transcendentals=0),
        name="second_half",
    )(tea, other, hbm(w_in), hbm(w_out))


def on_device(hidden_states, w_in, w_out, teacher, patch_map, row_pick, key_pick):
    seq_index = lax.axis_index("seq")
    tp_index = lax.axis_index("tp")
    tea_index = lax.axis_index("tea")
    at = jnp.full((1,), tp_index, jnp.int32)
    tea = jnp.full((1,), tea_index, jnp.int32)
    contract = (((1,), (1,)), ((), ()))

    picks = row_pick.reshape(GROUPS)
    group = jnp.full((1,), lax.axis_index(("seq", "tea")), jnp.int32)
    row_teacher, teacher_send = align(jnp.concatenate([at, group]), teacher, patch_map.reshape(1, ROWS), picks)
    teacher_send, at_next = lax.optimization_barrier((teacher_send, at))
    teacher_got = lax.all_to_all(teacher_send, "seq", 0, 0, tiled=True)

    pre_act, activation, *chunks = forward(at_next, hidden_states, w_in, w_out)
    activation, key_pick, picks = lax.optimization_barrier((activation, key_pick, picks))
    received = sum_split(*chunks)

    table = key_pick.reshape(GROUPS, GROUPS)
    of_rows = lax.dynamic_index_in_dim(table, seq_index, axis=0, keepdims=False)
    of_keys = lax.dynamic_index_in_dim(table, seq_index, axis=1, keepdims=False)
    local = jnp.repeat(jnp.stack([picks, of_rows, of_keys]), RB, axis=1)
    local = jnp.pad(local, ((0, 8 - 3), (0, E_WIDE - E - GROUPS * RB)))
    key_ids = jnp.arange(GROUPS * SHARD, dtype=jnp.int32)
    key_cell = key_ids // SHARD * RB + (tp_index * SHARD + key_ids % SHARD) // BLK
    spread = (jnp.arange(E_WIDE - E, dtype=jnp.int32)[:, None] == key_cell[None, :]).astype(bf16)

    *received, teacher_got = lax.optimization_barrier((*received, teacher_got))
    unit_student, inv_norm, row_send, key_send = normalise(chunks[0], local, teacher_got, received)
    rows = gather_ring(row_send)
    keys = lax.all_to_all(key_send, "seq", 0, 0, tiled=True).reshape(GROUPS * SHARD, E)
    teacher_got, inv_norm = lax.optimization_barrier((teacher_got, inv_norm))
    inv_norm = inv_norm[:, :1]
    key_teacher = teacher_got[:, :, :E].reshape(GROUPS * SHARD, E)
    gram_teacher = lax.dot_general(row_teacher, key_teacher, contract, preferred_element_type=f32)

    row_grad = gram_grads(at, rows, keys, gram_teacher, spread)
    unit_grad = row_grad[0]
    for piece in sum_ring(*row_grad):
        unit_grad = unit_grad + piece.astype(f32)
    inner = jnp.sum(unit_student * unit_grad, axis=-1, keepdims=True)
    grad_proj = ((unit_grad - unit_student * inner) * inv_norm).astype(bf16)
    pieces = gather_split(grad_proj)

    where = jnp.concatenate([at, tea])
    keep, give, grad_pre = backward(where, pieces, hidden_states, w_out, pre_act, activation)
    got = swap_tea(give)
    hidden_terms = hidden_grads(grad_pre, w_in)
    chip, hidden_terms = lax.optimization_barrier((pair_sum(keep, got), hidden_terms))
    hidden_sum = lax.psum_scatter(hidden_terms, "tp", scatter_dimension=0, tiled=True)
    chip = lax.all_to_all(chip, "seq", 0, 0, tiled=True)
    mine = to_all(jnp.sum(chip.astype(f32), axis=0).astype(bf16)).reshape(keep.shape)
    other = swap_tea(mine)
    grad_w_in, grad_w_out, grad_hidden = first_half(tea, mine, hidden_sum, hidden_states.shape[1])
    grad_w_in, grad_w_out = second_half(tea, other, grad_w_in, grad_w_out)
    return (grad_hidden, grad_w_in, grad_w_out)


def solution(mesh):
    return jax.shard_map(
        on_device,
        mesh=mesh,
        in_specs=(
            P(("seq", "tea"), None),
            P(None, "tp"),
            P("tp", None),
            P(("seq", "tea"), None),
            P(("seq", "tea")),
            P("seq", "tp", "tea", None),
            P(None, "tp", "tea", None),
        ),
        out_specs=(P(("seq", "tea"), "tp"), P(None, "tp"), P("tp", None)),
        check_vma=False,
    )
```

```python
import jax
import jax.numpy as jnp
from jax import lax
from jax.experimental import pallas as pl
from jax.experimental.pallas import tpu as pltpu
from jax.sharding import PartitionSpec as P

E = 1408
BLK = 128
RB = 3
SIDE = 4
NT = 8
GROUPS = SIDE * SIDE
SHARD = 48
ROWS = 384
E_WIDE = 1536
E_PAD = 1536

eps = 1e-06
bf16 = jnp.bfloat16
f32 = jnp.float32


def shift_tp(x, step):
    return lax.ppermute(x, "tp", [(i, (i + step) % NT) for i in range(NT)])


def swap_tea(x):
    return lax.ppermute(x, "tea", [(0, 1), (1, 0)])


LEFT = 768
RIGHT = 640


def gather_ring(x):
    before, after = shift_tp(x, 1), shift_tp(x, -1)
    before2, after2 = shift_tp(x, 2), shift_tp(x, -2)
    far_after = shift_tp(jnp.concatenate([after, after2[:, LEFT:]], axis=1), -2)
    far_before = shift_tp(jnp.concatenate([before, before2[:, :LEFT]], axis=1), 2)
    return [x, after, after2, far_after, before2, before, far_before]


def sum_ring(own, one, two, far_after, six, seven, far_before):
    far_after, far_before = shift_tp(far_after, 2).astype(f32), shift_tp(far_before, -2).astype(f32)
    one, seven = one + far_after[:, :E], seven + far_before[:, :E]
    two = two + jnp.concatenate([far_after[:, E:], jnp.zeros((SHARD, RIGHT), f32)], axis=1)
    six = six + jnp.concatenate([jnp.zeros((SHARD, LEFT), f32), far_before[:, E:]], axis=1)
    one, two, six, seven = (v.astype(bf16) for v in (one, two, six, seven))
    return [shift_tp(two, 2), shift_tp(six, -2), shift_tp(one, 1), shift_tp(seven, -1)]


def gather_split(x):
    before, after = shift_tp(x, 1), shift_tp(x, -1)
    before2, after2 = shift_tp(x, 2), shift_tp(x, -2)
    before3, after3 = shift_tp(before2, 1), shift_tp(after2, -1)
    left, right = shift_tp(before2[:, :LEFT], 2), shift_tp(after2[:, LEFT:], -2)
    return [x, after, after2, after3, left, right, before3, before2, before]


def pass_split(own, one, two, three, left, right, five, six, seven):
    three, five = shift_tp(three, 1), shift_tp(five, -1)
    left, right = shift_tp(left, 2), shift_tp(right, -2)
    one, seven = shift_tp(one, 1), shift_tp(seven, -1)
    blank = jnp.zeros(left.shape, f32), jnp.zeros(right.shape, f32)
    two = two + three.astype(f32) + jnp.concatenate([left.astype(f32), blank[1]], axis=1)
    six = six + five.astype(f32) + jnp.concatenate([blank[0], right.astype(f32)], axis=1)
    return one, seven, two.astype(bf16), six.astype(bf16)


def sum_split(*terms):
    one, seven, two, six = pass_split(*terms)
    return [one, seven, shift_tp(two, 2), shift_tp(six, -2)]


def to_all(x):
    return lax.all_to_all(jnp.broadcast_to(x[None], (GROUPS,) + x.shape), "seq", 0, 0, tiled=True)


def in_vmem(count):
    return [pl.BlockSpec(memory_space=pltpu.VMEM)] * count


def in_place(count):
    return [pl.BlockSpec(memory_space=pltpu.HBM)] * count


def hbm(x):
    return pltpu.with_memory_space_constraint(x, pltpu.HBM)


IN_SMEM = pl.BlockSpec(memory_space=pltpu.SMEM)
def scoped(mib):
    return pltpu.CompilerParams(vmem_limit_bytes=mib * 1024 * 1024)


PIECE_ORDER = (0, 1, 5, 2, 4, 3, 6)


def spot_of(at, d):
    return pl.multiple_of(lax.rem(at + d, NT) * SHARD, SHARD)


PARTS = 7
PLACES = (0, 1, 2, 3, 6, 7, 5)
STAGE = [pltpu.VMEM((5, SHARD, E_WIDE), bf16), pltpu.SemaphoreType.DMA((NT + 1,))]
WIDE, FULL = pltpu.HBM((SHARD, E_WIDE), f32), pltpu.HBM((SHARD, E_WIDE), bf16)
SPLIT = [WIDE, FULL, WIDE, FULL] + [pltpu.HBM((SHARD, E_WIDE // 2), bf16)] * 2 + [FULL, WIDE, FULL]
WIDE = pltpu.HBM((SHARD, E), f32)
CHUNKS = [
    WIDE,
    WIDE,
    WIDE,
    pltpu.HBM((SHARD, E + LEFT), bf16),
    WIDE,
    WIDE,
    pltpu.HBM((SHARD, E + RIGHT), bf16),
]


def far_parts(total_ref, at, after_ref, before_ref):
    half = total_ref[pl.ds(spot_of(at, 4), SHARD), :].astype(bf16)
    after_ref[:, :E] = total_ref[pl.ds(spot_of(at, 3), SHARD), :].astype(bf16)
    after_ref[:, E:] = half[:, :LEFT]
    before_ref[:, :E] = total_ref[pl.ds(spot_of(at, 5), SHARD), :].astype(bf16)
    before_ref[:, E:] = half[:, LEFT:]


def chunk_out(total_ref, at, targets, stage_ref, sems):
    wide = total_ref.shape[1]
    copies = []
    slot = 0
    for n, d, cols in (
        (3, 3, None),
        (6, 5, None),
        (4, 4, pl.ds(0, LEFT)),
        (5, 4, pl.ds(LEFT, wide - LEFT)),
        (1, 1, None),
        (8, 7, None),
        (2, 2, None),
        (7, 6, None),
        (0, 0, None),
    ):
        rows = pl.ds(spot_of(at, d), SHARD)
        if d in (0, 2, 6):
            source = total_ref.at[rows, :]
        else:
            if n != 5:
                stage_ref[slot] = total_ref[rows, :].astype(bf16)
                slot += 1
            source = stage_ref.at[slot - 1] if cols is None else stage_ref.at[slot - 1, :, cols]
        copies.append(pltpu.make_async_copy(source, targets[n], sems.at[n]))
        copies[-1].start()
    return copies


def chunk_store(total_ref, at, targets):
    far_parts(total_ref, at, targets[3], targets[6])
    for n in (0, 1, 2, 4, 5):
        targets[n][...] = total_ref[pl.ds(spot_of(at, PLACES[n]), SHARD), :]


def align_body(at_ref, teacher_hbm, patch_ref, rows_hbm, own_hbm, teacher_ref, rows_ref, own_ref, sems):
    copy = pltpu.make_async_copy(teacher_hbm, teacher_ref, sems.at[0])
    copy.start()
    copy.wait()
    teacher = teacher_ref[...].astype(f32)
    unit = (teacher * lax.rsqrt(jnp.sum(teacher * teacher, axis=-1, keepdims=True) + eps)).astype(bf16)
    ids = lax.broadcasted_iota(jnp.int32, (teacher.shape[0], ROWS), 0)
    hot = (ids == patch_ref[...] - at_ref[1] * teacher.shape[0]).astype(f32).astype(bf16)
    rows_ref[...] = lax.dot_general(
        hot, unit, (((0,), (0,)), ((), ())), preferred_element_type=f32
    ).astype(bf16)
    own_ref[...] = rows_ref[pl.ds(spot_of(at_ref[0], 0), SHARD), :]
    copies = [
        pltpu.make_async_copy(own_ref, own_hbm, sems.at[1]),
        pltpu.make_async_copy(rows_ref, rows_hbm, sems.at[2]),
    ]
    for copy in copies:
        copy.start()
    for copy in copies:
        copy.wait()


def align(at, teacher, patch):
    return pl.pallas_call(
        align_body,
        out_shape=[pltpu.HBM((ROWS, E), bf16), pltpu.HBM((SHARD, E), bf16)],
        in_specs=[IN_SMEM] + in_place(1) + in_vmem(1),
        out_specs=in_place(2),
        scratch_shapes=[
            pltpu.VMEM(teacher.shape, bf16),
            pltpu.VMEM((ROWS, E), bf16),
            pltpu.VMEM((SHARD, E), bf16),
            pltpu.SemaphoreType.DMA((3,)),
        ],
        compiler_params=scoped(12),
        cost_estimate=pl.CostEstimate(flops=250_000_000, bytes_accessed=4_000_000, transcendentals=0),
        name="align",
    )(at, hbm(teacher), patch)


def forward_body(at_ref, row_pick_ref, key_pick_ref, hidden_ref, w_in_ref, w_out_ref, pre_hbm, act_hbm, *refs):
    targets = refs[: NT + 1]
    total_ref, pre_ref, act_ref, sems, stage_ref, stage_sems = refs[NT + 1 :]
    pre = jnp.dot(hidden_ref[...], w_in_ref[...], preferred_element_type=f32)
    pre_ref[...] = pre
    act = (pre / (1.0 + jnp.exp(-pre))).astype(bf16)
    act_ref[...] = act
    copies = [
        pltpu.make_async_copy(pre_ref, pre_hbm, sems.at[0]),
        pltpu.make_async_copy(act_ref, act_hbm, sems.at[1]),
    ]
    for copy in copies:
        copy.start()
    total_ref[:, :E] = jnp.dot(act, w_out_ref[...], preferred_element_type=f32)
    shape = (16, E_WIDE - E)
    lane = lax.broadcasted_iota(jnp.int32, shape, 1)
    block = lax.broadcasted_iota(jnp.int32, shape, 0)
    counts = jnp.zeros(shape, f32)
    for j in range(GROUPS):
        key_block = key_pick_ref[at_ref[1], 0, 0, j]
        hit = (block == row_pick_ref[0, 0, 0, j]) & (lane == j * RB + key_block)
        counts = counts + jnp.where(hit, 1.0, 0.0)
    total_ref[:, E:] = jnp.zeros((ROWS, E_WIDE - E), f32)
    for r in range(NT):
        total_ref[r * SHARD : r * SHARD + 16, E:] = counts
    copies += chunk_out(total_ref, at_ref[0], targets, stage_ref, stage_sems)
    for copy in copies:
        copy.wait()


def forward(where, row_pick, key_pick, hidden_states, w_in, w_out):
    rows, width = hidden_states.shape[0], w_in.shape[1]
    return pl.pallas_call(
        forward_body,
        out_shape=[pltpu.HBM((rows, width), f32), pltpu.HBM((rows, width), bf16)] + SPLIT,
        in_specs=[IN_SMEM] * 3 + in_vmem(3),
        out_specs=in_place(3 + NT),
        scratch_shapes=[
            pltpu.VMEM((rows, E_WIDE), f32),
            pltpu.VMEM((rows, width), f32),
            pltpu.VMEM((rows, width), bf16),
            pltpu.SemaphoreType.DMA((2,)),
        ]
        + STAGE,
        compiler_params=scoped(16),
        cost_estimate=pl.CostEstimate(flops=900_000_000, bytes_accessed=8_000_000, transcendentals=100_000),
        name="forward",
    )(where, row_pick, key_pick, hidden_states, w_in, w_out)


RECEIVED = 4


def normalise_body(own_hbm, *refs):
    parts, refs = refs[:RECEIVED], refs[RECEIVED:]
    unit_hbm, inv_hbm, row_hbm, send_hbm, counts_hbm, own_ref, unit_ref, inv_ref, row_ref, counts_ref, got_ref, sems = refs
    first = pltpu.make_async_copy(own_hbm, own_ref, sems.at[RECEIVED])
    first.start()
    copies = [pltpu.make_async_copy(parts[i], got_ref.at[i], sems.at[i]) for i in range(RECEIVED)]
    for copy in copies:
        copy.start()
    first.wait()
    total = own_ref[...]
    for i in range(RECEIVED):
        copies[i].wait()
        total = total + got_ref[i].astype(f32)
    counts = total[:, E:]
    total = total[:, :E]
    inv = lax.rsqrt(jnp.sum(total * total, axis=-1, keepdims=True) + eps)
    unit = total * inv
    row_ref[:, :E] = unit.astype(bf16)
    row_ref[:, E:] = counts.astype(bf16)
    base = RECEIVED + 1
    copies = [pltpu.make_async_copy(row_ref, send_hbm.at[j], sems.at[base + j]) for j in range(GROUPS)]
    base += GROUPS
    copies.append(pltpu.make_async_copy(row_ref.at[:, pl.ds(0, E)], row_hbm, sems.at[base]))
    for copy in copies:
        copy.start()
    unit_ref[...] = unit
    inv_ref[...] = jnp.broadcast_to(inv, inv_ref.shape)
    counts_ref[...] = counts[:16]
    for n, (source, target) in enumerate(((unit_ref, unit_hbm), (inv_ref, inv_hbm), (counts_ref, counts_hbm))):
        copies.append(pltpu.make_async_copy(source, target, sems.at[base + 1 + n]))
        copies[-1].start()
    for copy in copies:
        copy.wait()


def normalise(own, parts):
    return pl.pallas_call(
        normalise_body,
        out_shape=[
            pltpu.HBM((SHARD, E), f32),
            pltpu.HBM((SHARD, BLK), f32),
            pltpu.HBM((SHARD, E), bf16),
            pltpu.HBM((GROUPS, SHARD, E_WIDE), bf16),
            pltpu.HBM((16, E_WIDE - E), f32),
        ],
        in_specs=in_place(1 + RECEIVED),
        out_specs=in_place(5),
        scratch_shapes=[
            pltpu.VMEM((SHARD, E_WIDE), f32),
            pltpu.VMEM((SHARD, E), f32),
            pltpu.VMEM((SHARD, BLK), f32),
            pltpu.VMEM((SHARD, E_WIDE), bf16),
            pltpu.VMEM((16, E_WIDE - E), f32),
            pltpu.VMEM((RECEIVED, SHARD, E_WIDE), bf16),
            pltpu.SemaphoreType.DMA((RECEIVED + GROUPS + 5,)),
        ],
        compiler_params=scoped(12),
        cost_estimate=pl.CostEstimate(flops=1_000_000, bytes_accessed=4_000_000, transcendentals=0),
        name="normalise",
    )(hbm(own), *[hbm(part) for part in parts])


def gather_in(at, pieces, target_ref, wide, sems):
    copies = []

    def bring(source, d, start, size):
        rows = pl.ds(spot_of(at, d), SHARD)
        copies.append(pltpu.make_async_copy(source, target_ref.at[rows, pl.ds(start, size)], sems.at[len(copies)]))
        copies[-1].start()

    for n in range(PARTS):
        source = pieces[n]
        if n in (3, 6):
            start, size = (LEFT, wide - LEFT) if n == 3 else (0, LEFT)
            bring(source.at[:, pl.ds(wide, size)], 4, start, size)
            source = source.at[:, pl.ds(0, wide)]
        bring(source, PLACES[n], 0, wide)
    return copies


def gram_body(at_ref, *refs):
    pieces, refs = dict(zip(PIECE_ORDER, refs[:PARTS])), refs[PARTS:]
    keys_hbm, teacher_hbm, counts_ref, spread_ref, choose_ref, cell_ref = refs[:6]
    targets, refs = refs[6 : 6 + PARTS], refs[6 + PARTS :]
    row_ref, key_ref, extra_ref, teacher_ref, grad_ref, total_ref, sems = refs
    contract = (((1,), (1,)), ((), ()))
    extra = pltpu.make_async_copy(keys_hbm.at[:, pl.ds(0, 16), pl.ds(E, E_WIDE - E)], extra_ref, sems.at[PARTS + 2])
    extra.start()
    row_copies = gather_in(at_ref[0], pieces, row_ref, E, sems)
    step = GROUPS * SHARD // 2
    copies = []
    base = PARTS + 3
    for i in range(2):
        some = []
        for j in range(i * GROUPS // 2, (i + 1) * GROUPS // 2):
            some.append(
                pltpu.make_async_copy(
                    keys_hbm.at[j, :, pl.ds(0, E)], key_ref.at[pl.ds(j * SHARD, SHARD), :], sems.at[base + j]
                )
            )
        span = pl.ds(i * step, step)
        some.append(pltpu.make_async_copy(teacher_hbm.at[:, span], teacher_ref.at[:, span], sems.at[base + GROUPS + i]))
        for copy in some:
            copy.start()
        copies.append(some)
    extra.wait()
    theirs = jnp.dot(
        extra_ref[...].reshape(GROUPS * 16, E_WIDE - E), choose_ref[...], preferred_element_type=f32
    ).astype(bf16)
    theirs = lax.dot_general(theirs, cell_ref[...], (((0,), (0,)), ((), ())), preferred_element_type=f32)
    ours = jnp.dot(counts_ref[...].astype(bf16), spread_ref[...], preferred_element_type=f32)
    tile = (ours + theirs[:16]) * (E / 8.0)
    for copy in row_copies:
        copy.wait()
    for i in range(2):
        span = pl.ds(i * step, step)
        for copy in copies[i]:
            copy.wait()
        diff = (
            lax.dot_general(row_ref[...], key_ref[span, :], contract, preferred_element_type=f32)
            - teacher_ref[:, span]
        )
        for a in range(RB):
            grad_ref[pl.ds(a * BLK, BLK), span] = (
                diff[a * BLK : (a + 1) * BLK] * tile[a : a + 1, i * step : (i + 1) * step]
            ).astype(bf16)
    for c, wide in ((0, 768), (768, 640)):
        total_ref[:, pl.ds(c, wide)] = jnp.dot(
            grad_ref[...], key_ref[:, pl.ds(c, wide)], preferred_element_type=f32
        )
    chunk_store(total_ref, at_ref[0], targets)


def gram_grads(at, pieces, keys, gram_teacher, counts, spread, choose, cell):
    return pl.pallas_call(
        gram_body,
        out_shape=[jax.ShapeDtypeStruct(chunk.shape, chunk.dtype) for chunk in CHUNKS],
        in_specs=[IN_SMEM] + in_place(PARTS + 2) + in_vmem(4),
        out_specs=in_vmem(PARTS),
        scratch_shapes=[
            pltpu.VMEM((ROWS, E), bf16),
            pltpu.VMEM((GROUPS * SHARD, E), bf16),
            pltpu.VMEM((GROUPS, 16, E_WIDE - E), bf16),
            pltpu.VMEM((ROWS, GROUPS * SHARD), f32),
            pltpu.VMEM((ROWS, GROUPS * SHARD), bf16),
            pltpu.VMEM((ROWS, E), f32),
            pltpu.SemaphoreType.DMA((PARTS + 3 + GROUPS + 2,)),
        ],
        compiler_params=scoped(20),
        cost_estimate=pl.CostEstimate(flops=1_700_000_000, bytes_accessed=9_000_000, transcendentals=0),
        name="gram_grads",
    )(at, *[hbm(pieces[n]) for n in PIECE_ORDER], keys, hbm(gram_teacher), counts, spread, choose, cell)


def split_in(at, pieces, target_ref, wide, sems):
    copies = []
    for n in range(NT + 1):
        d = n if n <= 4 else n - 1
        cols = {4: pl.ds(0, LEFT), 5: pl.ds(LEFT, wide - LEFT)}.get(n, pl.ds(0, wide))
        rows = pl.ds(spot_of(at, d), SHARD)
        copies.append(pltpu.make_async_copy(pieces[n], target_ref.at[rows, cols], sems.at[n]))
        copies[-1].start()
    return copies


SPLIT_ORDER = (0, 1, 8, 2, 7, 3, 6, 4, 5)


def backward_body(at_ref, *refs):
    pieces, refs = dict(zip(SPLIT_ORDER, refs[: NT + 1])), refs[NT + 1 :]
    hidden_ref, w_out_ref, pre_ref, act_ref = refs[:4]
    keep_hbm, give_hbm, grad_pre_hbm, keep_ref, give_ref, grad_pre_ref, proj_ref, sems = refs[4:]
    at, tea = at_ref[0], at_ref[1]
    contract = (((1,), (1,)), ((), ()))
    over_rows = (((0,), (0,)), ((), ()))
    copies = split_in(at, pieces, proj_ref, E, sems)
    proj_ref[:, E:] = jnp.zeros((ROWS, E_PAD - E), bf16)
    pre = pre_ref[...]
    sigma = 1.0 / (1.0 + jnp.exp(-pre))
    slope = sigma * (1.0 + pre * (1.0 - sigma))
    for copy in copies:
        copy.wait()
    grad_act = lax.dot_general(proj_ref[:, :E], w_out_ref[...], contract, preferred_element_type=f32)
    grad_pre = (grad_act * slope).astype(bf16)
    grad_pre_ref[...] = grad_pre
    copies = [pltpu.make_async_copy(grad_pre_ref, grad_pre_hbm, sems.at[0])]
    copies[0].start()
    d_half, e_half = hidden_ref.shape[1] // 2, E_PAD // 2
    in_rows, out_rows = d_half // GROUPS, e_half // GROUPS
    for n, (ref, target, side) in enumerate(((keep_ref, keep_hbm, tea), (give_ref, give_hbm, 1 - tea))):
        part = hidden_ref[:, pl.ds(pl.multiple_of(side * d_half, d_half), d_half)]
        grad = lax.dot_general(part, grad_pre, over_rows, preferred_element_type=f32)
        for c in range(GROUPS):
            ref[c, pl.ds(0, in_rows), :] = grad[c * in_rows : (c + 1) * in_rows].astype(ref.dtype)
        part = proj_ref[:, pl.ds(pl.multiple_of(side * e_half, e_half), e_half)]
        grad = lax.dot_general(part, act_ref[...], over_rows, preferred_element_type=f32)
        for c in range(GROUPS):
            ref[c, pl.ds(in_rows, out_rows), :] = grad[c * out_rows : (c + 1) * out_rows].astype(ref.dtype)
        copies.append(pltpu.make_async_copy(ref, target, sems.at[n + 1]))
        copies[-1].start()
    for copy in copies:
        copy.wait()


def backward(where, pieces, hidden_states, w_out, pre_act, activation):
    rows, d_model = hidden_states.shape
    width = activation.shape[1]
    halves = (GROUPS, (d_model + E_PAD) // 2 // GROUPS, width)
    return pl.pallas_call(
        backward_body,
        out_shape=[
            pltpu.HBM(halves, bf16),
            pltpu.HBM(halves, bf16),
            pltpu.HBM((rows, width), bf16),
        ],
        in_specs=[IN_SMEM] + in_place(NT + 1) + in_vmem(4),
        out_specs=in_place(3),
        scratch_shapes=[
            pltpu.VMEM(halves, bf16),
            pltpu.VMEM(halves, bf16),
            pltpu.VMEM((rows, width), bf16),
            pltpu.VMEM((ROWS, E_PAD), bf16),
            pltpu.SemaphoreType.DMA((NT + 1,)),
        ],
        compiler_params=scoped(14),
        cost_estimate=pl.CostEstimate(flops=1_200_000_000, bytes_accessed=9_000_000, transcendentals=100_000),
        name="backward",
    )(where, *[pieces[d] for d in SPLIT_ORDER], hidden_states, w_out, pre_act, activation)


def hidden_body(grad_pre_hbm, w_in_ref, terms_hbm, grad_pre_ref, terms_ref, sems):
    first = pltpu.make_async_copy(grad_pre_hbm, grad_pre_ref, sems.at[NT])
    first.start()
    contract = (((1,), (1,)), ((), ()))
    share = w_in_ref.shape[0] // NT
    copies = []
    first.wait()
    for d in range(NT):
        span = pl.ds(d * ROWS, ROWS)
        terms_ref[span, :] = lax.dot_general(
            grad_pre_ref[...], w_in_ref[pl.ds(d * share, share), :], contract, preferred_element_type=f32
        ).astype(bf16)
        copies.append(pltpu.make_async_copy(terms_ref.at[span, :], terms_hbm.at[span, :], sems.at[d]))
        copies[-1].start()
    for copy in copies:
        copy.wait()


def hidden_grads(grad_pre, w_in):
    shape = (NT * ROWS, w_in.shape[0] // NT)
    return pl.pallas_call(
        hidden_body,
        out_shape=pltpu.HBM(shape, bf16),
        in_specs=in_place(1) + in_vmem(1),
        out_specs=in_place(1)[0],
        scratch_shapes=[
            pltpu.VMEM(grad_pre.shape, bf16),
            pltpu.VMEM(shape, bf16),
            pltpu.SemaphoreType.DMA((NT + 1,)),
        ],
        compiler_params=scoped(6),
        cost_estimate=pl.CostEstimate(flops=600_000_000, bytes_accessed=4_000_000, transcendentals=0),
        name="hidden_grads",
    )(hbm(grad_pre), w_in)


def pair_body(keep_ref, got_ref, sum_ref):
    sum_ref[...] = (keep_ref[...].astype(f32) + got_ref[...].astype(f32)).astype(bf16)


def pair_sum(keep, got):
    return pl.pallas_call(
        pair_body,
        out_shape=jax.ShapeDtypeStruct(keep.shape, bf16),
        in_specs=in_vmem(2),
        out_specs=in_vmem(1)[0],
        compiler_params=scoped(8),
        cost_estimate=pl.CostEstimate(flops=600_000, bytes_accessed=5_000_000, transcendentals=0),
        name="pair_sum",
    )(keep, got)


def half_out(ref, side, w_in_hbm, w_out_hbm, w_in_ref, w_out_ref, flat_ref, sems):
    d_half, e_half = w_in_ref.shape[0], E_PAD // 2
    in_rows, out_rows = d_half // GROUPS, e_half // GROUPS
    for c in range(GROUPS):
        w_in_ref[pl.ds(c * in_rows, in_rows), :] = ref[c, pl.ds(0, in_rows), :].astype(f32)
    copy = pltpu.make_async_copy(
        w_in_ref, w_in_hbm.at[pl.ds(pl.multiple_of(side * d_half, d_half), d_half), :], sems.at[0]
    )
    copy.start()
    for c in range(GROUPS):
        flat_ref[pl.ds(c * out_rows, out_rows), :] = ref[c, pl.ds(in_rows, out_rows), :].astype(f32)
    for c in range(0, e_half, BLK):
        w_out_ref[:, pl.ds(c, BLK)] = flat_ref[pl.ds(c, BLK), :].T
    for which, start, size in ((0, 0, e_half), (1, e_half, E - e_half)):

        @pl.when(side == which)
        def _():
            part = pltpu.make_async_copy(
                w_out_ref.at[:, pl.ds(0, size)], w_out_hbm.at[:, pl.ds(start, size)], sems.at[1]
            )
            part.start()
            part.wait()

    copy.wait()


def first_body(tea_ref, mine_ref, sum_hbm, w_in_hbm, w_out_hbm, hidden_ref, w_in_ref, w_out_ref, flat_ref, sum_ref, sems):
    copy = pltpu.make_async_copy(sum_hbm, sum_ref, sems.at[2])
    copy.start()
    half_out(mine_ref, tea_ref[0], w_in_hbm, w_out_hbm, w_in_ref, w_out_ref, flat_ref, sems)
    copy.wait()
    hidden_ref[...] = sum_ref[...].astype(f32)


def second_body(tea_ref, other_ref, w_in_old, w_out_old, w_in_hbm, w_out_hbm, w_in_ref, w_out_ref, flat_ref, sems):
    half_out(other_ref, 1 - tea_ref[0], w_in_hbm, w_out_hbm, w_in_ref, w_out_ref, flat_ref, sems)


def half_scratch(d_model, width):
    return [
        pltpu.VMEM((d_model // 2, width), f32),
        pltpu.VMEM((width, E_PAD // 2), f32),
        pltpu.VMEM((E_PAD // 2, width), f32),
    ]


def first_half(tea, mine, hidden, d_model):
    width = mine.shape[-1]
    return pl.pallas_call(
        first_body,
        out_shape=[
            pltpu.HBM((d_model, width), f32),
            pltpu.HBM((width, E), f32),
            jax.ShapeDtypeStruct(hidden.shape, f32),
        ],
        in_specs=[IN_SMEM] + in_vmem(1) + in_place(1),
        out_specs=in_place(2) + in_vmem(1),
        scratch_shapes=half_scratch(d_model, width)
        + [pltpu.VMEM(hidden.shape, bf16), pltpu.SemaphoreType.DMA((3,))],
        compiler_params=scoped(12),
        cost_estimate=pl.CostEstimate(flops=0, bytes_accessed=5_000_000, transcendentals=0),
        name="first_half",
    )(tea, mine, hbm(hidden))


def second_half(tea, other, w_in, w_out):
    return pl.pallas_call(
        second_body,
        out_shape=[pltpu.HBM(w_in.shape, f32), pltpu.HBM(w_out.shape, f32)],
        in_specs=[IN_SMEM] + in_vmem(1) + in_place(2),
        out_specs=in_place(2),
        scratch_shapes=half_scratch(w_in.shape[0], w_in.shape[1]) + [pltpu.SemaphoreType.DMA((2,))],
        input_output_aliases={2: 0, 3: 1},
        compiler_params=scoped(12),
        cost_estimate=pl.CostEstimate(flops=0, bytes_accessed=4_000_000, transcendentals=0),
        name="second_half",
    )(tea, other, hbm(w_in), hbm(w_out))


def on_device(hidden_states, w_in, w_out, teacher, patch_map, row_pick, key_pick):
    seq_index = lax.axis_index("seq")
    tp_index = lax.axis_index("tp")
    tea_index = lax.axis_index("tea")
    at = jnp.full((1,), tp_index, jnp.int32)
    tea = jnp.full((1,), tea_index, jnp.int32)
    contract = (((1,), (1,)), ((), ()))

    group = jnp.full((1,), lax.axis_index(("seq", "tea")), jnp.int32)
    row_teacher, own_teacher = align(jnp.concatenate([at, group]), teacher, patch_map.reshape(1, ROWS))
    seq_at = jnp.full((1,), seq_index, jnp.int32)
    own_teacher, at_next = lax.optimization_barrier((own_teacher, jnp.concatenate([at, seq_at])))
    key_teacher = lax.all_gather(own_teacher, "seq", axis=0, tiled=True)

    pre_act, activation, *chunks = forward(at_next, row_pick, key_pick, hidden_states, w_in, w_out)
    received = sum_split(*chunks)

    unit_student, inv_norm, row_send, key_send, counts = normalise(chunks[0], received)
    inv_norm, late = lax.optimization_barrier((inv_norm, jnp.concatenate([at, seq_at])))
    inv_norm = inv_norm[:, :1]
    rows = gather_ring(row_send)
    keys = lax.all_to_all(key_send, "seq", 0, 0, tiled=True)

    key_ids = jnp.arange(GROUPS * SHARD, dtype=jnp.int32)
    key_group, key_block = key_ids // SHARD, (late[0] * SHARD + key_ids % SHARD) // BLK
    lanes = jnp.arange(E_WIDE - E, dtype=jnp.int32)
    spread = (lanes[:, None] == (key_group * RB + key_block)[None, :]).astype(bf16)
    cell = (jnp.arange(GROUPS * 16, dtype=jnp.int32)[:, None] == (key_group * 16 + key_block)[None, :]).astype(bf16)
    choose = ((lanes[:, None] == late[1] * RB + lanes[None, :]) & (lanes[None, :] < RB)).astype(bf16)

    *rows, key_teacher = lax.optimization_barrier((*rows, key_teacher))
    gram_teacher = lax.dot_general(row_teacher, key_teacher, contract, preferred_element_type=f32)
    row_grad = gram_grads(at, rows, keys, gram_teacher, counts, spread, choose, cell)
    unit_grad = row_grad[0]
    for piece in sum_ring(*row_grad):
        unit_grad = unit_grad + piece.astype(f32)
    inner = jnp.sum(unit_student * unit_grad, axis=-1, keepdims=True)
    grad_proj = ((unit_grad - unit_student * inner) * inv_norm).astype(bf16)
    pieces = gather_split(grad_proj)

    where = jnp.concatenate([at, tea])
    keep, give, grad_pre = backward(where, pieces, hidden_states, w_out, pre_act, activation)
    got = swap_tea(give)
    hidden_terms = hidden_grads(grad_pre, w_in)
    chip, hidden_terms = lax.optimization_barrier((pair_sum(keep, got), hidden_terms))
    hidden_sum = lax.psum_scatter(hidden_terms, "tp", scatter_dimension=0, tiled=True)
    chip = lax.all_to_all(chip, "seq", 0, 0, tiled=True)
    mine = to_all(jnp.sum(chip.astype(f32), axis=0).astype(bf16)).reshape(keep.shape)
    other = swap_tea(mine)
    grad_w_in, grad_w_out, grad_hidden = first_half(tea, mine, hidden_sum, hidden_states.shape[1])
    grad_w_in, grad_w_out = second_half(tea, other, grad_w_in, grad_w_out)
    return (grad_hidden, grad_w_in, grad_w_out)


def solution(mesh):
    return jax.shard_map(
        on_device,
        mesh=mesh,
        in_specs=(
            P(("seq", "tea"), None),
            P(None, "tp"),
            P("tp", None),
            P(("seq", "tea"), None),
            P(("seq", "tea")),
            P("seq", "tp", "tea", None),
            P(None, "tp", "tea", None),
        ),
        out_specs=(P(("seq", "tea"), "tp"), P(None, "tp"), P("tp", None)),
        check_vma=False,
    )
```

```python
import jax
import jax.numpy as jnp
from jax import lax
from jax.experimental import pallas as pl
from jax.experimental.pallas import tpu as pltpu
from jax.sharding import PartitionSpec as P

E = 1408
BLK = 128
RB = 3
SIDE = 4
NT = 8
GROUPS = SIDE * SIDE
SHARD = 48
ROWS = 384
E_WIDE = 1536
E_PAD = 1536

eps = 1e-06
bf16 = jnp.bfloat16
f32 = jnp.float32


def shift_tp(x, step):
    return lax.ppermute(x, "tp", [(i, (i + step) % NT) for i in range(NT)])


def swap_tea(x):
    return lax.ppermute(x, "tea", [(0, 1), (1, 0)])


LEFT = 768
RIGHT = 640


def gather_ring(x):
    before, after = shift_tp(x, 1), shift_tp(x, -1)
    before2, after2 = shift_tp(x, 2), shift_tp(x, -2)
    far_after = shift_tp(jnp.concatenate([after, after2[:, LEFT:]], axis=1), -2)
    far_before = shift_tp(jnp.concatenate([before, before2[:, :LEFT]], axis=1), 2)
    return [x, after, after2, far_after, before2, before, far_before]


def gather_split(x):
    before, after = shift_tp(x, 1), shift_tp(x, -1)
    before2, after2 = shift_tp(x, 2), shift_tp(x, -2)
    before3, after3 = shift_tp(before2, 1), shift_tp(after2, -1)
    left, right = shift_tp(before2[:, :LEFT], 2), shift_tp(after2[:, LEFT:], -2)
    return [x, after, after2, after3, left, right, before3, before2, before]


def pass_split(own, one, two, three, left, right, five, six, seven):
    three, five = shift_tp(three, 1), shift_tp(five, -1)
    left, right = shift_tp(left, 2), shift_tp(right, -2)
    one, seven = shift_tp(one, 1), shift_tp(seven, -1)
    blank = jnp.zeros(left.shape, f32), jnp.zeros(right.shape, f32)
    two = two + three.astype(f32) + jnp.concatenate([left.astype(f32), blank[1]], axis=1)
    six = six + five.astype(f32) + jnp.concatenate([blank[0], right.astype(f32)], axis=1)
    return one, seven, two.astype(bf16), six.astype(bf16)


def sum_split(*terms):
    one, seven, two, six = pass_split(*terms)
    return [one, seven, shift_tp(two, 2), shift_tp(six, -2)]


def to_all(x):
    return lax.all_to_all(jnp.broadcast_to(x[None], (GROUPS,) + x.shape), "seq", 0, 0, tiled=True)


def in_vmem(count):
    return [pl.BlockSpec(memory_space=pltpu.VMEM)] * count


def in_place(count):
    return [pl.BlockSpec(memory_space=pltpu.HBM)] * count


def hbm(x):
    return pltpu.with_memory_space_constraint(x, pltpu.HBM)


IN_SMEM = pl.BlockSpec(memory_space=pltpu.SMEM)
def scoped(mib):
    return pltpu.CompilerParams(vmem_limit_bytes=mib * 1024 * 1024)


PIECE_ORDER = (0, 1, 5, 2, 4, 3, 6)


def spot_of(at, d):
    return pl.multiple_of(lax.rem(at + d, NT) * SHARD, SHARD)


PARTS = 7
PLACES = (0, 1, 2, 3, 6, 7, 5)
STAGE = [pltpu.VMEM((5, SHARD, E), bf16), pltpu.SemaphoreType.DMA((NT + 1,))]
WIDE, FULL = pltpu.HBM((SHARD, E), f32), pltpu.HBM((SHARD, E), bf16)
SPLIT = [WIDE, FULL, WIDE, FULL, pltpu.HBM((SHARD, LEFT), bf16), pltpu.HBM((SHARD, RIGHT), bf16), FULL, WIDE, FULL]


def chunk_out(total_ref, at, targets, stage_ref, sems):
    copies = []
    slot = 0
    for n, d, cols in (
        (3, 3, None),
        (6, 5, None),
        (4, 4, pl.ds(0, LEFT)),
        (5, 4, pl.ds(LEFT, RIGHT)),
        (1, 1, None),
        (8, 7, None),
        (2, 2, None),
        (7, 6, None),
        (0, 0, None),
    ):
        rows = pl.ds(spot_of(at, d), SHARD)
        if d in (0, 2, 6):
            source = total_ref.at[rows, :]
        else:
            if n != 5:
                stage_ref[slot] = total_ref[rows, :].astype(bf16)
                slot += 1
            source = stage_ref.at[slot - 1] if cols is None else stage_ref.at[slot - 1, :, cols]
        copies.append(pltpu.make_async_copy(source, targets[n], sems.at[n]))
        copies[-1].start()
    return copies


def chunk_store(total_ref, at, targets):
    for n, target in enumerate(targets):
        d = n if n <= 4 else n - 1
        cols = {4: pl.ds(0, LEFT), 5: pl.ds(LEFT, RIGHT)}.get(n, pl.ds(0, E))
        target[...] = total_ref[pl.ds(spot_of(at, d), SHARD), cols].astype(target.dtype)


def align_body(at_ref, teacher_hbm, patch_ref, picks_ref, rows_hbm, send_hbm, teacher_ref, rows_ref, own_ref, extra_ref, sems):
    copy = pltpu.make_async_copy(teacher_hbm, teacher_ref, sems.at[GROUPS])
    copy.start()
    for j in range(GROUPS):
        extra_ref[j] = jnp.full(extra_ref.shape[1:], picks_ref[j], jnp.int32).astype(f32).astype(bf16)
    extra = pltpu.make_async_copy(extra_ref, send_hbm.at[:, :, pl.ds(E, E_WIDE - E)], sems.at[GROUPS + 1])
    extra.start()
    copy.wait()
    teacher = teacher_ref[...].astype(f32)
    unit = (teacher * lax.rsqrt(jnp.sum(teacher * teacher, axis=-1, keepdims=True) + eps)).astype(bf16)
    ids = lax.broadcasted_iota(jnp.int32, (teacher.shape[0], ROWS), 0)
    hot = (ids == patch_ref[...] - at_ref[1] * teacher.shape[0]).astype(f32).astype(bf16)
    rows_ref[...] = lax.dot_general(
        hot, unit, (((0,), (0,)), ((), ())), preferred_element_type=f32
    ).astype(bf16)
    copies = [pltpu.make_async_copy(rows_ref, rows_hbm, sems.at[GROUPS])]
    copies[0].start()
    own_ref[...] = rows_ref[pl.ds(spot_of(at_ref[0], 0), SHARD), :]
    for j in range(GROUPS):
        copies.append(pltpu.make_async_copy(own_ref, send_hbm.at[j, :, pl.ds(0, E)], sems.at[j]))
        copies[-1].start()
    copies.append(extra)
    for copy in copies:
        copy.wait()


def align(at, teacher, patch, picks):
    return pl.pallas_call(
        align_body,
        out_shape=[
            pltpu.HBM((ROWS, E), bf16),
            pltpu.HBM((GROUPS, SHARD, E_WIDE), bf16),
        ],
        in_specs=[IN_SMEM] + in_place(1) + in_vmem(1) + [IN_SMEM],
        out_specs=in_place(2),
        scratch_shapes=[
            pltpu.VMEM(teacher.shape, bf16),
            pltpu.VMEM((ROWS, E), bf16),
            pltpu.VMEM((SHARD, E), bf16),
            pltpu.VMEM((GROUPS, SHARD, E_WIDE - E), bf16),
            pltpu.SemaphoreType.DMA((GROUPS + 2,)),
        ],
        compiler_params=scoped(12),
        cost_estimate=pl.CostEstimate(flops=250_000_000, bytes_accessed=4_000_000, transcendentals=0),
        name="align",
    )(at, hbm(teacher), patch, picks)


def forward_body(at_ref, hidden_ref, w_in_ref, w_out_ref, pre_hbm, act_hbm, *refs):
    targets = refs[: NT + 1]
    total_ref, pre_ref, act_ref, sems, stage_ref, stage_sems = refs[NT + 1 :]
    pre = jnp.dot(hidden_ref[...], w_in_ref[...], preferred_element_type=f32)
    pre_ref[...] = pre
    act = (pre / (1.0 + jnp.exp(-pre))).astype(bf16)
    act_ref[...] = act
    copies = [
        pltpu.make_async_copy(pre_ref, pre_hbm, sems.at[0]),
        pltpu.make_async_copy(act_ref, act_hbm, sems.at[1]),
    ]
    for copy in copies:
        copy.start()
    total_ref[...] = jnp.dot(act, w_out_ref[...], preferred_element_type=f32)
    copies += chunk_out(total_ref, at_ref[0], targets, stage_ref, stage_sems)
    for copy in copies:
        copy.wait()


def forward(at, hidden_states, w_in, w_out):
    rows, width = hidden_states.shape[0], w_in.shape[1]
    return pl.pallas_call(
        forward_body,
        out_shape=[pltpu.HBM((rows, width), f32), pltpu.HBM((rows, width), bf16)] + SPLIT,
        in_specs=[IN_SMEM] + in_vmem(3),
        out_specs=in_place(3 + NT),
        scratch_shapes=[
            pltpu.VMEM((rows, E), f32),
            pltpu.VMEM((rows, width), f32),
            pltpu.VMEM((rows, width), bf16),
            pltpu.SemaphoreType.DMA((2,)),
        ]
        + STAGE,
        compiler_params=scoped(16),
        cost_estimate=pl.CostEstimate(flops=900_000_000, bytes_accessed=8_000_000, transcendentals=100_000),
        name="forward",
    )(at, hidden_states, w_in, w_out)


RECEIVED = 4


def normalise_body(local_ref, own_hbm, theirs_hbm, *refs):
    parts, refs = refs[: RECEIVED], refs[RECEIVED :]
    unit_hbm, inv_hbm, row_hbm, send_hbm, unit_ref, inv_ref, row_ref, got_ref, theirs_ref, sems = refs
    first = pltpu.make_async_copy(own_hbm, unit_ref, sems.at[RECEIVED + 1])
    first.start()
    copies = [pltpu.make_async_copy(parts[i], got_ref.at[i], sems.at[i]) for i in range(RECEIVED)]
    picks = pltpu.make_async_copy(
        theirs_hbm.at[:, pl.ds(0, 16), pl.ds(E, E_WIDE - E)], theirs_ref, sems.at[RECEIVED]
    )
    for copy in copies:
        copy.start()
    picks.start()
    first.wait()
    total = unit_ref[...]
    for i in range(RECEIVED):
        copies[i].wait()
        total = total + got_ref[i].astype(f32)
    inv = lax.rsqrt(jnp.sum(total * total, axis=-1, keepdims=True) + eps)
    unit = total * inv
    row_ref[:, :E] = unit.astype(bf16)
    copies = [
        pltpu.make_async_copy(row_ref.at[:, pl.ds(0, E)], send_hbm.at[j], sems.at[RECEIVED + 4 + j]) for j in range(GROUPS)
    ]
    for copy in copies:
        copy.start()
    unit_ref[...] = unit
    inv_ref[...] = jnp.broadcast_to(inv, inv_ref.shape)
    copies.append(pltpu.make_async_copy(unit_ref, unit_hbm, sems.at[RECEIVED + 1]))
    copies[-1].start()
    copies.append(pltpu.make_async_copy(inv_ref, inv_hbm, sems.at[RECEIVED + 2]))
    copies[-1].start()
    shape = (16, E_WIDE - E)
    lane = lax.broadcasted_iota(jnp.int32, shape, 1)
    block = lax.broadcasted_iota(jnp.int32, shape, 0)
    group, end = lane // RB, lane % RB
    picks.wait()
    other = jnp.zeros(shape, f32)
    for j in range(GROUPS):
        other = other + jnp.where(group == j, theirs_ref[j].astype(f32), 0.0)
    as_row = (local_ref[0:1, :] == block) & (local_ref[1:2, :] == end)
    as_key = (local_ref[2:3, :] == block) & (other.astype(jnp.int32) == end)
    counts = as_row.astype(f32) + as_key.astype(f32)
    counts = jnp.where((group < GROUPS) & (block < RB), counts, 0.0)
    row_ref[:, E:] = jnp.concatenate([counts, jnp.zeros((SHARD - 16, E_WIDE - E), f32)], axis=0).astype(bf16)
    copies.append(pltpu.make_async_copy(row_ref, row_hbm, sems.at[RECEIVED + 3]))
    copies[-1].start()
    for copy in copies:
        copy.wait()


def normalise(own, local, theirs, parts):
    return pl.pallas_call(
        normalise_body,
        out_shape=[
            pltpu.HBM((SHARD, E), f32),
            pltpu.HBM((SHARD, BLK), f32),
            pltpu.HBM((SHARD, E_WIDE), bf16),
            pltpu.HBM((GROUPS, SHARD, E), bf16),
        ],
        in_specs=in_vmem(1) + in_place(RECEIVED + 2),
        out_specs=in_place(4),
        scratch_shapes=[
            pltpu.VMEM((SHARD, E), f32),
            pltpu.VMEM((SHARD, BLK), f32),
            pltpu.VMEM((SHARD, E_WIDE), bf16),
            pltpu.VMEM((RECEIVED, SHARD, E), bf16),
            pltpu.VMEM((GROUPS, 16, E_WIDE - E), bf16),
            pltpu.SemaphoreType.DMA((RECEIVED + 4 + GROUPS,)),
        ],
        compiler_params=scoped(12),
        cost_estimate=pl.CostEstimate(flops=1_000_000, bytes_accessed=4_000_000, transcendentals=0),
        name="normalise",
    )(local, hbm(own), theirs, *[hbm(part) for part in parts])


def gather_in(at, pieces, target_ref, wide, sems):
    copies = []

    def bring(source, d, start, size):
        rows = pl.ds(spot_of(at, d), SHARD)
        copies.append(pltpu.make_async_copy(source, target_ref.at[rows, pl.ds(start, size)], sems.at[len(copies)]))
        copies[-1].start()

    for n in range(PARTS):
        source = pieces[n]
        if n in (3, 6):
            start, size = (LEFT, wide - LEFT) if n == 3 else (0, LEFT)
            bring(source.at[:, pl.ds(wide, size)], 4, start, size)
            source = source.at[:, pl.ds(0, wide)]
        bring(source, PLACES[n], 0, wide)
    return copies


def gram_body(at_ref, *refs):
    pieces, refs = dict(zip(PIECE_ORDER, refs[:PARTS])), refs[PARTS:]
    keys_hbm, teacher_hbm, spread_ref = refs[:3]
    refs = refs[3:]
    targets = refs[: NT + 1]
    row_ref, key_ref, teacher_ref, grad_ref, total_ref, sems = refs[NT + 1 :]
    contract = (((1,), (1,)), ((), ()))
    step = 256
    spans = [pl.ds(k, step) for k in range(0, GROUPS * SHARD, step)]
    row_copies = gather_in(at_ref[0], pieces, row_ref, E_WIDE, sems)
    copies = []
    for i, span in enumerate(spans):
        pair = (
            pltpu.make_async_copy(keys_hbm.at[span, :], key_ref.at[span, :], sems.at[PARTS + 2 + 2 * i]),
            pltpu.make_async_copy(teacher_hbm.at[:, span], teacher_ref.at[:, span], sems.at[PARTS + 3 + 2 * i]),
        )
        pair[0].start()
        pair[1].start()
        copies.append(pair)
    for copy in row_copies:
        copy.wait()
    counts = jnp.zeros((16, E_WIDE - E), f32)
    for d in range(NT):
        counts = counts + row_ref[pl.ds(d * SHARD, 16), E:].astype(f32)
    tile = jnp.dot(counts.astype(bf16), spread_ref[...], preferred_element_type=f32) * (E / 8.0)
    for i, span in enumerate(spans):
        copies[i][0].wait()
        copies[i][1].wait()
        diff = (
            lax.dot_general(row_ref[:, :E], key_ref[span, :], contract, preferred_element_type=f32)
            - teacher_ref[:, span]
        )
        for a in range(RB):
            grad_ref[pl.ds(a * BLK, BLK), span] = (
                diff[a * BLK : (a + 1) * BLK] * tile[a : a + 1, i * step : (i + 1) * step]
            ).astype(bf16)
    for c, wide in ((0, 768), (768, 640)):
        total_ref[:, pl.ds(c, wide)] = jnp.dot(
            grad_ref[...], key_ref[:, pl.ds(c, wide)], preferred_element_type=f32
        )
    chunk_store(total_ref, at_ref[0], targets)


def gram_grads(at, pieces, keys, gram_teacher, spread):
    steps = GROUPS * SHARD // 256
    return pl.pallas_call(
        gram_body,
        out_shape=[jax.ShapeDtypeStruct(chunk.shape, chunk.dtype) for chunk in SPLIT],
        in_specs=[IN_SMEM] + in_place(PARTS + 2) + in_vmem(1),
        out_specs=in_vmem(NT + 1),
        scratch_shapes=[
            pltpu.VMEM((ROWS, E_WIDE), bf16),
            pltpu.VMEM((GROUPS * SHARD, E), bf16),
            pltpu.VMEM((ROWS, GROUPS * SHARD), f32),
            pltpu.VMEM((ROWS, GROUPS * SHARD), bf16),
            pltpu.VMEM((ROWS, E), f32),
            pltpu.SemaphoreType.DMA((PARTS + 2 + 2 * steps,)),
        ],
        compiler_params=scoped(20),
        cost_estimate=pl.CostEstimate(flops=1_700_000_000, bytes_accessed=9_000_000, transcendentals=0),
        name="gram_grads",
    )(at, *[hbm(pieces[n]) for n in PIECE_ORDER], keys, hbm(gram_teacher), spread)


def split_in(at, pieces, target_ref, wide, sems):
    copies = []
    for n in range(NT + 1):
        d = n if n <= 4 else n - 1
        cols = {4: pl.ds(0, LEFT), 5: pl.ds(LEFT, wide - LEFT)}.get(n, pl.ds(0, wide))
        rows = pl.ds(spot_of(at, d), SHARD)
        copies.append(pltpu.make_async_copy(pieces[n], target_ref.at[rows, cols], sems.at[n]))
        copies[-1].start()
    return copies


SPLIT_ORDER = (0, 1, 8, 2, 7, 3, 6, 4, 5)


def backward_body(at_ref, *refs):
    pieces, refs = dict(zip(SPLIT_ORDER, refs[: NT + 1])), refs[NT + 1 :]
    hidden_ref, w_out_ref, pre_ref, act_ref = refs[:4]
    keep_hbm, give_hbm, grad_pre_hbm, keep_ref, give_ref, grad_pre_ref, proj_ref, sems = refs[4:]
    at, tea = at_ref[0], at_ref[1]
    contract = (((1,), (1,)), ((), ()))
    over_rows = (((0,), (0,)), ((), ()))
    copies = split_in(at, pieces, proj_ref, E, sems)
    proj_ref[:, E:] = jnp.zeros((ROWS, E_PAD - E), bf16)
    pre = pre_ref[...]
    sigma = 1.0 / (1.0 + jnp.exp(-pre))
    slope = sigma * (1.0 + pre * (1.0 - sigma))
    for copy in copies:
        copy.wait()
    grad_act = lax.dot_general(proj_ref[:, :E], w_out_ref[...], contract, preferred_element_type=f32)
    grad_pre = (grad_act * slope).astype(bf16)
    grad_pre_ref[...] = grad_pre
    copies = [pltpu.make_async_copy(grad_pre_ref, grad_pre_hbm, sems.at[0])]
    copies[0].start()
    d_half, e_half = hidden_ref.shape[1] // 2, E_PAD // 2
    in_rows, out_rows = d_half // GROUPS, e_half // GROUPS
    for n, (ref, target, side) in enumerate(((keep_ref, keep_hbm, tea), (give_ref, give_hbm, 1 - tea))):
        part = hidden_ref[:, pl.ds(pl.multiple_of(side * d_half, d_half), d_half)]
        grad = lax.dot_general(part, grad_pre, over_rows, preferred_element_type=f32)
        for c in range(GROUPS):
            ref[c, pl.ds(0, in_rows), :] = grad[c * in_rows : (c + 1) * in_rows].astype(ref.dtype)
        part = proj_ref[:, pl.ds(pl.multiple_of(side * e_half, e_half), e_half)]
        grad = lax.dot_general(part, act_ref[...], over_rows, preferred_element_type=f32)
        for c in range(GROUPS):
            ref[c, pl.ds(in_rows, out_rows), :] = grad[c * out_rows : (c + 1) * out_rows].astype(ref.dtype)
        copies.append(pltpu.make_async_copy(ref, target, sems.at[n + 1]))
        copies[-1].start()
    for copy in copies:
        copy.wait()


def backward(where, pieces, hidden_states, w_out, pre_act, activation):
    rows, d_model = hidden_states.shape
    width = activation.shape[1]
    halves = (GROUPS, (d_model + E_PAD) // 2 // GROUPS, width)
    return pl.pallas_call(
        backward_body,
        out_shape=[
            pltpu.HBM(halves, bf16),
            pltpu.HBM(halves, bf16),
            pltpu.HBM((rows, width), bf16),
        ],
        in_specs=[IN_SMEM] + in_place(NT + 1) + in_vmem(4),
        out_specs=in_place(3),
        scratch_shapes=[
            pltpu.VMEM(halves, bf16),
            pltpu.VMEM(halves, bf16),
            pltpu.VMEM((rows, width), bf16),
            pltpu.VMEM((ROWS, E_PAD), bf16),
            pltpu.SemaphoreType.DMA((NT + 1,)),
        ],
        compiler_params=scoped(14),
        cost_estimate=pl.CostEstimate(flops=1_200_000_000, bytes_accessed=9_000_000, transcendentals=100_000),
        name="backward",
    )(where, *[pieces[d] for d in SPLIT_ORDER], hidden_states, w_out, pre_act, activation)


def hidden_body(grad_pre_hbm, w_in_ref, terms_hbm, grad_pre_ref, terms_ref, sems):
    first = pltpu.make_async_copy(grad_pre_hbm, grad_pre_ref, sems.at[NT])
    first.start()
    contract = (((1,), (1,)), ((), ()))
    share = w_in_ref.shape[0] // NT
    copies = []
    first.wait()
    for d in range(NT):
        span = pl.ds(d * ROWS, ROWS)
        terms_ref[span, :] = lax.dot_general(
            grad_pre_ref[...], w_in_ref[pl.ds(d * share, share), :], contract, preferred_element_type=f32
        ).astype(bf16)
        copies.append(pltpu.make_async_copy(terms_ref.at[span, :], terms_hbm.at[span, :], sems.at[d]))
        copies[-1].start()
    for copy in copies:
        copy.wait()


def hidden_grads(grad_pre, w_in):
    shape = (NT * ROWS, w_in.shape[0] // NT)
    return pl.pallas_call(
        hidden_body,
        out_shape=pltpu.HBM(shape, bf16),
        in_specs=in_place(1) + in_vmem(1),
        out_specs=in_place(1)[0],
        scratch_shapes=[
            pltpu.VMEM(grad_pre.shape, bf16),
            pltpu.VMEM(shape, bf16),
            pltpu.SemaphoreType.DMA((NT + 1,)),
        ],
        compiler_params=scoped(6),
        cost_estimate=pl.CostEstimate(flops=600_000_000, bytes_accessed=4_000_000, transcendentals=0),
        name="hidden_grads",
    )(hbm(grad_pre), w_in)


def pair_body(keep_ref, got_ref, sum_ref):
    sum_ref[...] = (keep_ref[...].astype(f32) + got_ref[...].astype(f32)).astype(bf16)


def pair_sum(keep, got):
    return pl.pallas_call(
        pair_body,
        out_shape=jax.ShapeDtypeStruct(keep.shape, bf16),
        in_specs=in_vmem(2),
        out_specs=in_vmem(1)[0],
        compiler_params=scoped(8),
        cost_estimate=pl.CostEstimate(flops=600_000, bytes_accessed=5_000_000, transcendentals=0),
        name="pair_sum",
    )(keep, got)


def half_out(ref, side, w_in_hbm, w_out_hbm, w_in_ref, w_out_ref, flat_ref, sems):
    d_half, e_half = w_in_ref.shape[0], E_PAD // 2
    in_rows, out_rows = d_half // GROUPS, e_half // GROUPS
    for c in range(GROUPS):
        w_in_ref[pl.ds(c * in_rows, in_rows), :] = ref[c, pl.ds(0, in_rows), :].astype(f32)
    copy = pltpu.make_async_copy(
        w_in_ref, w_in_hbm.at[pl.ds(pl.multiple_of(side * d_half, d_half), d_half), :], sems.at[0]
    )
    copy.start()
    for c in range(GROUPS):
        flat_ref[pl.ds(c * out_rows, out_rows), :] = ref[c, pl.ds(in_rows, out_rows), :].astype(f32)
    for c in range(0, e_half, BLK):
        w_out_ref[:, pl.ds(c, BLK)] = flat_ref[pl.ds(c, BLK), :].T
    for which, start, size in ((0, 0, e_half), (1, e_half, E - e_half)):

        @pl.when(side == which)
        def _():
            part = pltpu.make_async_copy(
                w_out_ref.at[:, pl.ds(0, size)], w_out_hbm.at[:, pl.ds(start, size)], sems.at[1]
            )
            part.start()
            part.wait()

    copy.wait()


def first_body(tea_ref, mine_ref, sum_hbm, w_in_hbm, w_out_hbm, hidden_ref, w_in_ref, w_out_ref, flat_ref, sum_ref, sems):
    copy = pltpu.make_async_copy(sum_hbm, sum_ref, sems.at[2])
    copy.start()
    half_out(mine_ref, tea_ref[0], w_in_hbm, w_out_hbm, w_in_ref, w_out_ref, flat_ref, sems)
    copy.wait()
    hidden_ref[...] = sum_ref[...].astype(f32)


def second_body(tea_ref, other_ref, w_in_old, w_out_old, w_in_hbm, w_out_hbm, w_in_ref, w_out_ref, flat_ref, sems):
    half_out(other_ref, 1 - tea_ref[0], w_in_hbm, w_out_hbm, w_in_ref, w_out_ref, flat_ref, sems)


def half_scratch(d_model, width):
    return [
        pltpu.VMEM((d_model // 2, width), f32),
        pltpu.VMEM((width, E_PAD // 2), f32),
        pltpu.VMEM((E_PAD // 2, width), f32),
    ]


def first_half(tea, mine, hidden, d_model):
    width = mine.shape[-1]
    return pl.pallas_call(
        first_body,
        out_shape=[
            pltpu.HBM((d_model, width), f32),
            pltpu.HBM((width, E), f32),
            jax.ShapeDtypeStruct(hidden.shape, f32),
        ],
        in_specs=[IN_SMEM] + in_vmem(1) + in_place(1),
        out_specs=in_place(2) + in_vmem(1),
        scratch_shapes=half_scratch(d_model, width)
        + [pltpu.VMEM(hidden.shape, bf16), pltpu.SemaphoreType.DMA((3,))],
        compiler_params=scoped(12),
        cost_estimate=pl.CostEstimate(flops=0, bytes_accessed=5_000_000, transcendentals=0),
        name="first_half",
    )(tea, mine, hbm(hidden))


def second_half(tea, other, w_in, w_out):
    return pl.pallas_call(
        second_body,
        out_shape=[pltpu.HBM(w_in.shape, f32), pltpu.HBM(w_out.shape, f32)],
        in_specs=[IN_SMEM] + in_vmem(1) + in_place(2),
        out_specs=in_place(2),
        scratch_shapes=half_scratch(w_in.shape[0], w_in.shape[1]) + [pltpu.SemaphoreType.DMA((2,))],
        input_output_aliases={2: 0, 3: 1},
        compiler_params=scoped(12),
        cost_estimate=pl.CostEstimate(flops=0, bytes_accessed=4_000_000, transcendentals=0),
        name="second_half",
    )(tea, other, hbm(w_in), hbm(w_out))


def on_device(hidden_states, w_in, w_out, teacher, patch_map, row_pick, key_pick):
    seq_index = lax.axis_index("seq")
    tp_index = lax.axis_index("tp")
    tea_index = lax.axis_index("tea")
    at = jnp.full((1,), tp_index, jnp.int32)
    tea = jnp.full((1,), tea_index, jnp.int32)
    contract = (((1,), (1,)), ((), ()))

    picks = row_pick.reshape(GROUPS)
    group = jnp.full((1,), lax.axis_index(("seq", "tea")), jnp.int32)
    row_teacher, teacher_send = align(jnp.concatenate([at, group]), teacher, patch_map.reshape(1, ROWS), picks)
    teacher_send, at_next = lax.optimization_barrier((teacher_send, at))
    teacher_got = lax.all_to_all(teacher_send, "seq", 0, 0, tiled=True)

    pre_act, activation, *chunks = forward(at_next, hidden_states, w_in, w_out)
    activation, key_pick, picks = lax.optimization_barrier((activation, key_pick, picks))
    received = sum_split(*chunks)

    table = key_pick.reshape(GROUPS, GROUPS)
    of_rows = lax.dynamic_index_in_dim(table, seq_index, axis=0, keepdims=False)
    of_keys = lax.dynamic_index_in_dim(table, seq_index, axis=1, keepdims=False)
    local = jnp.repeat(jnp.stack([picks, of_rows, of_keys]), RB, axis=1)
    local = jnp.pad(local, ((0, 8 - 3), (0, E_WIDE - E - GROUPS * RB)))
    key_ids = jnp.arange(GROUPS * SHARD, dtype=jnp.int32)
    key_cell = key_ids // SHARD * RB + (tp_index * SHARD + key_ids % SHARD) // BLK
    spread = (jnp.arange(E_WIDE - E, dtype=jnp.int32)[:, None] == key_cell[None, :]).astype(bf16)

    *received, teacher_got = lax.optimization_barrier((*received, teacher_got))
    unit_student, inv_norm, row_send, key_send = normalise(chunks[0], local, teacher_got, received)
    rows = gather_ring(row_send)
    keys = lax.all_to_all(key_send, "seq", 0, 0, tiled=True).reshape(GROUPS * SHARD, E)
    teacher_got, inv_norm = lax.optimization_barrier((teacher_got, inv_norm))
    inv_norm = inv_norm[:, :1]
    key_teacher = teacher_got[:, :, :E].reshape(GROUPS * SHARD, E)
    gram_teacher = lax.dot_general(row_teacher, key_teacher, contract, preferred_element_type=f32)

    row_grad = gram_grads(at, rows, keys, gram_teacher, spread)
    unit_grad = row_grad[0]
    for piece in sum_split(*row_grad):
        unit_grad = unit_grad + piece.astype(f32)
    inner = jnp.sum(unit_student * unit_grad, axis=-1, keepdims=True)
    grad_proj = ((unit_grad - unit_student * inner) * inv_norm).astype(bf16)
    pieces = gather_split(grad_proj)

    where = jnp.concatenate([at, tea])
    keep, give, grad_pre = backward(where, pieces, hidden_states, w_out, pre_act, activation)
    got = swap_tea(give)
    hidden_terms = hidden_grads(grad_pre, w_in)
    chip, hidden_terms = lax.optimization_barrier((pair_sum(keep, got), hidden_terms))
    hidden_sum = lax.psum_scatter(hidden_terms, "tp", scatter_dimension=0, tiled=True)
    chip = lax.all_to_all(chip, "seq", 0, 0, tiled=True)
    mine = to_all(jnp.sum(chip.astype(f32), axis=0).astype(bf16)).reshape(keep.shape)
    other = swap_tea(mine)
    grad_w_in, grad_w_out, grad_hidden = first_half(tea, mine, hidden_sum, hidden_states.shape[1])
    grad_w_in, grad_w_out = second_half(tea, other, grad_w_in, grad_w_out)
    return (grad_hidden, grad_w_in, grad_w_out)


def solution(mesh):
    return jax.shard_map(
        on_device,
        mesh=mesh,
        in_specs=(
            P(("seq", "tea"), None),
            P(None, "tp"),
            P("tp", None),
            P(("seq", "tea"), None),
            P(("seq", "tea")),
            P("seq", "tp", "tea", None),
            P(None, "tp", "tea", None),
        ),
        out_specs=(P(("seq", "tea"), "tp"), P(None, "tp"), P("tp", None)),
        check_vma=False,
    )
```
